512 devices in a mesh: rows: 512 (over x, z, y, core).
Axes of the slice: x: 4, y: 8, z: 8, core: 2. Of those that a mesh axis runs over, the one named last changes fastest.
Arguments:
- features: float32 [262144, 256], P('rows'), may hold values from -6 to 6
- adjacency: float32 [1024, 6, 256, 256], P('rows'), may hold values from -0.25 to 0.25
- block_index: int32 [1024, 6], P('rows'), may hold values from 0 to 1023, as said below
- block_counts: int32 [1024], P('rows'), may hold values from 1 to 6, as said below
- labels: int32 [262144], P('rows'), may hold values from 0 to 127
- weight_in: float32 [256, 512], replicated, may hold values from -0.375 to 0.375
- weight_out: float32 [512, 128], replicated, may hold values from -0.25 to 0.25
Outputs:
- logits: float32 [262144, 128], P('rows')
- mean_loss: float32 [], replicated
- hidden_grad: float32 [262144, 512], P('rows')
- grad_in: float32 [256, 512], replicated
- grad_out: float32 [512, 128], replicated
The draws below stay inside these ranges and needn't reach their ends.
Inputs may be any that keep to these rules, and one draw needn't show every extreme that they name: `block_index`: row block b lies on device b // 2; every slot's column block lies at most 2 row blocks away from b, inside the graph. `block_counts`: some row block uses all 6 slots.
All inputs are finite; a program needn't handle non-finite values.
Results may differ from the reference program's by a relative error of at most 0.00011.
Values sent between devices are 32-bit elements; how exact they have to be, the bound alone decides.
No kernel may reach another device: no remote copies, remote signals or barrier semaphores. Data moves between devices by JAX's collectives and lax.ppermute only.
A program may use at most 64 MiB of HBM per device.

```python
import jax
import jax.numpy as jnp
from jax import lax

BLOCK = 256
F_IN = 256
HID = 512
CLASSES = 128
SLOTS = 6
REACH = 2
BLOCKS = 1024
NODES = 262144


def draw_block_index(key, part):
    key = jax.random.fold_in(key, 11)
    block_ids = jnp.arange(BLOCKS, dtype=jnp.int32)
    lowest = jnp.maximum(block_ids - REACH, 0)
    highest = jnp.minimum(block_ids + REACH + 1, BLOCKS)
    raw = jax.random.randint(key, (BLOCKS, SLOTS), 0, 1073741824, dtype=jnp.int32)
    return (lowest[:, None] + raw % (highest - lowest)[:, None]).astype(jnp.int32)


def draw_block_counts(key, part):
    key = jax.random.fold_in(key, 12)
    first, third = jax.random.split(key, 2)
    counts = 1 + jax.random.randint(first, (BLOCKS,), 0, SLOTS, dtype=jnp.int32)
    fullest = jax.random.randint(third, (), 0, BLOCKS, dtype=jnp.int32)
    counts = jnp.where(jnp.arange(BLOCKS, dtype=jnp.int32) == fullest, SLOTS, counts)
    return counts.astype(jnp.int32)


def place_ends(drawn, stream_key, least, high):
    place = [jax.random.randint(jax.random.fold_in(stream_key, axis), (), 0, length) for axis, length in enumerate(drawn.shape)]
    widest = drawn.shape.index(max(drawn.shape))
    next_to = place[:widest] + [(place[widest] + 1) % drawn.shape[widest]] + place[widest + 1:]
    return drawn.at[tuple(place)].set(least).at[tuple(next_to)].set(high)


def shard_levels(own_key, dims, shards, smallest, high):
    def one(position, parts):
        steps = jax.random.uniform(jax.random.fold_in(jax.random.fold_in(own_key, 6), position), (parts,), jnp.float32, smallest / len(shards), high / len(shards))
        return jnp.repeat(jnp.exp(steps), dims[position] // parts).reshape((-1,) + (1,) * (len(dims) - position - 1))

    gain = one(*shards[0])
    for cut in shards[1:]:
        gain = gain * one(*cut)
    return gain


def noise(own_key, dims, scale, limit, shards=(), kind=jnp.bfloat16):
    values = jax.random.normal(own_key, dims, jnp.float32) * scale
    if len(shards) > 0:
        values = shard_levels(own_key, dims, shards, -0.22, 0.18) * values
    return jnp.clip(values, min=-limit, max=limit).astype(kind)


def setup_inputs(seed: int = 0) -> dict:
    keys = jax.random.split(jax.random.key(seed), 8)
    return {
        "features": noise(keys[0], (NODES, F_IN), 1.0, 6.0, ((0, 512),), jnp.float32),
        "adjacency": noise(keys[1], (BLOCKS, SLOTS, BLOCK, BLOCK), (2 * BLOCK) ** -0.5, 0.25, ((0, 512),), jnp.float32),
        "block_index": draw_block_index(jax.random.fold_in(keys[7], 71), 0),
        "block_counts": draw_block_counts(jax.random.fold_in(keys[7], 71), 0),
        "labels": place_ends(jax.random.randint(keys[4], (NODES,), 0, CLASSES), jax.random.fold_in(keys[4], 1), 0, CLASSES - 1).astype(jnp.int32),
        "weight_in": noise(keys[5], (F_IN, HID), F_IN ** -0.5, 0.375, (), jnp.float32),
        "weight_out": noise(keys[6], (HID, CLASSES), HID ** -0.5, 0.25, (), jnp.float32),
    }


HIGH = lax.Precision.HIGHEST

def activate(values):
    return jax.nn.gelu(values, approximate=False)

def propagate(values, adjacency, block_index, block_counts):
    block_rows = adjacency.shape[2]
    grouped = values.reshape(adjacency.shape[0], block_rows, values.shape[1])
    usable_all = jnp.arange(adjacency.shape[1], dtype=jnp.int32)[None, :] < block_counts[:, None]

    def one_block(packed):
        tiles, column_ids, usable = packed
        picked = grouped[column_ids]
        tiles = jnp.where(usable[:, None, None], tiles, jnp.zeros_like(tiles))
        return jnp.einsum('kij,kjw->iw', tiles, picked, precision=HIGH)
    result = lax.map(one_block, (adjacency, block_index, usable_all))
    return result.reshape(-1, values.shape[1])

def reference(features, adjacency, block_index, block_counts, labels, weight_in, weight_out):
    spread_in = propagate(features, adjacency, block_index, block_counts)
    pre_hidden = jnp.dot(spread_in, weight_in, precision=HIGH)
    hidden = activate(pre_hidden)
    spread_hidden = propagate(hidden, adjacency, block_index, block_counts)
    logits = jnp.dot(spread_hidden, weight_out, precision=HIGH)
    totals = jnp.log(lax.optimization_barrier(jnp.sum(jnp.exp(logits), axis=1)))
    onehot = (labels[:, None] == jnp.arange(CLASSES, dtype=jnp.int32)[None, :]).astype(logits.dtype)
    row_loss = totals - lax.optimization_barrier(jnp.sum(onehot * logits, axis=1))
    mean_loss = jnp.sum(row_loss) / NODES
    logit_grad = jnp.exp(logits - totals[:, None]) - onehot
    grad_out = jnp.dot(spread_hidden.T, logit_grad, precision=HIGH)
    _, pull = jax.vjp(lambda values: propagate(values, adjacency, block_index, block_counts), jnp.zeros_like(logit_grad))
    returned = pull(logit_grad)[0]
    hidden_grad = jnp.dot(returned, weight_out.T, precision=HIGH)
    _, back = jax.vjp(activate, pre_hidden)
    pre_grad = back(hidden_grad)[0]
    grad_in = jnp.dot(spread_in.T, pre_grad, precision=HIGH)
    return (logits, mean_loss, hidden_grad, grad_in, grad_out)
```

```python
import jax
import jax.numpy as jnp
from jax import lax
from jax.sharding import Mesh, PartitionSpec as P

HIGH = lax.Precision.HIGH
ALL = ("x", "z", "y", "c")
BIG = ("x", "y")
MID = ("z",)


def activate(values):
    return jax.nn.gelu(values, approximate=False)


def dot(a, b, dims):
    return lax.dot_general(a, b, (dims, ((), ())), precision=HIGH)


def mate(value, devices):
    return lax.ppermute(value, ALL, [(i, i ^ 1) for i in range(devices)])


def beside(value, devices):
    pairs = [(i, i + 1) for i in range(1, devices - 1, 2)]
    return lax.ppermute(value, ALL, pairs + [(b, a) for a, b in pairs])


def exchange(value, axes):
    return lax.all_to_all(value, axes, 0, 0, tiled=True)


def spread(value, count):
    return jnp.broadcast_to(value[None], (count,) + value.shape)


def per_device(features, adjacency, block_index, block_counts, labels, weight_in, weight_out):
    devices = lax.axis_size(ALL)
    core = lax.axis_index("c")
    here, slots, rows = adjacency.shape[:3]
    nodes = here * rows
    classes = weight_out.shape[1]
    near = block_index - lax.axis_index(ALL) * here
    local = (near >= 0) & (near < here)
    right = near >= here
    outside = jnp.where(right, near - here, near + here)
    bucket = jnp.where(local, here + near, outside + jnp.where(right == (core == 0), 0, 2 * here))
    usable = jnp.arange(slots, dtype=jnp.int32)[None, :] < block_counts[:, None]
    feat_e = beside(features, devices)
    feat_i = mate(features, devices)
    pieces = []
    for s in range(3 * here):
        take = usable & (bucket == s)
        pieces.append(jnp.sum(jnp.where(take[:, :, None, None], adjacency, 0.0), axis=1))
    band = jnp.concatenate([p.reshape(nodes, rows) for p in pieces], axis=1)
    spread_in = dot(band, jnp.concatenate([feat_i, features, feat_e], axis=0), ((1,), (0,)))
    pre_hidden = dot(spread_in, weight_in, ((1,), (0,)))
    hidden, back = jax.vjp(activate, pre_hidden)
    scores = dot(hidden, weight_out, ((1,), (0,)))
    scores_e = beside(scores, devices)
    scores_i = mate(scores, devices)
    logits = dot(band, jnp.concatenate([scores_i, scores, scores_e], axis=0), ((1,), (0,)))
    totals = jnp.log(jnp.sum(jnp.exp(logits), axis=1))
    onehot = (labels[:, None] == jnp.arange(classes, dtype=jnp.int32)[None, :]).astype(jnp.float32)
    loss = jnp.sum(totals - jnp.sum(onehot * logits, axis=1))
    logit_grad = jnp.exp(logits - totals[:, None]) - onehot
    returns = dot(band, logit_grad, ((0,), (0,)))
    ret_e = beside(returns[2 * nodes :], devices)
    ret_i = mate(returns[:nodes], devices)
    returned = returns[nodes : 2 * nodes] + ret_e + ret_i
    hidden_grad = dot(returned, weight_out, ((1,), (1,)))
    pre_grad = back(hidden_grad)[0]
    grad_in = dot(spread_in, pre_grad, ((0,), (0,)))
    grad_out = dot(hidden, returned, ((0,), (0,)))
    width = 128
    tiles = grad_in.shape[1] // width
    flat = jnp.concatenate(
        [grad_in[:, t * width : (t + 1) * width] for t in range(tiles)] + [grad_out], axis=0
    )
    half = flat.shape[0] // 2
    keep = jnp.where(core == 0, flat[:half], flat[half:])
    give = jnp.where(core == 0, flat[half:], flat[:half])
    big, mid = lax.axis_size(BIG), lax.axis_size(MID)
    tail = jnp.full((8, width), loss)
    parts = jnp.concatenate([give, tail], axis=0)
    parts = mate(parts, devices)
    shard = half // big
    mine = (keep + parts[:half]).reshape(big, shard, width)
    loss_row = jnp.broadcast_to(tail[:1] + parts[half : half + 1], (big, 1, width))
    summed = jnp.sum(exchange(jnp.concatenate([mine, loss_row], axis=1), BIG), axis=0)
    summed = jnp.sum(exchange(spread(summed, mid), MID), axis=0)
    mean_loss = summed[shard, 0] / (nodes * devices)
    own = exchange(spread(summed[:shard], big), BIG).reshape(half, width)
    other = mate(own, devices)
    low = jnp.where(core == 0, own, other)
    high = jnp.where(core == 0, other, own)
    whole = jnp.concatenate([low, high], axis=0)
    deep = grad_in.shape[0]
    grad_in = jnp.concatenate([whole[t * deep : (t + 1) * deep] for t in range(tiles)], axis=1)
    return (logits, mean_loss, hidden_grad, grad_in, whole[tiles * deep :])


def solution(mesh):
    grid = Mesh(mesh.devices.reshape(4, 8, 8, 2), ALL)
    split = P(ALL)
    return jax.shard_map(
        per_device,
        mesh=grid,
        in_specs=(split, split, split, split, split, P(), P()),
        out_specs=(split, P(), split, P(), P()),
        check_vma=False,
    )
```

```python
import jax
import jax.numpy as jnp
from jax import lax
from jax.experimental import pallas as pl
from jax.experimental.pallas import tpu as pltpu
from jax.sharding import Mesh, PartitionSpec as P

ALL = ("x", "z", "y", "c")
BIG = ("x", "y")
MID = ("z",)
LANES = 128
F32 = jnp.float32
BF16 = jnp.bfloat16
VMEM_LIMIT = 24 * 1024 * 1024
SQRT_HALF = 0.7071067811865476
INV_SQRT_2PI = 0.3989422804014327


def mate(value, devices):
    return lax.ppermute(value, ALL, [(i, i ^ 1) for i in range(devices)])


def beside(value, devices):
    pairs = [(i, i + 1) for i in range(1, devices - 1, 2)]
    return lax.ppermute(value, ALL, pairs + [(b, a) for a, b in pairs])


def exchange(value, axes):
    return lax.all_to_all(value, axes, 0, 0, tiled=True)


def spread(value, count):
    return jnp.broadcast_to(value[None], (count,) + value.shape)


def halves(value):
    high = value.astype(BF16)
    return high, (value - high.astype(F32)).astype(BF16)


def mm(a, b, dims=((1,), (0,))):
    return lax.dot_general(a, b, (dims, ((), ())), preferred_element_type=F32)


def fold(wide):
    half = wide.shape[1] // 2
    return wide[:, :half] + wide[:, half:]


def erfc(value):
    size = jnp.abs(value)
    t = 1.0 / (1.0 + 0.5 * size)
    poly = jnp.full_like(t, 0.17087277)
    for term in (-0.82215223, 1.48851587, -1.13520398, 0.27886807, -0.18628806, 0.09678418,
                 0.37409196, 1.00002368, -1.26551223):
        poly = poly * t + term
    tail = t * jnp.exp(poly - size * size)
    return jnp.where(value < 0, 2.0 - tail, tail)


def prepare(sel, adjacency, features, w_in, w_out, labels,
            loc_h, loc_l, halo_h, halo_l, s_loc, win_h, win_l, wout_hl, wout_hh, wout_ll, onehot, band):
    here, slots, rows, _ = adjacency.shape
    for b in range(here):
        band[...] = jnp.zeros_like(band)
        for k in range(slots):
            place = sel[b, k]

            @pl.when(place >= 0)
            def _():
                band[place] += adjacency[b, k]

        at = pl.ds(b * rows, rows)
        for s in range(3 * here):
            high, low = halves(band[s])
            if here <= s < 2 * here:
                cols = pl.ds((s - here) * rows, rows)
                loc_h[at, cols] = high
                loc_l[at, cols] = low
            else:
                cols = pl.ds((s if s < here else s - here) * rows, rows)
                halo_h[at, cols] = high
                halo_l[at, cols] = low
    feat_h, feat_l = halves(features[...])
    s_loc[...] = mm(loc_h[...], feat_h) + mm(loc_h[...], feat_l) + mm(loc_l[...], feat_h)
    high, low = halves(w_in[...])
    win_h[...] = high
    win_l[...] = low
    high, low = halves(w_out[...])
    classes = high.shape[1]
    for ref, left, right in ((wout_hl, high, low), (wout_hh, high, high), (wout_ll, low, low)):
        ref[:, :classes] = left
        ref[:, classes:] = right
    columns = lax.broadcasted_iota(jnp.int32, (classes, labels.shape[1]), 0)
    onehot[...] = jnp.where(columns == labels[...], 1.0, 0.0).T


def spread_forward(halo_h, halo_l, s_loc, feat_i, feat_e, win_h, win_l, wout_hl, spread_in, scores):
    half = feat_i.shape[0]
    fi_h, fi_l = halves(feat_i[...])
    fe_h, fe_l = halves(feat_e[...])
    hi, he = halo_h[:, :half], halo_h[:, half:]
    li, le = halo_l[:, :half], halo_l[:, half:]
    near = mm(hi, fi_h) + mm(hi, fi_l) + mm(li, fi_h)
    far = mm(he, fe_h) + mm(he, fe_l) + mm(le, fe_h)
    s = s_loc[...] + near + far
    spread_in[...] = s
    s_h, s_l = halves(s)
    pre = mm(s_h, win_h[...]) + mm(s_h, win_l[...]) + mm(s_l, win_h[...])
    hid_h, hid_l = halves(0.5 * pre * erfc(-SQRT_HALF * pre))
    scores[...] = fold(mm(hid_h, wout_hl[...]) + mm(hid_l, wout_hl[...]))


def beside_forward(loc_h, loc_l, spread_in, scores, win_h, win_l, slope, hid_th, hid_tl, in_th, in_tl, logits_loc):
    s = spread_in[...]
    s_h, s_l = halves(s)
    pre = mm(s_h, win_h[...]) + mm(s_h, win_l[...]) + mm(s_l, win_h[...])
    gate = 0.5 * erfc(-SQRT_HALF * pre)
    slope[...] = gate + pre * (INV_SQRT_2PI * jnp.exp(-0.5 * pre * pre))
    high, low = halves((pre * gate).T)
    hid_th[...] = high
    hid_tl[...] = low
    high, low = halves(s.T)
    in_th[...] = high
    in_tl[...] = low
    pair = jnp.concatenate(halves(scores[...]), axis=1)
    logits_loc[...] = fold(mm(loc_h[...], pair) + mm(loc_l[...], pair))


def classify(halo_h, halo_l, logits_loc, sco_i, sco_e, onehot, logits, grads_t, loss, out_i, out_e):
    half = sco_i.shape[0]
    classes = logits.shape[1]
    pair_i = jnp.concatenate(halves(sco_i[...]), axis=1)
    pair_e = jnp.concatenate(halves(sco_e[...]), axis=1)
    wide = mm(halo_h[:, :half], pair_i) + mm(halo_l[:, :half], pair_i)
    wide = wide + mm(halo_h[:, half:], pair_e) + mm(halo_l[:, half:], pair_e)
    values = logits_loc[...] + fold(wide)
    logits[...] = values
    totals = jnp.log(jnp.sum(jnp.exp(values), axis=1, keepdims=True))
    hot = onehot[...]
    row_loss = totals - jnp.sum(hot * values, axis=1, keepdims=True)
    loss[...] = jnp.broadcast_to(jnp.sum(row_loss, axis=0, keepdims=True), loss.shape)
    high, low = halves((jnp.exp(values - totals) - hot).T)
    grads = jnp.concatenate([high, low], axis=0)
    grads_t[...] = grads
    for out, cols in ((out_i, pl.ds(0, half)), (out_e, pl.ds(half, half))):
        tall = mm(grads, halo_h[:, cols]) + mm(grads, halo_l[:, cols])
        out[...] = tall[:classes] + tall[classes:]


def beside_classify(grads_t, loc_h, loc_l, out):
    tall = mm(grads_t[...], loc_h[...]) + mm(grads_t[...], loc_l[...])
    half = tall.shape[0] // 2
    out[...] = tall[:half] + tall[half:]


def backward(core, ret_loc, ret_i, ret_e, wout_hh, wout_ll, slope, in_th, in_tl, hid_th, hid_tl, loss,
             hidden_grad, keep, give):
    returned = (ret_loc[...] + ret_i[...] + ret_e[...]).T
    pair = jnp.concatenate(halves(returned), axis=1)
    across = ((1,), (1,))
    grad = mm(pair, wout_hh[...], across) + mm(pair, wout_ll[...], across)
    hidden_grad[...] = grad
    pre_h, pre_l = halves(grad * slope[...])
    grad_in = mm(in_th[...], pre_h) + mm(in_th[...], pre_l) + mm(in_tl[...], pre_h)
    grad_out = fold(mm(hid_th[...], pair) + mm(hid_tl[...], pair))
    deep = grad_in.shape[0]
    rows = keep.shape[0]
    give[rows:, :] = loss[...]
    pieces = [grad_in[:, t : t + LANES] for t in range(0, grad_in.shape[1], LANES)] + [grad_out]
    for first, second in ((keep, give), (give, keep)):

        @pl.when(core[0] == (0 if first is keep else 1))
        def _():
            at = 0
            for piece in pieces:
                ref, start = (first, at) if at < rows else (second, at - rows)
                ref[pl.ds(start, piece.shape[0]), :] = piece
                at += piece.shape[0]


def assemble(core, own, other, grad_in, grad_out):
    deep = grad_in.shape[0]
    rows = own.shape[0]
    for first, second in ((own, other), (other, own)):

        @pl.when(core[0] == (0 if first is own else 1))
        def _():
            tiles = grad_in.shape[1] // LANES
            for t in range(tiles):
                at = t * deep
                ref, start = (first, at) if at < rows else (second, at - rows)
                grad_in[:, pl.ds(t * LANES, LANES)] = ref[pl.ds(start, deep), :]
            grad_out[...] = second[pl.ds(tiles * deep - rows, grad_out.shape[0]), :]


def call(body, outs, args, scalars=0, flops=0, scratch=()):
    smem = pl.BlockSpec(memory_space=pltpu.SMEM)
    vmem = pl.BlockSpec(memory_space=pltpu.VMEM)
    moved = sum(a.size * a.dtype.itemsize for a in args)
    return pl.pallas_call(
        body,
        out_shape=[jax.ShapeDtypeStruct(shape, kind) for shape, kind in outs],
        in_specs=[smem] * scalars + [vmem] * (len(args) - scalars),
        out_specs=[vmem] * len(outs),
        scratch_shapes=scratch,
        cost_estimate=pl.CostEstimate(flops=flops, bytes_accessed=moved, transcendentals=0),
        compiler_params=pltpu.CompilerParams(vmem_limit_bytes=VMEM_LIMIT),
        name=body.__name__,
    )(*args)


def per_device(features, adjacency, block_index, block_counts, labels, weight_in, weight_out):
    devices = lax.axis_size(ALL)
    core = lax.axis_index("c")
    cores = jnp.full((1,), core, jnp.int32)
    here, slots, rows = adjacency.shape[:3]
    nodes = here * rows
    deep, hid = weight_in.shape
    classes = weight_out.shape[1]
    near = block_index - lax.axis_index(ALL) * here
    local = (near >= 0) & (near < here)
    right = near >= here
    outside = jnp.where(right, near - here, near + here)
    bucket = jnp.where(local, here + near, outside + jnp.where(right == (core == 0), 0, 2 * here))
    usable = jnp.arange(slots, dtype=jnp.int32)[None, :] < block_counts[:, None]
    sel = jnp.where(usable, bucket, -1)

    feat_e = beside(features, devices)
    feat_i = mate(features, devices)
    loc = ((nodes, nodes), BF16)
    halo = ((nodes, 2 * nodes), BF16)
    w_pair = ((hid, 2 * classes), BF16)
    loc_h, loc_l, halo_h, halo_l, s_loc, win_h, win_l, wout_hl, wout_hh, wout_ll, onehot = call(
        prepare,
        [loc, loc, halo, halo, ((nodes, deep), F32), ((deep, hid), BF16), ((deep, hid), BF16),
         w_pair, w_pair, w_pair, ((nodes, classes), F32)],
        [sel, adjacency, features, weight_in, weight_out, labels.reshape(1, nodes)],
        scalars=1,
        flops=6 * nodes * nodes * deep,
        scratch=[pltpu.VMEM((3 * here, rows, rows), F32)],
    )
    spread_in, scores = call(
        spread_forward,
        [((nodes, deep), F32), ((nodes, classes), F32)],
        [halo_h, halo_l, s_loc, feat_i, feat_e, win_h, win_l, wout_hl],
        flops=20 * nodes * nodes * deep,
    )
    sco_e = beside(scores, devices)
    sco_i = mate(scores, devices)
    slope, hid_th, hid_tl, in_th, in_tl, logits_loc = call(
        beside_forward,
        [((nodes, hid), F32), ((hid, nodes), BF16), ((hid, nodes), BF16), ((deep, nodes), BF16), ((deep, nodes), BF16),
         ((nodes, classes), F32)],
        [loc_h, loc_l, spread_in, scores, win_h, win_l],
        flops=12 * nodes * nodes * deep,
    )
    logits, grads_t, loss, out_i, out_e = call(
        classify,
        [((nodes, classes), F32), ((2 * classes, nodes), BF16), ((8, LANES), F32), ((classes, nodes), F32),
         ((classes, nodes), F32)],
        [halo_h, halo_l, logits_loc, sco_i, sco_e, onehot],
        flops=16 * nodes * nodes * classes,
    )
    ret_e = beside(out_e, devices)
    ret_i = mate(out_i, devices)
    (ret_loc,) = call(
        beside_classify, [((classes, nodes), F32)], [grads_t, loc_h, loc_l], flops=8 * nodes * nodes * classes
    )
    half = (deep * hid + hid * classes) // LANES // 2
    hidden_grad, keep, give = call(
        backward,
        [((nodes, hid), F32), ((half, LANES), F32), ((half + 8, LANES), F32)],
        [cores, ret_loc, ret_i, ret_e, wout_hh, wout_ll, slope, in_th, in_tl, hid_th, hid_tl, loss],
        scalars=1,
        flops=12 * nodes * nodes * deep,
    )
    parts = mate(give, devices)
    big, mid = lax.axis_size(BIG), lax.axis_size(MID)
    shard = half // big
    mine = (keep + parts[:half]).reshape(big, shard, LANES)
    loss_row = jnp.broadcast_to(loss[:1] + parts[half : half + 1], (big, 1, LANES))
    summed = jnp.sum(exchange(jnp.concatenate([mine, loss_row], axis=1), BIG), axis=0)
    summed = jnp.sum(exchange(spread(summed, mid), MID), axis=0)
    mean_loss = summed[shard, 0] / (nodes * devices)
    own = exchange(spread(summed[:shard], big), BIG).reshape(half, LANES)
    other = mate(own, devices)
    grad_in, grad_out = call(
        assemble, [((deep, hid), F32), ((hid, classes), F32)], [cores, own, other], scalars=1
    )
    return (logits, mean_loss, hidden_grad, grad_in, grad_out)


def solution(mesh):
    grid = Mesh(mesh.devices.reshape(4, 8, 8, 2), ALL)
    split = P(ALL)
    return jax.shard_map(
        per_device,
        mesh=grid,
        in_specs=(split, split, split, split, split, P(), P()),
        out_specs=(split, P(), split, P(), P()),
        check_vma=False,
    )
```

```python
import functools

import jax
import jax.numpy as jnp
from jax import lax
from jax.experimental import pallas as pl
from jax.experimental.pallas import tpu as pltpu
from jax.sharding import Mesh, PartitionSpec as P

ALL = ("x", "z", "y", "c")
BIG = ("x", "y")
MID = ("z",)
LANES = 128
F32 = jnp.float32
BF16 = jnp.bfloat16
VMEM_LIMIT = 24 * 1024 * 1024
CHUNK = 256
SQRT_HALF = 0.7071067811865476
INV_SQRT_2PI = 0.3989422804014327


def mate(value, devices):
    return lax.ppermute(value, ALL, [(i, i ^ 1) for i in range(devices)])


def beside(value, devices):
    pairs = [(i, i + 1) for i in range(1, devices - 1, 2)]
    return lax.ppermute(value, ALL, pairs + [(b, a) for a, b in pairs])


def exchange(value, axes):
    return lax.all_to_all(value, axes, 0, 0, tiled=True)


def spread(value, count):
    return jnp.broadcast_to(value[None], (count,) + value.shape)


def position():
    place = 0
    for axis in ALL:
        place = place * lax.axis_size(axis) + lax.axis_index(axis)
    return place


def halves(value):
    high = value.astype(BF16)
    return high, (value - high.astype(F32)).astype(BF16)


def mm(a, b, dims=((1,), (0,))):
    return lax.dot_general(a, b, (dims, ((), ())), preferred_element_type=F32)


def fold(wide):
    half = wide.shape[1] // 2
    return wide[:, :half] + wide[:, half:]


def erfc(value):
    size = jnp.abs(value)
    t = 1.0 / (1.0 + 0.5 * size)
    poly = jnp.full_like(t, 0.17087277)
    for term in (-0.82215223, 1.48851587, -1.13520398, 0.27886807, -0.18628806, 0.09678418,
                 0.37409196, 1.00002368, -1.26551223):
        poly = poly * t + term
    tail = t * jnp.exp(poly - size * size)
    return jnp.where(value < 0, 2.0 - tail, tail)


def prepare(block_index, block_counts, adjacency, features, w_in, w_out, labels,
            loc_h, loc_l, halo_h, halo_l, s_loc, win_h, win_l, wout_hl, wout_hh, wout_ll, onehot, feat_out,
            slots_in, feat_in, win_in, wout_in, labels_in, band, sems):
    here, slots, rows, _ = adjacency.shape
    moves = [(features, feat_in), (w_in, win_in), (w_out, wout_in), (labels, labels_in)]
    moves += [(adjacency.at[b, k], slots_in.at[b, k]) for b in range(here) for k in range(slots)]
    moves = [pltpu.make_async_copy(source, target, sems.at[i]) for i, (source, target) in enumerate(moves)]
    for move in moves:
        move.start()
    core = lax.axis_index("c")
    first = position() * here
    band[...] = jnp.zeros_like(band)
    for move in moves[:4]:
        move.wait()
    high, low = halves(win_in[...])
    win_h[...] = high
    win_l[...] = low
    high, low = halves(wout_in[...])
    classes = high.shape[1]
    for ref, left, right in ((wout_hl, high, low), (wout_hh, high, high), (wout_ll, low, low)):
        ref[:, :classes] = left
        ref[:, classes:] = right
    columns = lax.broadcasted_iota(jnp.int32, (classes, labels_in.shape[1]), 0)
    onehot[...] = jnp.where(columns == labels_in[...], 1.0, 0.0).T
    feat_out[...] = feat_in[...]
    feat_h, feat_l = halves(feat_in[...])
    for b in range(here):
        for k in range(slots):
            moves[4 + b * slots + k].wait()
            near = block_index[b, k] - first
            right = near >= here
            outside = jnp.where(right, near - here, near + here)
            outside += jnp.where(right == (core == 0), 0, 2 * here)
            place = jnp.where((near >= 0) & (near < here), here + near, outside)

            @pl.when(k < block_counts[b])
            def _():
                band[b, place] += slots_in[b, k]

        at = pl.ds(b * rows, rows)
        for s in range(3 * here):
            high, low = halves(band[b, s])
            if here <= s < 2 * here:
                cols = pl.ds((s - here) * rows, rows)
                loc_h[at, cols] = high
                loc_l[at, cols] = low
            else:
                cols = pl.ds((s if s < here else s - here) * rows, rows)
                halo_h[at, cols] = high
                halo_l[at, cols] = low
        s_loc[at, :] = mm(loc_h[at, :], feat_h) + mm(loc_h[at, :], feat_l) + mm(loc_l[at, :], feat_h)


def add_features(halo_h, halo_l, s_loc, feat_e, out):
    half = feat_e.shape[0]
    high, low = halves(feat_e[...])
    he, le = halo_h[:, half:], halo_l[:, half:]
    out[...] = s_loc[...] + mm(he, high) + mm(he, low) + mm(le, high)


def spread_forward(halo_h, halo_l, s_loc, feat_i, win_h, win_l, wout_hl, spread_in, scores):
    half = feat_i.shape[0]
    high, low = halves(feat_i[...])
    for start in range(0, half, CHUNK):
        at = pl.ds(start, CHUNK)
        hi, li = halo_h[at, :half], halo_l[at, :half]
        s = s_loc[at, :] + mm(hi, high) + mm(hi, low) + mm(li, high)
        spread_in[at, :] = s
        s_h, s_l = halves(s)
        pre = mm(s_h, win_h[...]) + mm(s_h, win_l[...]) + mm(s_l, win_h[...])
        hid_h, hid_l = halves(0.5 * pre * erfc(-SQRT_HALF * pre))
        scores[at, :] = fold(mm(hid_h, wout_hl[...]) + mm(hid_l, wout_hl[...]))


def beside_forward(loc_h, loc_l, spread_in, scores, win_h, win_l, slope, hid_th, hid_tl, in_th, in_tl, logits_loc, sco_out):
    sco_out[...] = scores[...]
    s = spread_in[...]
    s_h, s_l = halves(s)
    pre = mm(s_h, win_h[...]) + mm(s_h, win_l[...]) + mm(s_l, win_h[...])
    gate = 0.5 * erfc(-SQRT_HALF * pre)
    slope[...] = gate + pre * (INV_SQRT_2PI * jnp.exp(-0.5 * pre * pre))
    high, low = halves((pre * gate).T)
    hid_th[...] = high
    hid_tl[...] = low
    high, low = halves(s.T)
    in_th[...] = high
    in_tl[...] = low
    pair = jnp.concatenate(halves(scores[...]), axis=1)
    logits_loc[...] = fold(mm(loc_h[...], pair) + mm(loc_l[...], pair))


def add_scores(halo_h, halo_l, logits_loc, sco_e, out):
    half = sco_e.shape[0]
    pair = jnp.concatenate(halves(sco_e[...]), axis=1)
    out[...] = logits_loc[...] + fold(mm(halo_h[:, half:], pair) + mm(halo_l[:, half:], pair))


def classify(halo_h, halo_l, logits_loc, sco_i, onehot, logits, grads_t, loss, out):
    half = sco_i.shape[0]
    classes = logits.shape[1]
    pair = jnp.concatenate(halves(sco_i[...]), axis=1)
    wide = mm(halo_h[:, :half], pair) + mm(halo_l[:, :half], pair)
    values = logits_loc[...] + fold(wide)
    logits[...] = values
    totals = jnp.log(jnp.sum(jnp.exp(values), axis=1, keepdims=True))
    hot = onehot[...]
    row_loss = totals - jnp.sum(hot * values, axis=1, keepdims=True)
    loss[...] = jnp.broadcast_to(jnp.sum(row_loss, axis=0, keepdims=True), loss.shape)
    high, low = halves((jnp.exp(values - totals) - hot).T)
    grads = jnp.concatenate([high, low], axis=0)
    grads_t[...] = grads
    tall = mm(grads, halo_h[:, half:]) + mm(grads, halo_l[:, half:])
    out[...] = tall[:classes] + tall[classes:]


def beside_classify(grads_t, halo_h, halo_l, loc_h, loc_l, out, own):
    grads = grads_t[...]
    classes, half = out.shape
    for ref, high, low in ((out, halo_h[:, :half], halo_l[:, :half]), (own, loc_h[...], loc_l[...])):
        tall = mm(grads, high) + mm(grads, low)
        ref[...] = tall[:classes] + tall[classes:]


def backward(ret_near, ret_i, wout_hh, wout_ll, slope, in_th, in_tl, hid_th, hid_tl, loss,
             hidden_grad, keep, give):
    returned = (ret_near[...] + ret_i[...]).T
    pair = jnp.concatenate(halves(returned), axis=1)
    across = ((1,), (1,))
    grad = mm(pair, wout_hh[...], across) + mm(pair, wout_ll[...], across)
    hidden_grad[...] = grad
    pre_h, pre_l = halves(grad * slope[...])
    grad_in = mm(in_th[...], pre_h) + mm(in_th[...], pre_l) + mm(in_tl[...], pre_h)
    grad_out = fold(mm(hid_th[...], pair) + mm(hid_tl[...], pair))
    grad_out = jnp.where(last_element(grad_out), loss[:1, :], grad_out)
    rows = keep.shape[0]
    pieces = [grad_in[:, t : t + LANES] for t in range(0, grad_in.shape[1], LANES)] + [grad_out]
    core = lax.axis_index("c")
    for first, second in ((keep, give), (give, keep)):

        @pl.when(core == (0 if first is keep else 1))
        def _():
            at = 0
            for piece in pieces:
                ref, start = (first, at) if at < rows else (second, at - rows)
                ref[pl.ds(start, piece.shape[0]), :] = piece
                at += piece.shape[0]


def last_element(value):
    row = lax.broadcasted_iota(jnp.int32, value.shape, 0)
    column = lax.broadcasted_iota(jnp.int32, value.shape, 1)
    return (row == value.shape[0] - 1) & (column == value.shape[1] - 1)


def assemble(nodes_total, own, other, grad_in, grad_out, mean_loss):
    deep = grad_in.shape[0]
    rows = own.shape[0]
    core = lax.axis_index("c")
    for first, second in ((own, other), (other, own)):

        @pl.when(core == (0 if first is own else 1))
        def _():
            tiles = grad_in.shape[1] // LANES
            for t in range(tiles):
                at = t * deep
                ref, start = (first, at) if at < rows else (second, at - rows)
                grad_in[:, pl.ds(t * LANES, LANES)] = ref[pl.ds(start, deep), :]
            grad_out[...] = second[pl.ds(tiles * deep - rows, grad_out.shape[0]), :]

    end = pl.ds(grad_out.shape[0] - 8, 8)
    value = grad_out[end, :]
    there = last_element(value)
    mean_loss[0, 0] = jnp.sum(jnp.where(there, value, 0.0)) / nodes_total
    others = jnp.sum(jnp.where(there, 0.0, value), axis=1, keepdims=True)
    grad_out[end, :] = jnp.where(there, -others, value)


def call(body, outs, args, scalars=0, flops=0, scratch=(), space=pltpu.VMEM, name=""):
    smem = pl.BlockSpec(memory_space=pltpu.SMEM)
    vmem = pl.BlockSpec(memory_space=pltpu.VMEM)
    moved = sum(a.size * a.dtype.itemsize for a in args)
    return pl.pallas_call(
        body,
        out_shape=[jax.ShapeDtypeStruct(shape, kind) for shape, kind in outs],
        in_specs=[smem] * scalars + [pl.BlockSpec(memory_space=space)] * (len(args) - scalars),
        out_specs=[smem if shape == (1, 1) else vmem for shape, _ in outs],
        scratch_shapes=scratch,
        cost_estimate=pl.CostEstimate(flops=flops, bytes_accessed=moved, transcendentals=0),
        compiler_params=pltpu.CompilerParams(vmem_limit_bytes=VMEM_LIMIT),
        name=name or body.__name__,
    )(*args)


def per_device(features, adjacency, block_index, block_counts, labels, weight_in, weight_out):
    devices = lax.axis_size(ALL)
    here, slots, rows = adjacency.shape[:3]
    nodes = here * rows
    deep, hid = weight_in.shape
    classes = weight_out.shape[1]

    feat_e = beside(features, devices)
    loc = ((nodes, nodes), BF16)
    halo = ((nodes, 2 * nodes), BF16)
    w_pair = ((hid, 2 * classes), BF16)
    loc_h, loc_l, halo_h, halo_l, s_loc, win_h, win_l, wout_hl, wout_hh, wout_ll, onehot, feat_out = call(
        prepare,
        [loc, loc, halo, halo, ((nodes, deep), F32), ((deep, hid), BF16), ((deep, hid), BF16),
         w_pair, w_pair, w_pair, ((nodes, classes), F32), ((nodes, deep), F32)],
        [pltpu.with_memory_space_constraint(v, pltpu.HBM)
         for v in (block_index, block_counts, adjacency, features, weight_in, weight_out, labels.reshape(1, nodes))],
        scalars=2,
        flops=6 * nodes * nodes * deep,
        scratch=[
            pltpu.VMEM(adjacency.shape, F32),
            pltpu.VMEM(features.shape, F32),
            pltpu.VMEM(weight_in.shape, F32),
            pltpu.VMEM(weight_out.shape, F32),
            pltpu.VMEM((1, nodes), jnp.int32),
            pltpu.VMEM((here, 3 * here, rows, rows), F32),
            pltpu.SemaphoreType.DMA((4 + here * slots,)),
        ],
        space=pltpu.HBM,
    )
    feat_i = mate(feat_out, devices)
    (s_loc,) = call(
        add_features,
        [((nodes, deep), F32)],
        [halo_h, halo_l, s_loc, feat_e],
        flops=6 * nodes * nodes * deep,
    )
    spread_in, scores = call(
        spread_forward,
        [((nodes, deep), F32), ((nodes, classes), F32)],
        [halo_h, halo_l, s_loc, feat_i, win_h, win_l, wout_hl],
        flops=20 * nodes * nodes * deep,
    )
    sco_e = beside(scores, devices)
    slope, hid_th, hid_tl, in_th, in_tl, logits_loc, sco_out = call(
        beside_forward,
        [((nodes, hid), F32), ((hid, nodes), BF16), ((hid, nodes), BF16), ((deep, nodes), BF16), ((deep, nodes), BF16),
         ((nodes, classes), F32), ((nodes, classes), F32)],
        [loc_h, loc_l, spread_in, scores, win_h, win_l],
        flops=12 * nodes * nodes * deep,
    )
    sco_i = mate(sco_out, devices)
    (logits_loc,) = call(
        add_scores,
        [((nodes, classes), F32)],
        [halo_h, halo_l, logits_loc, sco_e],
        flops=8 * nodes * nodes * classes,
    )
    logits, grads_t, loss, out_e = call(
        classify,
        [((nodes, classes), F32), ((2 * classes, nodes), BF16), ((8, LANES), F32), ((classes, nodes), F32)],
        [halo_h, halo_l, logits_loc, sco_i, onehot],
        flops=12 * nodes * nodes * classes,
    )
    ret_e = beside(out_e, devices)
    out_i, ret_loc = call(
        beside_classify,
        [((classes, nodes), F32), ((classes, nodes), F32)],
        [grads_t, halo_h, halo_l, loc_h, loc_l],
        flops=16 * nodes * nodes * classes,
    )
    ret_i = mate(out_i, devices)
    ret_near = ret_loc + ret_e
    half = (deep * hid + hid * classes) // LANES // 2
    hidden_grad, keep, give = call(
        backward,
        [((nodes, hid), F32), ((half, LANES), F32), ((half, LANES), F32)],
        [ret_near, ret_i, wout_hh, wout_ll, slope, in_th, in_tl, hid_th, hid_tl, loss],
        flops=12 * nodes * nodes * deep,
    )
    big, mid = lax.axis_size(BIG), lax.axis_size(MID)
    mine = (keep + mate(give, devices)).reshape(big, half // big, LANES)
    summed = jnp.sum(exchange(mine, BIG), axis=0)
    summed = jnp.sum(exchange(spread(summed, mid), MID), axis=0)
    own = exchange(spread(summed, big), BIG).reshape(half, LANES)
    other = mate(own, devices)
    grad_in, grad_out, mean_loss = call(
        functools.partial(assemble, nodes * devices),
        [((deep, hid), F32), ((hid, classes), F32), ((1, 1), F32)],
        [own, other],
        name="assemble",
    )
    return (logits, mean_loss.reshape(()), hidden_grad, grad_in, grad_out)


def solution(mesh):
    grid = Mesh(mesh.devices.reshape(4, 8, 8, 2), ALL)
    split = P(ALL)
    return jax.shard_map(
        per_device,
        mesh=grid,
        in_specs=(split, split, split, split, split, P(), P()),
        out_specs=(split, P(), split, P(), P()),
        check_vma=False,
    )
```

```python
import functools
import math

import jax
import jax.numpy as jnp
import numpy as np
from jax import lax
from jax.experimental import pallas as pl
from jax.experimental.pallas import tpu as pltpu
from jax.sharding import PartitionSpec as P

AXIS = "rows"
GRID = (4, 8, 8, 2)
X, Z, Y = range(3)
LANES = 128
F32 = jnp.float32
BF16 = jnp.bfloat16
VMEM_LIMIT = 24 * 1024 * 1024
CHUNK = 256
SQRT_HALF = 0.7071067811865476
INV_SQRT_2PI = 0.3989422804014327


def mate(value):
    return lax.ppermute(value, AXIS, [(i, i ^ 1) for i in range(lax.axis_size(AXIS))])


def beside(value):
    pairs = [(i, i + 1) for i in range(1, lax.axis_size(AXIS) - 1, 2)]
    return lax.ppermute(value, AXIS, pairs + [(b, a) for a, b in pairs])


def groups(*per_core):
    ids = np.arange(math.prod(GRID)).reshape(GRID)
    found = []
    for core, axes in enumerate(per_core):
        rest = [axis for axis in range(3) if axis not in axes]
        size = math.prod(GRID[axis] for axis in axes)
        found += ids[..., core].transpose(rest + list(axes)).reshape(-1, size).tolist()
    return found


def exchange(value, members):
    return lax.all_to_all(value, AXIS, 0, 0, axis_index_groups=members, tiled=True)


def spread(value, count):
    return jnp.broadcast_to(value[None], (count,) + value.shape)


def halves(value):
    high = value.astype(BF16)
    return high, (value - high.astype(F32)).astype(BF16)


def mm(a, b, dims=((1,), (0,))):
    return lax.dot_general(a, b, (dims, ((), ())), preferred_element_type=F32)


def fold(wide):
    half = wide.shape[1] // 2
    return wide[:, :half] + wide[:, half:]


def erfc(value):
    size = jnp.abs(value)
    t = 1.0 / (1.0 + 0.5 * size)
    poly = jnp.full_like(t, 0.17087277)
    for term in (-0.82215223, 1.48851587, -1.13520398, 0.27886807, -0.18628806, 0.09678418,
                 0.37409196, 1.00002368, -1.26551223):
        poly = poly * t + term
    tail = t * jnp.exp(poly - size * size)
    return jnp.where(value < 0, 2.0 - tail, tail)


def prepare(block_index, block_counts, adjacency, features, w_in, w_out, labels,
            loc_h, loc_l, halo_h, halo_l, s_loc, win_h, win_l, wout_hl, wout_hh, wout_ll, onehot, feat_out,
            slots_in, feat_in, win_in, wout_in, labels_in, band, sems):
    here, slots, rows, _ = adjacency.shape
    moves = [(features, feat_in), (w_in, win_in), (w_out, wout_in), (labels, labels_in)]
    moves += [(adjacency.at[b, k], slots_in.at[b, k]) for b in range(here) for k in range(slots)]
    moves = [pltpu.make_async_copy(source, target, sems.at[i]) for i, (source, target) in enumerate(moves)]
    for move in moves:
        move.start()
    me = lax.axis_index(AXIS)
    core = lax.rem(me, 2)
    first = me * here
    band[...] = jnp.zeros_like(band)
    for move in moves[:4]:
        move.wait()
    high, low = halves(win_in[...])
    win_h[...] = high
    win_l[...] = low
    high, low = halves(wout_in[...])
    classes = high.shape[1]
    for ref, left, right in ((wout_hl, high, low), (wout_hh, high, high), (wout_ll, low, low)):
        ref[:, :classes] = left
        ref[:, classes:] = right
    columns = lax.broadcasted_iota(jnp.int32, (classes, labels_in.shape[1]), 0)
    onehot[...] = jnp.where(columns == labels_in[...], 1.0, 0.0).T
    feat_out[...] = feat_in[...]
    feat_h, feat_l = halves(feat_in[...])
    for b in range(here):
        for k in range(slots):
            moves[4 + b * slots + k].wait()
            near = block_index[b, k] - first
            right = near >= here
            outside = jnp.where(right, near - here, near + here)
            outside += jnp.where(right == (core == 0), 0, 2 * here)
            place = jnp.where((near >= 0) & (near < here), here + near, outside)

            @pl.when(k < block_counts[b])
            def _():
                band[b, place] += slots_in[b, k]

        at = pl.ds(b * rows, rows)
        for s in range(3 * here):
            high, low = halves(band[b, s])
            if here <= s < 2 * here:
                cols = pl.ds((s - here) * rows, rows)
                loc_h[at, cols] = high
                loc_l[at, cols] = low
            else:
                cols = pl.ds((s if s < here else s - here) * rows, rows)
                halo_h[at, cols] = high
                halo_l[at, cols] = low
        s_loc[at, :] = mm(loc_h[at, :], feat_h) + mm(loc_h[at, :], feat_l) + mm(loc_l[at, :], feat_h)


def add_features(halo_h, halo_l, s_loc, feat_e, out):
    half = feat_e.shape[0]
    high, low = halves(feat_e[...])
    he, le = halo_h[:, half:], halo_l[:, half:]
    out[...] = s_loc[...] + mm(he, high) + mm(he, low) + mm(le, high)


def spread_forward(halo_h, halo_l, s_loc, feat_i, win_h, win_l, wout_hl, spread_in, scores):
    half = feat_i.shape[0]
    high, low = halves(feat_i[...])
    for start in range(0, half, CHUNK):
        at = pl.ds(start, CHUNK)
        hi, li = halo_h[at, :half], halo_l[at, :half]
        s = s_loc[at, :] + mm(hi, high) + mm(hi, low) + mm(li, high)
        spread_in[at, :] = s
        s_h, s_l = halves(s)
        pre = mm(s_h, win_h[...]) + mm(s_h, win_l[...]) + mm(s_l, win_h[...])
        hid_h, hid_l = halves(0.5 * pre * erfc(-SQRT_HALF * pre))
        scores[at, :] = fold(mm(hid_h, wout_hl[...]) + mm(hid_l, wout_hl[...]))


def beside_forward(loc_h, loc_l, spread_in, scores, win_h, win_l, slope, hid_th, hid_tl, in_th, in_tl, logits_loc, sco_out):
    sco_out[...] = scores[...]
    s = spread_in[...]
    s_h, s_l = halves(s)
    pre = mm(s_h, win_h[...]) + mm(s_h, win_l[...]) + mm(s_l, win_h[...])
    gate = 0.5 * erfc(-SQRT_HALF * pre)
    slope[...] = gate + pre * (INV_SQRT_2PI * jnp.exp(-0.5 * pre * pre))
    high, low = halves((pre * gate).T)
    hid_th[...] = high
    hid_tl[...] = low
    high, low = halves(s.T)
    in_th[...] = high
    in_tl[...] = low
    pair = jnp.concatenate(halves(scores[...]), axis=1)
    logits_loc[...] = fold(mm(loc_h[...], pair) + mm(loc_l[...], pair))


def add_scores(halo_h, halo_l, logits_loc, sco_e, out):
    half = sco_e.shape[0]
    pair = jnp.concatenate(halves(sco_e[...]), axis=1)
    out[...] = logits_loc[...] + fold(mm(halo_h[:, half:], pair) + mm(halo_l[:, half:], pair))


def classify(halo_h, halo_l, logits_loc, sco_i, onehot, logits, grads_t, out):
    half = sco_i.shape[0]
    classes = logits.shape[1]
    pair = jnp.concatenate(halves(sco_i[...]), axis=1)
    wide = mm(halo_h[:, :half], pair) + mm(halo_l[:, :half], pair)
    values = logits_loc[...] + fold(wide)
    logits[...] = values
    totals = jnp.log(jnp.sum(jnp.exp(values), axis=1, keepdims=True))
    high, low = halves((jnp.exp(values - totals) - onehot[...]).T)
    grads = jnp.concatenate([high, low], axis=0)
    grads_t[...] = grads
    tall = mm(grads, halo_h[:, half:]) + mm(grads, halo_l[:, half:])
    out[...] = tall[:classes] + tall[classes:]


def beside_classify(grads_t, halo_h, halo_l, loc_h, loc_l, values, onehot, out, own, logits, loss):
    grads = grads_t[...]
    classes, half = out.shape
    for ref, high, low in ((out, halo_h[:, :half], halo_l[:, :half]), (own, loc_h[...], loc_l[...])):
        tall = mm(grads, high) + mm(grads, low)
        ref[...] = tall[:classes] + tall[classes:]
    scores = values[...]
    logits[...] = scores
    totals = jnp.log(jnp.sum(jnp.exp(scores), axis=1, keepdims=True))
    row_loss = totals - jnp.sum(onehot[...] * scores, axis=1, keepdims=True)
    loss[...] = jnp.broadcast_to(jnp.sum(row_loss, axis=0, keepdims=True), loss.shape)


def gradient_half(which, in_th, in_tl, hid_th, hid_tl, pre_h, pre_l, pair, loss, out):
    deep = in_th.shape[0] // 2
    hid = hid_th.shape[0] // 2
    at = pl.ds(pl.multiple_of(which * deep, deep), deep)
    high, low = in_th[at, :], in_tl[at, :]
    tall = mm(jnp.concatenate([high, low], axis=0), pre_h)
    grad_in = tall[:deep] + tall[deep:] + mm(high, pre_l)
    for t in range(grad_in.shape[1] // LANES):
        out[pl.ds(t * deep, deep), :] = grad_in[:, t * LANES : (t + 1) * LANES]
    at = pl.ds(pl.multiple_of(which * hid, hid), hid)
    grad_out = fold(mm(hid_th[at, :], pair) + mm(hid_tl[at, :], pair))
    grad_out = jnp.where(last_element(grad_out) & (which == 1), loss[:1, :], grad_out)
    out[pl.ds(out.shape[0] - hid, hid), :] = grad_out


def last_element(value):
    row = lax.broadcasted_iota(jnp.int32, value.shape, 0)
    column = lax.broadcasted_iota(jnp.int32, value.shape, 1)
    return (row == value.shape[0] - 1) & (column == value.shape[1] - 1)


def backward(ret_near, ret_i, wout_hh, wout_ll, slope, in_th, in_tl, hid_th, hid_tl, loss,
             grad, pre_h, pre_l, pair, give):
    returned = (ret_near[...] + ret_i[...]).T
    both = jnp.concatenate(halves(returned), axis=1)
    pair[...] = both
    across = ((1,), (1,))
    hidden_grad = mm(both, wout_hh[...], across) + mm(both, wout_ll[...], across)
    grad[...] = hidden_grad
    high, low = halves(hidden_grad * slope[...])
    pre_h[...] = high
    pre_l[...] = low
    other = 1 - lax.rem(lax.axis_index(AXIS), 2)
    gradient_half(other, in_th, in_tl, hid_th, hid_tl, high, low, both, loss, give)


def beside_backward(grad, pre_h, pre_l, pair, in_th, in_tl, hid_th, hid_tl, loss, hidden_grad, keep):
    hidden_grad[...] = grad[...]
    core = lax.rem(lax.axis_index(AXIS), 2)
    gradient_half(core, in_th, in_tl, hid_th, hid_tl, pre_h[...], pre_l[...], pair[...], loss, keep)


def assemble(nodes_total, own, other, grad_in, grad_out, mean_loss, ends, sems):
    deep = grad_in.shape[0] // 2
    hid = grad_out.shape[0] // 2
    tiles = grad_in.shape[1] // LANES
    core = lax.rem(lax.axis_index(AXIS), 2)
    moves = []

    def move(source, target):
        moves.append(pltpu.make_async_copy(source, target, sems.at[len(moves)]))
        moves[-1].start()

    for k, (half, which) in enumerate(((own, core), (other, 1 - core))):
        rows = pl.ds(pl.multiple_of(which * deep, deep), deep)
        for t in range(tiles):
            move(half.at[pl.ds(t * deep, deep), :], grad_in.at[rows, pl.ds(t * LANES, LANES)])
        start = pl.multiple_of(which * hid, hid)
        move(half.at[pl.ds(tiles * deep, hid - 8), :], grad_out.at[pl.ds(start, hid - 8), :])
        value = half[pl.ds(tiles * deep + hid - 8, 8), :]
        there = last_element(value) & (which == 1)
        loss = jnp.sum(jnp.where(there, value, 0.0))
        others = jnp.sum(jnp.where(there, 0.0, value), axis=1, keepdims=True)
        ends[k] = jnp.where(there, -others, value)
        move(ends.at[k], grad_out.at[pl.ds(start + hid - 8, 8), :])
        if k == 0:
            total = loss
    mean_loss[0, 0] = (total + loss) / nodes_total
    for copy in moves:
        copy.wait()


def call(body, outs, args, scalars=0, flops=0, scratch=(), space=pltpu.VMEM, out_space=pltpu.VMEM, name=""):
    smem = pl.BlockSpec(memory_space=pltpu.SMEM)
    out_spec = pl.BlockSpec(memory_space=out_space)
    moved = sum(a.size * a.dtype.itemsize for a in args)
    return pl.pallas_call(
        body,
        out_shape=[jax.ShapeDtypeStruct(shape, kind) for shape, kind in outs],
        in_specs=[smem] * scalars + [pl.BlockSpec(memory_space=space)] * (len(args) - scalars),
        out_specs=[smem if shape == (1, 1) else out_spec for shape, _ in outs],
        scratch_shapes=scratch,
        cost_estimate=pl.CostEstimate(flops=flops, bytes_accessed=moved, transcendentals=0),
        compiler_params=pltpu.CompilerParams(vmem_limit_bytes=VMEM_LIMIT),
        name=name or body.__name__,
    )(*args)


def per_device(features, adjacency, block_index, block_counts, labels, weight_in, weight_out):
    here, slots, rows = adjacency.shape[:3]
    nodes = here * rows
    deep, hid = weight_in.shape
    classes = weight_out.shape[1]

    feat_e = beside(features)
    loc = ((nodes, nodes), BF16)
    halo = ((nodes, 2 * nodes), BF16)
    w_pair = ((hid, 2 * classes), BF16)
    loc_h, loc_l, halo_h, halo_l, s_loc, win_h, win_l, wout_hl, wout_hh, wout_ll, onehot, feat_out = call(
        prepare,
        [loc, loc, halo, halo, ((nodes, deep), F32), ((deep, hid), BF16), ((deep, hid), BF16),
         w_pair, w_pair, w_pair, ((nodes, classes), F32), ((nodes, deep), F32)],
        [pltpu.with_memory_space_constraint(v, pltpu.HBM)
         for v in (block_index, block_counts, adjacency, features, weight_in, weight_out, labels.reshape(1, nodes))],
        scalars=2,
        flops=6 * nodes * nodes * deep,
        scratch=[
            pltpu.VMEM(adjacency.shape, F32),
            pltpu.VMEM(features.shape, F32),
            pltpu.VMEM(weight_in.shape, F32),
            pltpu.VMEM(weight_out.shape, F32),
            pltpu.VMEM((1, nodes), jnp.int32),
            pltpu.VMEM((here, 3 * here, rows, rows), F32),
            pltpu.SemaphoreType.DMA((4 + here * slots,)),
        ],
        space=pltpu.HBM,
    )
    feat_i = mate(feat_out)
    (s_loc,) = call(
        add_features,
        [((nodes, deep), F32)],
        [halo_h, halo_l, s_loc, feat_e],
        flops=6 * nodes * nodes * deep,
    )
    spread_in, scores = call(
        spread_forward,
        [((nodes, deep), F32), ((nodes, classes), F32)],
        [halo_h, halo_l, s_loc, feat_i, win_h, win_l, wout_hl],
        flops=20 * nodes * nodes * deep,
    )
    sco_e = beside(scores)
    slope, hid_th, hid_tl, in_th, in_tl, logits_loc, sco_out = call(
        beside_forward,
        [((nodes, hid), F32), ((hid, nodes), BF16), ((hid, nodes), BF16), ((deep, nodes), BF16), ((deep, nodes), BF16),
         ((nodes, classes), F32), ((nodes, classes), F32)],
        [loc_h, loc_l, spread_in, scores, win_h, win_l],
        flops=12 * nodes * nodes * deep,
    )
    sco_i = mate(sco_out)
    (logits_loc,) = call(
        add_scores,
        [((nodes, classes), F32)],
        [halo_h, halo_l, logits_loc, sco_e],
        flops=8 * nodes * nodes * classes,
    )
    values, grads_t, out_e = call(
        classify,
        [((nodes, classes), F32), ((2 * classes, nodes), BF16), ((classes, nodes), F32)],
        [halo_h, halo_l, logits_loc, sco_i, onehot],
        flops=12 * nodes * nodes * classes,
    )
    ret_e = beside(out_e)
    out_i, ret_loc, logits, loss = call(
        beside_classify,
        [((classes, nodes), F32), ((classes, nodes), F32), ((nodes, classes), F32), ((8, LANES), F32)],
        [grads_t, halo_h, halo_l, loc_h, loc_l, values, onehot],
        flops=16 * nodes * nodes * classes,
    )
    ret_i = mate(out_i)
    ret_near = ret_loc + ret_e
    half = (deep * hid + hid * classes) // LANES // 2
    sides = [in_th, in_tl, hid_th, hid_tl, loss]
    grad, pre_h, pre_l, pair, give = call(
        backward,
        [((nodes, hid), F32), ((nodes, hid), BF16), ((nodes, hid), BF16), ((nodes, 2 * classes), BF16),
         ((half, LANES), F32)],
        [ret_near, ret_i, wout_hh, wout_ll, slope, *sides],
        flops=12 * nodes * nodes * deep,
    )
    got = mate(give)
    hidden_grad, keep = call(
        beside_backward,
        [((nodes, hid), F32), ((half, LANES), F32)],
        [grad, pre_h, pre_l, pair, *sides],
        flops=6 * nodes * nodes * deep,
    )
    big, mid = groups((X, Y), (X, Z)), groups((Z,), (Y,))
    wide, narrow = len(big[0]), len(mid[0])
    mine = (keep + got).reshape(wide, half // wide, LANES)
    summed = jnp.sum(exchange(mine, big), axis=0)
    summed = jnp.sum(exchange(spread(summed, narrow), mid), axis=0)
    own = exchange(spread(summed, wide), big).reshape(half, LANES)
    other = mate(own)
    grad_in, grad_out, mean_loss = call(
        functools.partial(assemble, nodes * lax.axis_size(AXIS)),
        [((deep, hid), F32), ((hid, classes), F32), ((1, 1), F32)],
        [own, other],
        scratch=[pltpu.VMEM((2, 8, LANES), F32), pltpu.SemaphoreType.DMA((2 * (hid // LANES + 2),))],
        out_space=pltpu.HBM,
        name="assemble",
    )
    return (logits, mean_loss.reshape(()), hidden_grad, grad_in, grad_out)


def solution(mesh):
    split = P(AXIS)
    return jax.shard_map(
        per_device,
        mesh=mesh,
        in_specs=(split, split, split, split, split, P(), P()),
        out_specs=(split, P(), split, P(), P()),
        check_vma=False,
    )
```

```python
import functools
import math

import jax
import jax.numpy as jnp
import numpy as np
from jax import lax
from jax.experimental import pallas as pl
from jax.experimental.pallas import tpu as pltpu
from jax.sharding import PartitionSpec as P

AXIS = "rows"
GRID = (4, 8, 8, 2)
X, Z, Y = range(3)
LANES = 128
F32 = jnp.float32
BF16 = jnp.bfloat16
VMEM_LIMIT = 24 * 1024 * 1024
CHUNK = 256
SQRT_HALF = 0.7071067811865476
INV_SQRT_2PI = 0.3989422804014327


def mate(value):
    return lax.ppermute(value, AXIS, [(i, i ^ 1) for i in range(lax.axis_size(AXIS))])


def beside(value):
    pairs = [(i, i + 1) for i in range(1, lax.axis_size(AXIS) - 1, 2)]
    return lax.ppermute(value, AXIS, pairs + [(b, a) for a, b in pairs])


def groups(*per_core):
    ids = np.arange(math.prod(GRID)).reshape(GRID)
    found = []
    for core, axes in enumerate(per_core):
        rest = [axis for axis in range(3) if axis not in axes]
        size = math.prod(GRID[axis] for axis in axes)
        found += ids[..., core].transpose(rest + list(axes)).reshape(-1, size).tolist()
    return found


def exchange(value, members):
    return lax.all_to_all(value, AXIS, 0, 0, axis_index_groups=members, tiled=True)


def repeated(value, count):
    return jnp.broadcast_to(value[None], (count,) + value.shape)


def halves(value):
    high = value.astype(BF16)
    return high, (value - high.astype(F32)).astype(BF16)


def mm(a, b, dims=((1,), (0,))):
    return lax.dot_general(a, b, (dims, ((), ())), preferred_element_type=F32)


def fold(wide):
    half = wide.shape[1] // 2
    return wide[:, :half] + wide[:, half:]


def erfc(value):
    size = jnp.abs(value)
    t = 1.0 / (1.0 + 0.5 * size)
    poly = jnp.full_like(t, 0.17087277)
    for term in (-0.82215223, 1.48851587, -1.13520398, 0.27886807, -0.18628806, 0.09678418,
                 0.37409196, 1.00002368, -1.26551223):
        poly = poly * t + term
    tail = t * jnp.exp(poly - size * size)
    return jnp.where(value < 0, 2.0 - tail, tail)


def prepare(block_index, block_counts, adjacency, features, w_in, w_out, labels,
            loc_h, loc_l, halo_h, halo_l, s_loc, win_h, win_l, wout_hl, wout_hh, wout_ll, onehot, feat_out,
            slots_in, feat_in, win_in, wout_in, labels_in, band, sems):
    here, slots, rows, _ = adjacency.shape
    moves = [(features, feat_in), (w_in, win_in), (w_out, wout_in), (labels, labels_in)]
    moves += [(adjacency.at[b, k], slots_in.at[b, k]) for b in range(here) for k in range(slots)]
    moves = [pltpu.make_async_copy(source, target, sems.at[i]) for i, (source, target) in enumerate(moves)]
    for move in moves:
        move.start()
    me = lax.axis_index(AXIS)
    core = lax.rem(me, 2)
    first = me * here
    band[...] = jnp.zeros_like(band)
    for move in moves[:4]:
        move.wait()
    high, low = halves(win_in[...])
    win_h[...] = high
    win_l[...] = low
    high, low = halves(wout_in[...])
    classes = high.shape[1]
    for ref, left, right in ((wout_hl, high, low), (wout_hh, high, high), (wout_ll, low, low)):
        ref[:, :classes] = left
        ref[:, classes:] = right
    columns = lax.broadcasted_iota(jnp.int32, (classes, labels_in.shape[1]), 0)
    onehot[...] = jnp.where(columns == labels_in[...], 1.0, 0.0).T
    feat_out[...] = feat_in[...]
    feat_h, feat_l = halves(feat_in[...])
    for b in range(here):
        for k in range(slots):
            moves[4 + b * slots + k].wait()
            near = block_index[b, k] - first
            right = near >= here
            outside = jnp.where(right, near - here, near + here)
            outside += jnp.where(right == (core == 0), 0, 2 * here)
            place = jnp.where((near >= 0) & (near < here), here + near, outside)

            @pl.when(k < block_counts[b])
            def _():
                band[b, place] += slots_in[b, k]

        at = pl.ds(b * rows, rows)
        for s in range(3 * here):
            high, low = halves(band[b, s])
            if here <= s < 2 * here:
                cols = pl.ds((s - here) * rows, rows)
                loc_h[at, cols] = high
                loc_l[at, cols] = low
            else:
                cols = pl.ds((s if s < here else s - here) * rows, rows)
                halo_h[at, cols] = high
                halo_l[at, cols] = low
        s_loc[at, :] = mm(loc_h[at, :], feat_h) + mm(loc_h[at, :], feat_l) + mm(loc_l[at, :], feat_h)


def add_features(halo_h, halo_l, s_loc, feat_e, out):
    half = feat_e.shape[0]
    high, low = halves(feat_e[...])
    he, le = halo_h[:, half:], halo_l[:, half:]
    out[...] = s_loc[...] + mm(he, high) + mm(he, low) + mm(le, high)


def spread(halo_h, halo_l, s_loc, feat_i, spread_in):
    half = feat_i.shape[0]
    high, low = halves(feat_i[...])
    hi, li = halo_h[:, :half], halo_l[:, :half]
    spread_in[...] = s_loc[...] + mm(hi, high) + mm(hi, low) + mm(li, high)


def layer(spread_in, win_h, win_l):
    s_h, s_l = halves(spread_in)
    pre = mm(s_h, win_h[...]) + mm(s_h, win_l[...]) + mm(s_l, win_h[...])
    gate = 0.5 * erfc(-SQRT_HALF * pre)
    return pre * gate, gate + pre * (INV_SQRT_2PI * jnp.exp(-0.5 * pre * pre))


def forward(high_band, low_band, spread_in, win_h, win_l, wout_hl, logits_before,
            scores_sum, slope, hid_h, hid_l, *in_t, first, part):
    hidden, slope[...] = layer(spread_in[...], win_h, win_l)
    high, low = halves(hidden)
    hid_h[...] = high
    hid_l[...] = low
    pair = jnp.concatenate(halves(fold(mm(high, wout_hl[...]) + mm(low, wout_hl[...]))), axis=1)
    nodes = spread_in.shape[0]
    cols = slice(part * nodes, (part + 1) * nodes)
    logits = fold(mm(high_band[:, cols], pair) + mm(low_band[:, cols], pair))
    scores_sum[...] = logits if first else logits_before[...] + logits
    if in_t:
        turn(spread_in, *in_t)


def turn(spread_in, in_th, in_tl):
    high, low = halves(spread_in[...].T)
    in_th[...] = high
    in_tl[...] = low


def stacked(grads, high, low):
    tall = mm(grads, high) + mm(grads, low)
    half = tall.shape[0] // 2
    return tall[:half] + tall[half:]


def classify(values, onehot, grads_t, loss):
    scores = values[...]
    totals = jnp.log(jnp.sum(jnp.exp(scores), axis=1, keepdims=True))
    hot = onehot[...]
    grads_t[...] = jnp.concatenate(halves((jnp.exp(scores - totals) - hot).T), axis=0)
    row_loss = totals - jnp.sum(hot * scores, axis=1, keepdims=True)
    loss[...] = jnp.broadcast_to(jnp.sum(row_loss, axis=0, keepdims=True), loss.shape)


def gradient_half(which, in_ts, pre, grad_out_t, loss, out):
    deep = in_ts[0][0].shape[0] // 2
    at = pl.ds(pl.multiple_of(which * deep, deep), deep)
    grad_in = 0.0
    for (in_th, in_tl), (pre_h, pre_l) in zip(in_ts, pre, strict=True):
        high, low = in_th[at, :], in_tl[at, :]
        tall = mm(jnp.concatenate([high, low], axis=0), pre_h)
        grad_in = grad_in + (tall[:deep] + tall[deep:] + mm(high, pre_l))
    for t in range(grad_in.shape[1] // LANES):
        out[pl.ds(t * deep, deep), :] = grad_in[:, t * LANES : (t + 1) * LANES]
    hid = grad_out_t.shape[1] // 2
    grad_out = jnp.where(which == 1, grad_out_t[:, hid:], grad_out_t[:, :hid]).T
    grad_out = jnp.where(last_element(grad_out) & (which == 1), loss[:1, :], grad_out)
    rows = deep * (grad_in.shape[1] // LANES)
    out[pl.ds(rows, hid), :] = grad_out
    return rows + hid


def last_element(value):
    row = lax.broadcasted_iota(jnp.int32, value.shape, 0)
    column = lax.broadcasted_iota(jnp.int32, value.shape, 1)
    return (row == value.shape[0] - 1) & (column == value.shape[1] - 1)


def backward(grads_t, halo_h, halo_l, loc_h, loc_l, slope_o, slope_i, slope_e, hid_oh, hid_ol, hid_ih, hid_il, hid_eh, hid_el,
             in_oh, in_ol, in_ih, in_il, in_eh, in_el, wout_hh, wout_ll, loss,
             pre_oh, pre_ol, pre_ih, pre_il, pre_eh, pre_el, total_out_t, ret_loc, out_e, give):
    grads = grads_t[...]
    half = loc_h.shape[1]
    own = stacked(grads, loc_h[...], loc_l[...])
    near = stacked(grads, halo_h[:, :half], halo_l[:, :half])
    far = stacked(grads, halo_h[:, half:], halo_l[:, half:])
    ret_loc[...] = own
    out_e[...] = far
    across = ((1,), (1,))
    grad_out_t = 0.0
    pre = []
    for returned_t, slope, hid_h, hid_l, pre_h, pre_l in (
        (own, slope_o, hid_oh, hid_ol, pre_oh, pre_ol),
        (near, slope_i, hid_ih, hid_il, pre_ih, pre_il),
        (far, slope_e, hid_eh, hid_el, pre_eh, pre_el),
    ):
        both = jnp.concatenate(halves(returned_t.T), axis=1)
        hidden_grad = mm(both, wout_hh[...], across) + mm(both, wout_ll[...], across)
        high, low = halves(hidden_grad * slope[...])
        pre_h[...] = high
        pre_l[...] = low
        pre.append((high, low))
        tall = jnp.concatenate(halves(returned_t), axis=0)
        grad_out_t = grad_out_t + stacked(tall, hid_h[...], hid_l[...])
    total_out_t[...] = grad_out_t
    other = 1 - lax.rem(lax.axis_index(AXIS), 2)
    in_ts = ((in_oh, in_ol), (in_ih, in_il), (in_eh, in_el))
    end = gradient_half(other, in_ts, pre, grad_out_t, loss, give)
    classes = near.shape[0]
    for t in range(half // LANES):
        give[pl.ds(end + t * classes, classes), :] = near[:, t * LANES : (t + 1) * LANES]


def backward_kept(in_oh, in_ol, in_ih, in_il, in_eh, in_el, pre_oh, pre_ol, pre_ih, pre_il, pre_eh, pre_el,
                  total_out_t, loss, values, keep, logits):
    core = lax.rem(lax.axis_index(AXIS), 2)
    in_ts = ((in_oh, in_ol), (in_ih, in_il), (in_eh, in_el))
    pre = [(h[...], l[...]) for h, l in ((pre_oh, pre_ol), (pre_ih, pre_il), (pre_eh, pre_el))]
    gradient_half(core, in_ts, pre, total_out_t[...], loss, keep)
    logits[...] = values[...]


def finish_hidden(ret_loc, ret_e, got, wout_hh, wout_ll, hidden_grad):
    classes, nodes = ret_loc.shape
    start = got.shape[0] - classes * (nodes // LANES)
    ret_i = [got[pl.ds(start + t * classes, classes), :] for t in range(nodes // LANES)]
    returned_t = ret_loc[...] + ret_e[...] + jnp.concatenate(ret_i, axis=1)
    both = jnp.concatenate(halves(returned_t.T), axis=1)
    across = ((1,), (1,))
    hidden_grad[...] = mm(both, wout_hh[...], across) + mm(both, wout_ll[...], across)


def add_halves(keep, got, out):
    out[...] = keep[...] + got[: keep.shape[0], :]


def sum_repeated(received, passed, out, copied):
    total = received[0]
    for k in range(1, received.shape[0]):
        total = total + received[k]
    out[...] = jnp.broadcast_to(total[None], out.shape)
    copied[...] = passed[...]


def sum_repeated_after(received, after, out):
    del after
    total = received[0]
    for k in range(1, received.shape[0]):
        total = total + received[k]
    out[...] = jnp.broadcast_to(total[None], out.shape)


def assemble(nodes_total, own, other, grad_in, grad_out, mean_loss):
    deep = grad_in.shape[0] // 2
    hid = grad_out.shape[0] // 2
    tiles = grad_in.shape[1] // LANES
    core = lax.rem(lax.axis_index(AXIS), 2)
    for half, which in ((own, core), (other, 1 - core)):
        at = pl.ds(pl.multiple_of(which * deep, deep), deep)
        for t in range(tiles):
            grad_in[at, t * LANES : (t + 1) * LANES] = half[pl.ds(t * deep, deep), :]
        at = pl.ds(pl.multiple_of(which * hid, hid), hid)
        grad_out[at, :] = half[pl.ds(tiles * deep, hid), :]
    end = pl.ds(2 * hid - 8, 8)
    value = grad_out[end, :]
    there = last_element(value)
    mean_loss[0, 0] = jnp.sum(jnp.where(there, value, 0.0)) / nodes_total
    others = jnp.sum(jnp.where(there, 0.0, value), axis=1, keepdims=True)
    grad_out[end, :] = jnp.where(there, -others, value)


def call(body, outs, args, scalars=0, anywhere=0, flops=0, scratch=(), space=pltpu.VMEM, name=""):
    smem = pl.BlockSpec(memory_space=pltpu.SMEM)
    vmem = pl.BlockSpec(memory_space=pltpu.VMEM)
    moved = sum(a.size * a.dtype.itemsize for a in args)
    return pl.pallas_call(
        body,
        out_shape=[jax.ShapeDtypeStruct(shape, kind) for shape, kind in outs],
        in_specs=[smem] * scalars
        + [pl.BlockSpec(memory_space=space)] * (len(args) - scalars - anywhere)
        + [pl.BlockSpec(memory_space=pl.ANY)] * anywhere,
        out_specs=[smem if shape == (1, 1) else vmem for shape, _ in outs],
        scratch_shapes=scratch,
        cost_estimate=pl.CostEstimate(flops=flops, bytes_accessed=moved, transcendentals=0),
        compiler_params=pltpu.CompilerParams(vmem_limit_bytes=VMEM_LIMIT),
        name=name or body.__name__,
    )(*args)


def per_device(features, adjacency, block_index, block_counts, labels, weight_in, weight_out):
    here, slots, rows = adjacency.shape[:3]
    nodes = here * rows
    deep, hid = weight_in.shape
    classes = weight_out.shape[1]

    feat_e = beside(features)
    loc = ((nodes, nodes), BF16)
    halo = ((nodes, 2 * nodes), BF16)
    w_pair = ((hid, 2 * classes), BF16)
    loc_h, loc_l, halo_h, halo_l, s_loc, win_h, win_l, wout_hl, wout_hh, wout_ll, onehot, feat_out = call(
        prepare,
        [loc, loc, halo, halo, ((nodes, deep), F32), ((deep, hid), BF16), ((deep, hid), BF16),
         w_pair, w_pair, w_pair, ((nodes, classes), F32), ((nodes, deep), F32)],
        [pltpu.with_memory_space_constraint(v, pltpu.HBM)
         for v in (block_index, block_counts, adjacency, features, weight_in, weight_out, labels.reshape(1, nodes))],
        scalars=2,
        flops=6 * nodes * nodes * deep,
        scratch=[
            pltpu.VMEM(adjacency.shape, F32),
            pltpu.VMEM(features.shape, F32),
            pltpu.VMEM(weight_in.shape, F32),
            pltpu.VMEM(weight_out.shape, F32),
            pltpu.VMEM((1, nodes), jnp.int32),
            pltpu.VMEM((here, 3 * here, rows, rows), F32),
            pltpu.SemaphoreType.DMA((4 + here * slots,)),
        ],
        space=pltpu.HBM,
    )
    feat_i = mate(feat_out)
    (s_loc,) = call(
        add_features,
        [((nodes, deep), F32)],
        [halo_h, halo_l, s_loc, feat_e],
        flops=6 * nodes * nodes * deep,
    )
    wide_f, wide_h = ((nodes, hid), F32), ((nodes, hid), BF16)
    thin, thin_t, in_t = ((nodes, classes), F32), ((classes, nodes), F32), ((deep, nodes), BF16)
    (spread_in,) = call(
        spread, [((nodes, deep), F32)], [halo_h, halo_l, s_loc, feat_i], flops=6 * nodes * nodes * deep
    )
    spread_e = beside(spread_in)
    spread_i = mate(spread_in)
    in_oh, in_ol = call(turn, [in_t, in_t], [spread_in])

    def layer_of(high, low, rows_in, before, name, part):
        return call(
            functools.partial(forward, first=name == "forward_own", part=part),
            [thin, wide_f, wide_h, wide_h] + [in_t] * (0 if name == "forward_own" else 2),
            [high, low, rows_in, win_h, win_l, wout_hl, before],
            flops=16 * nodes * nodes * deep,
            name=name,
        )

    logits_o, slope_o, *kept_o = layer_of(loc_h, loc_l, spread_in, onehot, "forward_own", 0)
    logits_i, slope_i, *kept_i = layer_of(halo_h, halo_l, spread_i, logits_o, "forward_mate", 0)
    values, slope_e, *kept_e = layer_of(halo_h, halo_l, spread_e, logits_i, "forward_beside", 1)
    grads_t, loss = call(classify, [((2 * classes, nodes), BF16), ((8, LANES), F32)], [values, onehot])
    half = (deep * hid + hid * classes) // LANES // 2
    in_ts = [in_oh, in_ol, *kept_i[2:], *kept_e[2:]]
    *pre, total_out_t, ret_loc, out_e, give = call(
        backward,
        [wide_h] * 6 + [((classes, hid), F32), thin_t, thin_t, ((half + classes * (nodes // LANES), LANES), F32)],
        [grads_t, halo_h, halo_l, loc_h, loc_l, slope_o, slope_i, slope_e, *kept_o[:2], *kept_i[:2], *kept_e[:2],
         *in_ts, wout_hh, wout_ll, loss],
        flops=30 * nodes * nodes * deep,
    )
    got = mate(give)
    keep, logits = call(
        backward_kept,
        [((half, LANES), F32), thin],
        [*in_ts, *pre, total_out_t, loss, values],
        flops=10 * nodes * nodes * deep,
    )
    big, mid = groups((X, Y), (X, Z)), groups((Z,), (Y,))
    wide, narrow = len(big[0]), len(mid[0])
    shard = half // wide
    (mine,) = call(add_halves, [((half, LANES), F32)], [keep, got])
    received = exchange(mine.reshape(wide, shard, LANES), big)
    summed, out_e = call(sum_repeated, [((narrow, shard, LANES), F32), thin_t], [received, out_e])
    ret_e = beside(out_e)
    received = exchange(summed, mid)
    (summed,) = call(sum_repeated_after, [((wide, shard, LANES), F32)], [received, ret_e], anywhere=1)
    own = exchange(summed, big).reshape(half, LANES)
    other = mate(own)
    (hidden_grad,) = call(
        finish_hidden, [wide_f], [ret_loc, ret_e, got, wout_hh, wout_ll], flops=4 * nodes * nodes * deep
    )
    grad_in, grad_out, mean_loss = call(
        functools.partial(assemble, nodes * lax.axis_size(AXIS)),
        [((deep, hid), F32), ((hid, classes), F32), ((1, 1), F32)],
        [own, other],
        name="assemble",
    )
    return (logits, mean_loss.reshape(()), hidden_grad, grad_in, grad_out)


def solution(mesh):
    split = P(AXIS)
    return jax.shard_map(
        per_device,
        mesh=mesh,
        in_specs=(split, split, split, split, split, P(), P()),
        out_specs=(split, P(), split, P(), P()),
        check_vma=False,
    )
```

```python
import functools
import math

import jax
import jax.numpy as jnp
import numpy as np
from jax import lax
from jax.experimental import pallas as pl
from jax.experimental.pallas import tpu as pltpu
from jax.sharding import PartitionSpec as P

AXIS = "rows"
GRID = (4, 8, 8, 2)
X, Z, Y = range(3)
LANES = 128
F32 = jnp.float32
BF16 = jnp.bfloat16
VMEM_LIMIT = 24 * 1024 * 1024
CHUNK = 256
SQRT_HALF = 0.7071067811865476
INV_SQRT_2PI = 0.3989422804014327
HALF_ERFC = (
    0.0251311707,
    -0.0914511383,
    0.0845433265,
    -0.00280424249,
    0.0707159187,
    0.0842709431,
    0.103921354,
    0.112834799,
    0.112837931,
)


def mate(value):
    return lax.ppermute(value, AXIS, [(i, i ^ 1) for i in range(lax.axis_size(AXIS))])


def beside(value):
    pairs = [(i, i + 1) for i in range(1, lax.axis_size(AXIS) - 1, 2)]
    return lax.ppermute(value, AXIS, pairs + [(b, a) for a, b in pairs])


def groups(*per_core):
    ids = np.arange(math.prod(GRID)).reshape(GRID)
    found = []
    for core, axes in enumerate(per_core):
        rest = [axis for axis in range(3) if axis not in axes]
        size = math.prod(GRID[axis] for axis in axes)
        found += ids[..., core].transpose(rest + list(axes)).reshape(-1, size).tolist()
    return found


def exchange(value, members):
    return lax.all_to_all(value, AXIS, 0, 0, axis_index_groups=members, tiled=True)


def repeated(value, count):
    return jnp.broadcast_to(value[None], (count,) + value.shape)


def halves(value):
    high = value.astype(BF16)
    return high, (value - high.astype(F32)).astype(BF16)


def mm(a, b, dims=((1,), (0,))):
    return lax.dot_general(a, b, (dims, ((), ())), preferred_element_type=F32)


def fold(wide):
    half = wide.shape[1] // 2
    return wide[:, :half] + wide[:, half:]


def prepare(block_index, block_counts, adjacency, features, w_in, w_out, labels,
            loc_h, loc_l, halo_h, halo_l, s_loc, win_h, win_l, wout_hl, wout_hh, wout_ll, onehot, feat_out,
            slots_in, feat_in, win_in, wout_in, labels_in, band, sems):
    here, slots, rows, _ = adjacency.shape
    moves = [(features, feat_in), (w_in, win_in), (w_out, wout_in), (labels, labels_in)]
    moves += [(adjacency.at[b, k], slots_in.at[b, k]) for b in range(here) for k in range(slots)]
    moves = [pltpu.make_async_copy(source, target, sems.at[i]) for i, (source, target) in enumerate(moves)]
    for move in moves:
        move.start()
    me = lax.axis_index(AXIS)
    core = lax.rem(me, 2)
    first = me * here
    band[...] = jnp.zeros_like(band)
    for move in moves[:4]:
        move.wait()
    high, low = halves(win_in[...])
    win_h[...] = high
    win_l[...] = low
    high, low = halves(wout_in[...])
    classes = high.shape[1]
    for ref, left, right in ((wout_hl, high, low), (wout_hh, high, high), (wout_ll, low, low)):
        ref[:, :classes] = left
        ref[:, classes:] = right
    columns = lax.broadcasted_iota(jnp.int32, (classes, labels_in.shape[1]), 0)
    onehot[...] = jnp.where(columns == labels_in[...], 1.0, 0.0).T
    feat_out[...] = feat_in[...]
    feat_h, feat_l = halves(feat_in[...])
    for b in range(here):
        for k in range(slots):
            moves[4 + b * slots + k].wait()
            near = block_index[b, k] - first
            right = near >= here
            outside = jnp.where(right, near - here, near + here)
            outside += jnp.where(right == (core == 0), 0, 2 * here)
            place = jnp.where((near >= 0) & (near < here), here + near, outside)

            @pl.when(k < block_counts[b])
            def _():
                band[b, place] += slots_in[b, k]

        at = pl.ds(b * rows, rows)
        for s in range(3 * here):
            high, low = halves(band[b, s])
            if here <= s < 2 * here:
                cols = pl.ds((s - here) * rows, rows)
                loc_h[at, cols] = high
                loc_l[at, cols] = low
            else:
                cols = pl.ds((s if s < here else s - here) * rows, rows)
                halo_h[at, cols] = high
                halo_l[at, cols] = low
        s_loc[at, :] = mm(loc_h[at, :], feat_h) + mm(loc_h[at, :], feat_l) + mm(loc_l[at, :], feat_h)


def add_features(halo_h, halo_l, s_loc, feat_e, out):
    half = feat_e.shape[0]
    high, low = halves(feat_e[...])
    he, le = halo_h[:, half:], halo_l[:, half:]
    out[...] = s_loc[...] + mm(he, high) + mm(he, low) + mm(le, high)


def spread(halo_h, halo_l, s_loc, feat_i, spread_in):
    half = feat_i.shape[0]
    high, low = halves(feat_i[...])
    hi, li = halo_h[:, :half], halo_l[:, :half]
    spread_in[...] = s_loc[...] + mm(hi, high) + mm(hi, low) + mm(li, high)


def layer(spread_in, win_h, win_l):
    s_h, s_l = halves(spread_in)
    pre = mm(s_h, win_h[...]) + mm(s_h, win_l[...]) + mm(s_l, win_h[...])
    bell = jnp.exp(-0.5 * pre * pre)
    t = 1.0 / (1.0 + (0.4 * SQRT_HALF) * jnp.abs(pre))
    poly = jnp.full_like(t, HALF_ERFC[0])
    for term in HALF_ERFC[1:]:
        poly = poly * t + term
    tail = bell * (t * poly)
    gate = jnp.where(pre < 0, tail, 1.0 - tail)
    return pre * gate, gate + pre * (INV_SQRT_2PI * bell)


def forward(high_band, low_band, spread_in, win_h, win_l, wout_hl, logits_before,
            scores_sum, slope, hid_h, hid_l, *in_t, first, part):
    hidden, slope[...] = layer(spread_in[...], win_h, win_l)
    high, low = halves(hidden)
    hid_h[...] = high
    hid_l[...] = low
    pair = jnp.concatenate(halves(fold(mm(high, wout_hl[...]) + mm(low, wout_hl[...]))), axis=1)
    nodes = spread_in.shape[0]
    cols = slice(part * nodes, (part + 1) * nodes)
    logits = fold(mm(high_band[:, cols], pair) + mm(low_band[:, cols], pair))
    scores_sum[...] = logits if first else logits_before[...] + logits
    if in_t:
        turn(spread_in, *in_t)


def turn(spread_in, in_th, in_tl):
    high, low = halves(spread_in[...].T)
    in_th[...] = high
    in_tl[...] = low


def stacked(grads, high, low):
    tall = mm(grads, high) + mm(grads, low)
    half = tall.shape[0] // 2
    return tall[:half] + tall[half:]


def classify(values, onehot, grads_t, loss):
    scores = values[...]
    totals = jnp.log(jnp.sum(jnp.exp(scores), axis=1, keepdims=True))
    hot = onehot[...]
    grads_t[...] = jnp.concatenate(halves((jnp.exp(scores - totals) - hot).T), axis=0)
    row_loss = totals - jnp.sum(hot * scores, axis=1, keepdims=True)
    loss[...] = jnp.broadcast_to(jnp.sum(row_loss, axis=0, keepdims=True), loss.shape)


def gradient_half(which, parts, loss, out):
    deep, hid = parts[0][2][0].shape[0] // 2, parts[0][1][0].shape[1] // 2
    at = pl.ds(pl.multiple_of(which * deep, deep), deep)
    cols = pl.ds(pl.multiple_of(which * hid, hid), hid)
    grad_in = grad_out_t = 0.0
    for returned_t, (hid_h, hid_l), (in_th, in_tl), (pre_h, pre_l) in parts:
        high, low = in_th[at, :], in_tl[at, :]
        tall = mm(jnp.concatenate([high, low], axis=0), pre_h)
        grad_in = grad_in + (tall[:deep] + tall[deep:] + mm(high, pre_l))
        tall = jnp.concatenate(halves(returned_t), axis=0)
        grad_out_t = grad_out_t + stacked(tall, hid_h[:, cols], hid_l[:, cols])
    for t in range(grad_in.shape[1] // LANES):
        out[pl.ds(t * deep, deep), :] = grad_in[:, t * LANES : (t + 1) * LANES]
    grad_out = grad_out_t.T
    grad_out = jnp.where(last_element(grad_out) & (which == 1), loss[:1, :], grad_out)
    rows = deep * (grad_in.shape[1] // LANES)
    out[pl.ds(rows, hid), :] = grad_out
    return rows + hid


def last_element(value):
    row = lax.broadcasted_iota(jnp.int32, value.shape, 0)
    column = lax.broadcasted_iota(jnp.int32, value.shape, 1)
    return (row == value.shape[0] - 1) & (column == value.shape[1] - 1)


def backward(grads_t, halo_h, halo_l, loc_h, loc_l, slope_o, slope_i, slope_e, hid_oh, hid_ol, hid_ih, hid_il, hid_eh, hid_el,
             in_oh, in_ol, in_ih, in_il, in_eh, in_el, wout_hh, wout_ll, loss,
             pre_oh, pre_ol, pre_ih, pre_il, pre_eh, pre_el, ret_loc, out_i, out_e, give):
    grads = grads_t[...]
    half = loc_h.shape[1]
    own = stacked(grads, loc_h[...], loc_l[...])
    near = stacked(grads, halo_h[:, :half], halo_l[:, :half])
    far = stacked(grads, halo_h[:, half:], halo_l[:, half:])
    ret_loc[...] = own
    out_i[...] = near
    out_e[...] = far
    across = ((1,), (1,))
    parts = []
    for returned_t, slope, hidden, inputs, pre_h, pre_l in (
        (own, slope_o, (hid_oh, hid_ol), (in_oh, in_ol), pre_oh, pre_ol),
        (near, slope_i, (hid_ih, hid_il), (in_ih, in_il), pre_ih, pre_il),
        (far, slope_e, (hid_eh, hid_el), (in_eh, in_el), pre_eh, pre_el),
    ):
        both = jnp.concatenate(halves(returned_t.T), axis=1)
        hidden_grad = mm(both, wout_hh[...], across) + mm(both, wout_ll[...], across)
        high, low = halves(hidden_grad * slope[...])
        pre_h[...] = high
        pre_l[...] = low
        parts.append((returned_t, hidden, inputs, (high, low)))
    other = 1 - lax.rem(lax.axis_index(AXIS), 2)
    end = gradient_half(other, parts, loss, give)
    classes = near.shape[0]
    for t in range(half // LANES):
        give[pl.ds(end + t * classes, classes), :] = near[:, t * LANES : (t + 1) * LANES]


def backward_kept(hid_oh, hid_ol, hid_ih, hid_il, hid_eh, hid_el, in_oh, in_ol, in_ih, in_il, in_eh, in_el,
                  pre_oh, pre_ol, pre_ih, pre_il, pre_eh, pre_el, ret_loc, out_i, out_e, loss, values,
                  keep, logits):
    core = lax.rem(lax.axis_index(AXIS), 2)
    parts = (
        (ret_loc[...], (hid_oh, hid_ol), (in_oh, in_ol), (pre_oh[...], pre_ol[...])),
        (out_i[...], (hid_ih, hid_il), (in_ih, in_il), (pre_ih[...], pre_il[...])),
        (out_e[...], (hid_eh, hid_el), (in_eh, in_el), (pre_eh[...], pre_el[...])),
    )
    gradient_half(core, parts, loss, keep)
    logits[...] = values[...]


def finish_hidden(ret_loc, ret_e, got, wout_hh, wout_ll, hidden_grad):
    classes, nodes = ret_loc.shape
    start = got.shape[0] - classes * (nodes // LANES)
    ret_i = [got[pl.ds(start + t * classes, classes), :] for t in range(nodes // LANES)]
    returned_t = ret_loc[...] + ret_e[...] + jnp.concatenate(ret_i, axis=1)
    both = jnp.concatenate(halves(returned_t.T), axis=1)
    across = ((1,), (1,))
    hidden_grad[...] = mm(both, wout_hh[...], across) + mm(both, wout_ll[...], across)


def add_halves(keep, got, out):
    out[...] = keep[...] + got[: keep.shape[0], :]


def sum_repeated(received, *refs):
    out = refs[-1]
    total = received[0]
    for k in range(1, received.shape[0]):
        total = total + received[k]
    out[...] = jnp.broadcast_to(total[None], out.shape)


def assemble(nodes_total, own, other, grad_in, grad_out, mean_loss):
    deep = grad_in.shape[0] // 2
    hid = grad_out.shape[0] // 2
    tiles = grad_in.shape[1] // LANES
    core = lax.rem(lax.axis_index(AXIS), 2)
    for half, which in ((own, core), (other, 1 - core)):
        at = pl.ds(pl.multiple_of(which * deep, deep), deep)
        for t in range(tiles):
            grad_in[at, t * LANES : (t + 1) * LANES] = half[pl.ds(t * deep, deep), :]
        at = pl.ds(pl.multiple_of(which * hid, hid), hid)
        grad_out[at, :] = half[pl.ds(tiles * deep, hid), :]
    end = pl.ds(2 * hid - 8, 8)
    value = grad_out[end, :]
    there = last_element(value)
    mean_loss[0, 0] = jnp.sum(jnp.where(there, value, 0.0)) / nodes_total
    others = jnp.sum(jnp.where(there, 0.0, value), axis=1, keepdims=True)
    grad_out[end, :] = jnp.where(there, -others, value)


def call(body, outs, args, scalars=0, anywhere=0, flops=0, scratch=(), space=pltpu.VMEM, name=""):
    smem = pl.BlockSpec(memory_space=pltpu.SMEM)
    vmem = pl.BlockSpec(memory_space=pltpu.VMEM)
    moved = sum(a.size * a.dtype.itemsize for a in args)
    return pl.pallas_call(
        body,
        out_shape=[jax.ShapeDtypeStruct(shape, kind) for shape, kind in outs],
        in_specs=[smem] * scalars
        + [pl.BlockSpec(memory_space=space)] * (len(args) - scalars - anywhere)
        + [pl.BlockSpec(memory_space=pl.ANY)] * anywhere,
        out_specs=[smem if shape == (1, 1) else vmem for shape, _ in outs],
        scratch_shapes=scratch,
        cost_estimate=pl.CostEstimate(flops=flops, bytes_accessed=moved, transcendentals=0),
        compiler_params=pltpu.CompilerParams(vmem_limit_bytes=VMEM_LIMIT),
        name=name or body.__name__,
    )(*args)


def per_device(features, adjacency, block_index, block_counts, labels, weight_in, weight_out):
    here, slots, rows = adjacency.shape[:3]
    nodes = here * rows
    deep, hid = weight_in.shape
    classes = weight_out.shape[1]

    feat_e = beside(features)
    loc = ((nodes, nodes), BF16)
    halo = ((nodes, 2 * nodes), BF16)
    w_pair = ((hid, 2 * classes), BF16)
    loc_h, loc_l, halo_h, halo_l, s_loc, win_h, win_l, wout_hl, wout_hh, wout_ll, onehot, feat_out = call(
        prepare,
        [loc, loc, halo, halo, ((nodes, deep), F32), ((deep, hid), BF16), ((deep, hid), BF16),
         w_pair, w_pair, w_pair, ((nodes, classes), F32), ((nodes, deep), F32)],
        [pltpu.with_memory_space_constraint(v, pltpu.HBM)
         for v in (block_index, block_counts, adjacency, features, weight_in, weight_out, labels.reshape(1, nodes))],
        scalars=2,
        flops=6 * nodes * nodes * deep,
        scratch=[
            pltpu.VMEM(adjacency.shape, F32),
            pltpu.VMEM(features.shape, F32),
            pltpu.VMEM(weight_in.shape, F32),
            pltpu.VMEM(weight_out.shape, F32),
            pltpu.VMEM((1, nodes), jnp.int32),
            pltpu.VMEM((here, 3 * here, rows, rows), F32),
            pltpu.SemaphoreType.DMA((4 + here * slots,)),
        ],
        space=pltpu.HBM,
    )
    feat_i = mate(feat_out)
    (s_loc,) = call(
        add_features,
        [((nodes, deep), F32)],
        [halo_h, halo_l, s_loc, feat_e],
        flops=6 * nodes * nodes * deep,
    )
    wide_f, wide_h = ((nodes, hid), F32), ((nodes, hid), BF16)
    thin, thin_t, in_t = ((nodes, classes), F32), ((classes, nodes), F32), ((deep, nodes), BF16)
    (spread_in,) = call(
        spread, [((nodes, deep), F32)], [halo_h, halo_l, s_loc, feat_i], flops=6 * nodes * nodes * deep
    )
    spread_e = beside(spread_in)
    spread_i = mate(spread_in)
    in_oh, in_ol = call(turn, [in_t, in_t], [spread_in])

    def layer_of(high, low, rows_in, before, name, part):
        return call(
            functools.partial(forward, first=name == "forward_own", part=part),
            [thin, wide_f, wide_h, wide_h] + [in_t] * (0 if name == "forward_own" else 2),
            [high, low, rows_in, win_h, win_l, wout_hl, before],
            flops=16 * nodes * nodes * deep,
            name=name,
        )

    logits_o, slope_o, *kept_o = layer_of(loc_h, loc_l, spread_in, onehot, "forward_own", 0)
    logits_i, slope_i, *kept_i = layer_of(halo_h, halo_l, spread_i, logits_o, "forward_mate", 0)
    values, slope_e, *kept_e = layer_of(halo_h, halo_l, spread_e, logits_i, "forward_beside", 1)
    grads_t, loss = call(classify, [((2 * classes, nodes), BF16), ((8, LANES), F32)], [values, onehot])
    half = (deep * hid + hid * classes) // LANES // 2
    hids = [*kept_o[:2], *kept_i[:2], *kept_e[:2]]
    in_ts = [in_oh, in_ol, *kept_i[2:], *kept_e[2:]]
    *pre, ret_loc, out_i, out_e, give = call(
        backward,
        [wide_h] * 6 + [thin_t] * 3 + [((half + classes * (nodes // LANES), LANES), F32)],
        [grads_t, halo_h, halo_l, loc_h, loc_l, slope_o, slope_i, slope_e, *hids,
         *in_ts, wout_hh, wout_ll, loss],
        flops=30 * nodes * nodes * deep,
    )
    got = mate(give)
    keep, logits = call(
        backward_kept,
        [((half, LANES), F32), thin],
        [*hids, *in_ts, *pre, ret_loc, out_i, out_e, loss, values],
        flops=10 * nodes * nodes * deep,
    )
    big, mid = groups((X, Y), (X, Z)), groups((Z,), (Y,))
    wide, narrow = len(big[0]), len(mid[0])
    shard = half // wide
    (mine,) = call(add_halves, [((half, LANES), F32)], [keep, got])
    received = exchange(mine.reshape(wide, shard, LANES), big)
    ret_e = beside(out_e)
    (summed,) = call(sum_repeated, [((narrow, shard, LANES), F32)], [received, ret_e], anywhere=1)
    received = exchange(summed, mid)
    (summed,) = call(sum_repeated, [((wide, shard, LANES), F32)], [received])
    own = exchange(summed, big).reshape(half, LANES)
    other = mate(own)
    (hidden_grad,) = call(
        finish_hidden, [wide_f], [ret_loc, ret_e, got, wout_hh, wout_ll], flops=4 * nodes * nodes * deep
    )
    grad_in, grad_out, mean_loss = call(
        functools.partial(assemble, nodes * lax.axis_size(AXIS)),
        [((deep, hid), F32), ((hid, classes), F32), ((1, 1), F32)],
        [own, other],
        name="assemble",
    )
    return (logits, mean_loss.reshape(()), hidden_grad, grad_in, grad_out)


def solution(mesh):
    split = P(AXIS)
    return jax.shard_map(
        per_device,
        mesh=mesh,
        in_specs=(split, split, split, split, split, P(), P()),
        out_specs=(split, P(), split, P(), P()),
        check_vma=False,
    )
```

```python
import functools
import math

import jax
import jax.numpy as jnp
import numpy as np
from jax import lax
from jax.experimental import pallas as pl
from jax.experimental.pallas import tpu as pltpu
from jax.sharding import PartitionSpec as P

AXIS = "rows"
GRID = (4, 8, 8, 2)
X, Z, Y = range(3)
LANES = 128
F32 = jnp.float32
BF16 = jnp.bfloat16
VMEM_LIMIT = 24 * 1024 * 1024
CHUNK = 256
SQRT_HALF = 0.7071067811865476
INV_SQRT_2PI = 0.3989422804014327
HALF_ERFC = (
    0.0251311707,
    -0.0914511383,
    0.0845433265,
    -0.00280424249,
    0.0707159187,
    0.0842709431,
    0.103921354,
    0.112834799,
    0.112837931,
)


def mate(value):
    return lax.ppermute(value, AXIS, [(i, i ^ 1) for i in range(lax.axis_size(AXIS))])


def beside(value):
    pairs = [(i, i + 1) for i in range(1, lax.axis_size(AXIS) - 1, 2)]
    return lax.ppermute(value, AXIS, pairs + [(b, a) for a, b in pairs])


def groups(*per_core):
    ids = np.arange(math.prod(GRID)).reshape(GRID)
    found = []
    for core, axes in enumerate(per_core):
        rest = [axis for axis in range(3) if axis not in axes]
        size = math.prod(GRID[axis] for axis in axes)
        found += ids[..., core].transpose(rest + list(axes)).reshape(-1, size).tolist()
    return found


def exchange(value, members):
    return lax.all_to_all(value, AXIS, 0, 0, axis_index_groups=members, tiled=True)


def repeated(value, count):
    return jnp.broadcast_to(value[None], (count,) + value.shape)


def halves(value):
    high = value.astype(BF16)
    return high, (value - high.astype(F32)).astype(BF16)


def mm(a, b, dims=((1,), (0,))):
    return lax.dot_general(a, b, (dims, ((), ())), preferred_element_type=F32)


def fold(wide):
    half = wide.shape[1] // 2
    return wide[:, :half] + wide[:, half:]


def prepare(block_index, block_counts, adjacency, features, w_in, w_out, labels,
            loc_h, loc_l, halo_h, halo_l, s_loc, win_h, win_l, wout_hl, wout_hh, wout_ll, onehot, feat_out,
            slots_in, feat_in, win_in, wout_in, labels_in, band, sems):
    here, slots, rows, _ = adjacency.shape
    moves = [(features, feat_in), (w_in, win_in), (w_out, wout_in), (labels, labels_in)]
    moves += [(adjacency.at[b, k], slots_in.at[b, k]) for b in range(here) for k in range(slots)]
    moves = [pltpu.make_async_copy(source, target, sems.at[i]) for i, (source, target) in enumerate(moves)]
    for move in moves:
        move.start()
    me = lax.axis_index(AXIS)
    core = lax.rem(me, 2)
    first = me * here
    band[...] = jnp.zeros_like(band)
    for move in moves[:4]:
        move.wait()
    high, low = halves(win_in[...])
    win_h[...] = high
    win_l[...] = low
    high, low = halves(wout_in[...])
    classes = high.shape[1]
    for ref, left, right in ((wout_hl, high, low), (wout_hh, high, high), (wout_ll, low, low)):
        ref[:, :classes] = left
        ref[:, classes:] = right
    columns = lax.broadcasted_iota(jnp.int32, (classes, labels_in.shape[1]), 0)
    onehot[...] = jnp.where(columns == labels_in[...], 1.0, 0.0).T
    feat_out[...] = feat_in[...]
    feat_h, feat_l = halves(feat_in[...])
    for b in range(here):
        for k in range(slots):
            moves[4 + b * slots + k].wait()
            near = block_index[b, k] - first
            right = near >= here
            outside = jnp.where(right, near - here, near + here)
            outside += jnp.where(right == (core == 0), 0, 2 * here)
            place = jnp.where((near >= 0) & (near < here), here + near, outside)

            @pl.when(k < block_counts[b])
            def _():
                band[b, place] += slots_in[b, k]

        at = pl.ds(b * rows, rows)
        for s in range(3 * here):
            high, low = halves(band[b, s])
            if here <= s < 2 * here:
                cols = pl.ds((s - here) * rows, rows)
                loc_h[at, cols] = high
                loc_l[at, cols] = low
            else:
                cols = pl.ds((s if s < here else s - here) * rows, rows)
                halo_h[at, cols] = high
                halo_l[at, cols] = low
        s_loc[at, :] = mm(loc_h[at, :], feat_h) + mm(loc_h[at, :], feat_l) + mm(loc_l[at, :], feat_h)


def add_features(halo_h, halo_l, s_loc, feat_e, out):
    half = feat_e.shape[0]
    high, low = halves(feat_e[...])
    he, le = halo_h[:, half:], halo_l[:, half:]
    out[...] = s_loc[...] + mm(he, high) + mm(he, low) + mm(le, high)


def spread(halo_h, halo_l, s_loc, feat_i, spread_in):
    half = feat_i.shape[0]
    high, low = halves(feat_i[...])
    hi, li = halo_h[:, :half], halo_l[:, :half]
    spread_in[...] = s_loc[...] + mm(hi, high) + mm(hi, low) + mm(li, high)


def layer(spread_in, win_h, win_l):
    s_h, s_l = halves(spread_in)
    pre = mm(s_h, win_h[...]) + mm(s_h, win_l[...]) + mm(s_l, win_h[...])
    bell = jnp.exp(-0.5 * pre * pre)
    t = 1.0 / (1.0 + (0.4 * SQRT_HALF) * jnp.abs(pre))
    poly = jnp.full_like(t, HALF_ERFC[0])
    for term in HALF_ERFC[1:]:
        poly = poly * t + term
    tail = bell * (t * poly)
    gate = jnp.where(pre < 0, tail, 1.0 - tail)
    return pre * gate, gate + pre * (INV_SQRT_2PI * bell)


def forward(high_band, low_band, spread_in, win_h, win_l, wout_hl, logits_before,
            scores_sum, slope, hid_h, hid_l, *in_t, first, part):
    hidden, slope[...] = layer(spread_in[...], win_h, win_l)
    high, low = halves(hidden)
    hid_h[...] = high
    hid_l[...] = low
    pair = jnp.concatenate(halves(fold(mm(high, wout_hl[...]) + mm(low, wout_hl[...]))), axis=1)
    nodes = spread_in.shape[0]
    cols = slice(part * nodes, (part + 1) * nodes)
    logits = fold(mm(high_band[:, cols], pair) + mm(low_band[:, cols], pair))
    scores_sum[...] = logits if first else logits_before[...] + logits
    if in_t:
        turn(spread_in, *in_t)


def turn(spread_in, in_th, in_tl):
    high, low = halves(spread_in[...].T)
    in_th[...] = high
    in_tl[...] = low


def stacked(grads, high, low):
    tall = mm(grads, high) + mm(grads, low)
    half = tall.shape[0] // 2
    return tall[:half] + tall[half:]


def classify(values, onehot, grads_t, loss):
    scores = values[...]
    totals = jnp.log(jnp.sum(jnp.exp(scores), axis=1, keepdims=True))
    hot = onehot[...]
    grads_t[...] = jnp.concatenate(halves((jnp.exp(scores - totals) - hot).T), axis=0)
    row_loss = totals - jnp.sum(hot * scores, axis=1, keepdims=True)
    loss[...] = jnp.broadcast_to(jnp.sum(row_loss, axis=0, keepdims=True), loss.shape)


def gradient_half(which, parts, loss, out):
    deep, hid = parts[0][2][0].shape[0] // 2, parts[0][1][0].shape[1] // 2
    at = pl.ds(pl.multiple_of(which * deep, deep), deep)
    cols = pl.ds(pl.multiple_of(which * hid, hid), hid)
    grad_in = grad_out_t = 0.0
    for returned_t, (hid_h, hid_l), (in_th, in_tl), (pre_h, pre_l) in parts:
        high, low = in_th[at, :], in_tl[at, :]
        tall = mm(jnp.concatenate([high, low], axis=0), pre_h)
        grad_in = grad_in + (tall[:deep] + tall[deep:] + mm(high, pre_l))
        tall = jnp.concatenate(halves(returned_t), axis=0)
        grad_out_t = grad_out_t + stacked(tall, hid_h[:, cols], hid_l[:, cols])
    for t in range(grad_in.shape[1] // LANES):
        out[pl.ds(t * deep, deep), :] = grad_in[:, t * LANES : (t + 1) * LANES]
    grad_out = grad_out_t.T
    grad_out = jnp.where(last_element(grad_out) & (which == 1), loss[:1, :], grad_out)
    rows = deep * (grad_in.shape[1] // LANES)
    out[pl.ds(rows, hid), :] = grad_out
    return rows + hid


def last_element(value):
    row = lax.broadcasted_iota(jnp.int32, value.shape, 0)
    column = lax.broadcasted_iota(jnp.int32, value.shape, 1)
    return (row == value.shape[0] - 1) & (column == value.shape[1] - 1)


def backward(grads_t, halo_h, halo_l, loc_h, loc_l, slope_o, slope_i, slope_e, hid_oh, hid_ol, hid_ih, hid_il, hid_eh, hid_el,
             in_oh, in_ol, in_ih, in_il, in_eh, in_el, wout_hh, wout_ll, loss,
             pre_oh, pre_ol, pre_ih, pre_il, pre_eh, pre_el, ret_loc, out_i, out_e, give):
    grads = grads_t[...]
    half = loc_h.shape[1]
    own = stacked(grads, loc_h[...], loc_l[...])
    near = stacked(grads, halo_h[:, :half], halo_l[:, :half])
    far = stacked(grads, halo_h[:, half:], halo_l[:, half:])
    ret_loc[...] = own
    out_i[...] = near
    out_e[...] = far
    across = ((1,), (1,))
    parts = []
    for returned_t, slope, hidden, inputs, pre_h, pre_l in (
        (own, slope_o, (hid_oh, hid_ol), (in_oh, in_ol), pre_oh, pre_ol),
        (near, slope_i, (hid_ih, hid_il), (in_ih, in_il), pre_ih, pre_il),
        (far, slope_e, (hid_eh, hid_el), (in_eh, in_el), pre_eh, pre_el),
    ):
        both = jnp.concatenate(halves(returned_t.T), axis=1)
        hidden_grad = mm(both, wout_hh[...], across) + mm(both, wout_ll[...], across)
        high, low = halves(hidden_grad * slope[...])
        pre_h[...] = high
        pre_l[...] = low
        parts.append((returned_t, hidden, inputs, (high, low)))
    other = 1 - lax.rem(lax.axis_index(AXIS), 2)
    end = gradient_half(other, parts, loss, give)
    classes = near.shape[0]
    for t in range(half // LANES):
        give[pl.ds(end + t * classes, classes), :] = near[:, t * LANES : (t + 1) * LANES]


def backward_kept(hid_oh, hid_ol, hid_ih, hid_il, hid_eh, hid_el, in_oh, in_ol, in_ih, in_il, in_eh, in_el,
                  pre_oh, pre_ol, pre_ih, pre_il, pre_eh, pre_el, ret_loc, out_i, out_e, loss, values,
                  keep, logits):
    core = lax.rem(lax.axis_index(AXIS), 2)
    parts = (
        (ret_loc[...], (hid_oh, hid_ol), (in_oh, in_ol), (pre_oh[...], pre_ol[...])),
        (out_i[...], (hid_ih, hid_il), (in_ih, in_il), (pre_ih[...], pre_il[...])),
        (out_e[...], (hid_eh, hid_el), (in_eh, in_el), (pre_eh[...], pre_el[...])),
    )
    gradient_half(core, parts, loss, keep)
    logits[...] = values[...]


def finish_hidden(ret_loc, ret_e, got, wout_hh, wout_ll, hidden_grad):
    classes, nodes = ret_loc.shape
    start = got.shape[0] - classes * (nodes // LANES)
    ret_i = [got[pl.ds(start + t * classes, classes), :] for t in range(nodes // LANES)]
    returned_t = ret_loc[...] + ret_e[...] + jnp.concatenate(ret_i, axis=1)
    both = jnp.concatenate(halves(returned_t.T), axis=1)
    across = ((1,), (1,))
    hidden_grad[...] = mm(both, wout_hh[...], across) + mm(both, wout_ll[...], across)


def sum_repeated(received, *refs):
    out = refs[-1]
    total = received[0]
    for k in range(1, received.shape[0]):
        total = total + received[k]
    out[...] = jnp.broadcast_to(total[None], out.shape)


def assemble(nodes_total, own, other, grad_in, grad_out, mean_loss):
    deep = grad_in.shape[0] // 2
    hid = grad_out.shape[0] // 2
    tiles = grad_in.shape[1] // LANES
    core = lax.rem(lax.axis_index(AXIS), 2)
    for half, which in ((own, core), (other, 1 - core)):
        at = pl.ds(pl.multiple_of(which * deep, deep), deep)
        for t in range(tiles):
            grad_in[at, t * LANES : (t + 1) * LANES] = half[pl.ds(t * deep, deep), :]
        at = pl.ds(pl.multiple_of(which * hid, hid), hid)
        grad_out[at, :] = half[pl.ds(tiles * deep, hid), :]
    end = pl.ds(2 * hid - 8, 8)
    value = grad_out[end, :]
    there = last_element(value)
    mean_loss[0, 0] = jnp.sum(jnp.where(there, value, 0.0)) / nodes_total
    others = jnp.sum(jnp.where(there, 0.0, value), axis=1, keepdims=True)
    grad_out[end, :] = jnp.where(there, -others, value)


def call(body, outs, args, scalars=0, anywhere=0, flops=0, scratch=(), space=pltpu.VMEM, name=""):
    smem = pl.BlockSpec(memory_space=pltpu.SMEM)
    vmem = pl.BlockSpec(memory_space=pltpu.VMEM)
    moved = sum(a.size * a.dtype.itemsize for a in args)
    return pl.pallas_call(
        body,
        out_shape=[jax.ShapeDtypeStruct(shape, kind) for shape, kind in outs],
        in_specs=[smem] * scalars
        + [pl.BlockSpec(memory_space=space)] * (len(args) - scalars - anywhere)
        + [pl.BlockSpec(memory_space=pl.ANY)] * anywhere,
        out_specs=[smem if shape == (1, 1) else vmem for shape, _ in outs],
        scratch_shapes=scratch,
        cost_estimate=pl.CostEstimate(flops=flops, bytes_accessed=moved, transcendentals=0),
        compiler_params=pltpu.CompilerParams(vmem_limit_bytes=VMEM_LIMIT),
        name=name or body.__name__,
    )(*args)


def per_device(features, adjacency, block_index, block_counts, labels, weight_in, weight_out):
    here, slots, rows = adjacency.shape[:3]
    nodes = here * rows
    deep, hid = weight_in.shape
    classes = weight_out.shape[1]

    feat_e = beside(features)
    loc = ((nodes, nodes), BF16)
    halo = ((nodes, 2 * nodes), BF16)
    w_pair = ((hid, 2 * classes), BF16)
    loc_h, loc_l, halo_h, halo_l, s_loc, win_h, win_l, wout_hl, wout_hh, wout_ll, onehot, feat_out = call(
        prepare,
        [loc, loc, halo, halo, ((nodes, deep), F32), ((deep, hid), BF16), ((deep, hid), BF16),
         w_pair, w_pair, w_pair, ((nodes, classes), F32), ((nodes, deep), F32)],
        [pltpu.with_memory_space_constraint(v, pltpu.HBM)
         for v in (block_index, block_counts, adjacency, features, weight_in, weight_out, labels.reshape(1, nodes))],
        scalars=2,
        flops=6 * nodes * nodes * deep,
        scratch=[
            pltpu.VMEM(adjacency.shape, F32),
            pltpu.VMEM(features.shape, F32),
            pltpu.VMEM(weight_in.shape, F32),
            pltpu.VMEM(weight_out.shape, F32),
            pltpu.VMEM((1, nodes), jnp.int32),
            pltpu.VMEM((here, 3 * here, rows, rows), F32),
            pltpu.SemaphoreType.DMA((4 + here * slots,)),
        ],
        space=pltpu.HBM,
    )
    feat_i = mate(feat_out)
    (s_loc,) = call(
        add_features,
        [((nodes, deep), F32)],
        [halo_h, halo_l, s_loc, feat_e],
        flops=6 * nodes * nodes * deep,
    )
    wide_f, wide_h = ((nodes, hid), F32), ((nodes, hid), BF16)
    thin, thin_t, in_t = ((nodes, classes), F32), ((classes, nodes), F32), ((deep, nodes), BF16)
    (spread_in,) = call(
        spread, [((nodes, deep), F32)], [halo_h, halo_l, s_loc, feat_i], flops=6 * nodes * nodes * deep
    )
    spread_e = beside(spread_in)
    spread_i = mate(spread_in)
    in_oh, in_ol = call(turn, [in_t, in_t], [spread_in])

    def layer_of(high, low, rows_in, before, name, part):
        return call(
            functools.partial(forward, first=name == "forward_own", part=part),
            [thin, wide_f, wide_h, wide_h] + [in_t] * (0 if name == "forward_own" else 2),
            [high, low, rows_in, win_h, win_l, wout_hl, before],
            flops=16 * nodes * nodes * deep,
            name=name,
        )

    logits_o, slope_o, *kept_o = layer_of(loc_h, loc_l, spread_in, onehot, "forward_own", 0)
    logits_i, slope_i, *kept_i = layer_of(halo_h, halo_l, spread_i, logits_o, "forward_mate", 0)
    values, slope_e, *kept_e = layer_of(halo_h, halo_l, spread_e, logits_i, "forward_beside", 1)
    grads_t, loss = call(classify, [((2 * classes, nodes), BF16), ((8, LANES), F32)], [values, onehot])
    half = (deep * hid + hid * classes) // LANES // 2
    hids = [*kept_o[:2], *kept_i[:2], *kept_e[:2]]
    in_ts = [in_oh, in_ol, *kept_i[2:], *kept_e[2:]]
    *pre, ret_loc, out_i, out_e, give = call(
        backward,
        [wide_h] * 6 + [thin_t] * 3 + [((half + classes * (nodes // LANES), LANES), F32)],
        [grads_t, halo_h, halo_l, loc_h, loc_l, slope_o, slope_i, slope_e, *hids,
         *in_ts, wout_hh, wout_ll, loss],
        flops=30 * nodes * nodes * deep,
    )
    got = mate(give)
    keep, logits = call(
        backward_kept,
        [((half, LANES), F32), thin],
        [*hids, *in_ts, *pre, ret_loc, out_i, out_e, loss, values],
        flops=10 * nodes * nodes * deep,
    )
    big, mid = groups((X, Y), (X, Z)), groups((Z,), (Y,))
    wide, narrow = len(big[0]), len(mid[0])
    shard = half // wide
    received = exchange((keep + got[:half]).reshape(wide, shard, LANES), big)
    ret_e = beside(out_e)
    (summed,) = call(sum_repeated, [((narrow, shard, LANES), F32)], [received])
    received = exchange(summed, mid)
    (summed,) = call(sum_repeated, [((wide, shard, LANES), F32)], [received, ret_e], anywhere=1)
    own = exchange(summed, big).reshape(half, LANES)
    other = mate(own)
    (hidden_grad,) = call(
        finish_hidden, [wide_f], [ret_loc, ret_e, got, wout_hh, wout_ll], flops=4 * nodes * nodes * deep
    )
    grad_in, grad_out, mean_loss = call(
        functools.partial(assemble, nodes * lax.axis_size(AXIS)),
        [((deep, hid), F32), ((hid, classes), F32), ((1, 1), F32)],
        [own, other],
        name="assemble",
    )
    return (logits, mean_loss.reshape(()), hidden_grad, grad_in, grad_out)


def solution(mesh):
    split = P(AXIS)
    return jax.shard_map(
        per_device,
        mesh=mesh,
        in_specs=(split, split, split, split, split, P(), P()),
        out_specs=(split, P(), split, P(), P()),
        check_vma=False,
    )
```

```python
import functools
import math

import jax
import jax.numpy as jnp
import numpy as np
from jax import lax
from jax.experimental import pallas as pl
from jax.experimental.pallas import tpu as pltpu
from jax.sharding import PartitionSpec as P

AXIS = "rows"
GRID = (4, 8, 8, 2)
X, Z, Y = range(3)
LANES = 128
F32 = jnp.float32
BF16 = jnp.bfloat16
VMEM_LIMIT = 24 * 1024 * 1024
CHUNK = 256
SQRT_HALF = 0.7071067811865476
INV_SQRT_2PI = 0.3989422804014327
HALF_ERFC = (
    0.0251311707,
    -0.0914511383,
    0.0845433265,
    -0.00280424249,
    0.0707159187,
    0.0842709431,
    0.103921354,
    0.112834799,
    0.112837931,
)


def mate(value):
    return lax.ppermute(value, AXIS, [(i, i ^ 1) for i in range(lax.axis_size(AXIS))])


def beside(value):
    pairs = [(i, i + 1) for i in range(1, lax.axis_size(AXIS) - 1, 2)]
    return lax.ppermute(value, AXIS, pairs + [(b, a) for a, b in pairs])


def groups(*per_core):
    ids = np.arange(math.prod(GRID)).reshape(GRID)
    found = []
    for core, axes in enumerate(per_core):
        rest = [axis for axis in range(3) if axis not in axes]
        size = math.prod(GRID[axis] for axis in axes)
        found += ids[..., core].transpose(rest + list(axes)).reshape(-1, size).tolist()
    return found


def exchange(value, members):
    return lax.all_to_all(value, AXIS, 0, 0, axis_index_groups=members, tiled=True)


def repeated(value, count):
    return jnp.broadcast_to(value[None], (count,) + value.shape)


def halves(value):
    high = value.astype(BF16)
    return high, (value - high.astype(F32)).astype(BF16)


def mm(a, b, dims=((1,), (0,))):
    return lax.dot_general(a, b, (dims, ((), ())), preferred_element_type=F32)


def fold(wide):
    half = wide.shape[1] // 2
    return wide[:, :half] + wide[:, half:]


def prepare(block_index, block_counts, adjacency, features, w_in, w_out, labels,
            loc_h, loc_l, halo_h, halo_l, s_loc, win_h, win_l, wout_hl, wout_hh, wout_ll, onehot, feat_out,
            slots_in, feat_in, win_in, wout_in, labels_in, band, sems):
    here, slots, rows, _ = adjacency.shape
    moves = [(features, feat_in), (w_in, win_in), (w_out, wout_in), (labels, labels_in)]
    moves += [(adjacency.at[b, k], slots_in.at[b, k]) for b in range(here) for k in range(slots)]
    moves = [pltpu.make_async_copy(source, target, sems.at[i]) for i, (source, target) in enumerate(moves)]
    for move in moves:
        move.start()
    me = lax.axis_index(AXIS)
    core = lax.rem(me, 2)
    first = me * here
    band[...] = jnp.zeros_like(band)
    for move in moves[:4]:
        move.wait()
    high, low = halves(win_in[...])
    win_h[...] = high
    win_l[...] = low
    high, low = halves(wout_in[...])
    classes = high.shape[1]
    for ref, left, right in ((wout_hl, high, low), (wout_hh, high, high), (wout_ll, low, low)):
        ref[:, :classes] = left
        ref[:, classes:] = right
    columns = lax.broadcasted_iota(jnp.int32, (classes, labels_in.shape[1]), 0)
    onehot[...] = jnp.where(columns == labels_in[...], 1.0, 0.0).T
    feat_out[...] = feat_in[...]
    feat_h, feat_l = halves(feat_in[...])
    for b in range(here):
        for k in range(slots):
            moves[4 + b * slots + k].wait()
            near = block_index[b, k] - first
            right = near >= here
            outside = jnp.where(right, near - here, near + here)
            outside += jnp.where(right == (core == 0), 0, 2 * here)
            place = jnp.where((near >= 0) & (near < here), here + near, outside)

            @pl.when(k < block_counts[b])
            def _():
                band[b, place] += slots_in[b, k]

        at = pl.ds(b * rows, rows)
        for s in range(3 * here):
            high, low = halves(band[b, s])
            if here <= s < 2 * here:
                cols = pl.ds((s - here) * rows, rows)
                loc_h[at, cols] = high
                loc_l[at, cols] = low
            else:
                cols = pl.ds((s if s < here else s - here) * rows, rows)
                halo_h[at, cols] = high
                halo_l[at, cols] = low
        s_loc[at, :] = mm(loc_h[at, :], feat_h) + mm(loc_h[at, :], feat_l) + mm(loc_l[at, :], feat_h)


def add_features(halo_h, halo_l, s_loc, feat_e, out):
    half = feat_e.shape[0]
    high, low = halves(feat_e[...])
    he, le = halo_h[:, half:], halo_l[:, half:]
    out[...] = s_loc[...] + mm(he, high) + mm(he, low) + mm(le, high)


def spread(halo_h, halo_l, s_loc, feat_i, spread_in):
    half = feat_i.shape[0]
    high, low = halves(feat_i[...])
    hi, li = halo_h[:, :half], halo_l[:, :half]
    spread_in[...] = s_loc[...] + mm(hi, high) + mm(hi, low) + mm(li, high)


def layer(spread_in, win_h, win_l):
    s_h, s_l = halves(spread_in)
    pre = mm(s_h, win_h[...]) + mm(s_h, win_l[...]) + mm(s_l, win_h[...])
    bell = jnp.exp(-0.5 * pre * pre)
    t = 1.0 / (1.0 + (0.4 * SQRT_HALF) * jnp.abs(pre))
    poly = jnp.full_like(t, HALF_ERFC[0])
    for term in HALF_ERFC[1:]:
        poly = poly * t + term
    tail = bell * (t * poly)
    gate = jnp.where(pre < 0, tail, 1.0 - tail)
    return pre * gate, gate + pre * (INV_SQRT_2PI * bell)


def forward(high_band, low_band, spread_in, win_h, win_l, wout_hl, logits_before,
            scores_sum, slope, hid_h, hid_l, *in_t, first, part):
    hidden, slope[...] = layer(spread_in[...], win_h, win_l)
    high, low = halves(hidden)
    hid_h[...] = high
    hid_l[...] = low
    pair = jnp.concatenate(halves(fold(mm(high, wout_hl[...]) + mm(low, wout_hl[...]))), axis=1)
    nodes = spread_in.shape[0]
    cols = slice(part * nodes, (part + 1) * nodes)
    logits = fold(mm(high_band[:, cols], pair) + mm(low_band[:, cols], pair))
    scores_sum[...] = logits if first else logits_before[...] + logits
    if in_t:
        turn(spread_in, *in_t)


def turn(spread_in, in_th, in_tl):
    high, low = halves(spread_in[...].T)
    in_th[...] = high
    in_tl[...] = low


def stacked(grads, high, low):
    tall = mm(grads, high) + mm(grads, low)
    half = tall.shape[0] // 2
    return tall[:half] + tall[half:]


def classify(values, onehot, grads_t, loss):
    scores = values[...]
    totals = jnp.log(jnp.sum(jnp.exp(scores), axis=1, keepdims=True))
    hot = onehot[...]
    grads_t[...] = jnp.concatenate(halves((jnp.exp(scores - totals) - hot).T), axis=0)
    row_loss = totals - jnp.sum(hot * scores, axis=1, keepdims=True)
    loss[...] = jnp.broadcast_to(jnp.sum(row_loss, axis=0, keepdims=True), loss.shape)


def gradient_half(which, parts, loss, out):
    deep, hid = parts[0][2][0].shape[0] // 2, parts[0][1][0].shape[1] // 2
    at = pl.ds(pl.multiple_of(which * deep, deep), deep)
    cols = pl.ds(pl.multiple_of(which * hid, hid), hid)
    grad_in = grad_out_t = 0.0
    for returned_t, (hid_h, hid_l), (in_th, in_tl), (pre_h, pre_l) in parts:
        high, low = in_th[at, :], in_tl[at, :]
        tall = mm(jnp.concatenate([high, low], axis=0), pre_h)
        grad_in = grad_in + (tall[:deep] + tall[deep:] + mm(high, pre_l))
        tall = jnp.concatenate(halves(returned_t), axis=0)
        grad_out_t = grad_out_t + stacked(tall, hid_h[:, cols], hid_l[:, cols])
    for t in range(grad_in.shape[1] // LANES):
        out[pl.ds(t * deep, deep), :] = grad_in[:, t * LANES : (t + 1) * LANES]
    grad_out = grad_out_t.T
    grad_out = jnp.where(last_element(grad_out) & (which == 1), loss[:1, :], grad_out)
    rows = deep * (grad_in.shape[1] // LANES)
    out[pl.ds(rows, hid), :] = grad_out
    return rows + hid


def last_element(value):
    row = lax.broadcasted_iota(jnp.int32, value.shape, 0)
    column = lax.broadcasted_iota(jnp.int32, value.shape, 1)
    return (row == value.shape[0] - 1) & (column == value.shape[1] - 1)


def backward(grads_t, halo_h, halo_l, loc_h, loc_l, slope_o, slope_i, slope_e, hid_oh, hid_ol, hid_ih, hid_il, hid_eh, hid_el,
             in_oh, in_ol, in_ih, in_il, in_eh, in_el, wout_hh, wout_ll, loss,
             pre_oh, pre_ol, pre_ih, pre_il, pre_eh, pre_el, ret_loc, out_i, out_e, give):
    grads = grads_t[...]
    half = loc_h.shape[1]
    own = stacked(grads, loc_h[...], loc_l[...])
    near = stacked(grads, halo_h[:, :half], halo_l[:, :half])
    far = stacked(grads, halo_h[:, half:], halo_l[:, half:])
    ret_loc[...] = own
    out_i[...] = near
    out_e[...] = far
    across = ((1,), (1,))
    parts = []
    for returned_t, slope, hidden, inputs, pre_h, pre_l in (
        (own, slope_o, (hid_oh, hid_ol), (in_oh, in_ol), pre_oh, pre_ol),
        (near, slope_i, (hid_ih, hid_il), (in_ih, in_il), pre_ih, pre_il),
        (far, slope_e, (hid_eh, hid_el), (in_eh, in_el), pre_eh, pre_el),
    ):
        both = jnp.concatenate(halves(returned_t.T), axis=1)
        hidden_grad = mm(both, wout_hh[...], across) + mm(both, wout_ll[...], across)
        high, low = halves(hidden_grad * slope[...])
        pre_h[...] = high
        pre_l[...] = low
        parts.append((returned_t, hidden, inputs, (high, low)))
    other = 1 - lax.rem(lax.axis_index(AXIS), 2)
    end = gradient_half(other, parts, loss, give)
    classes = near.shape[0]
    for t in range(half // LANES):
        give[pl.ds(end + t * classes, classes), :] = near[:, t * LANES : (t + 1) * LANES]


def backward_kept(hid_oh, hid_ol, hid_ih, hid_il, hid_eh, hid_el, in_oh, in_ol, in_ih, in_il, in_eh, in_el,
                  pre_oh, pre_ol, pre_ih, pre_il, pre_eh, pre_el, ret_loc, out_i, out_e, loss, values,
                  keep, logits):
    core = lax.rem(lax.axis_index(AXIS), 2)
    parts = (
        (ret_loc[...], (hid_oh, hid_ol), (in_oh, in_ol), (pre_oh[...], pre_ol[...])),
        (out_i[...], (hid_ih, hid_il), (in_ih, in_il), (pre_ih[...], pre_il[...])),
        (out_e[...], (hid_eh, hid_el), (in_eh, in_el), (pre_eh[...], pre_el[...])),
    )
    gradient_half(core, parts, loss, keep)
    logits[...] = values[...]


def finish_hidden(ret_loc, ret_e, got, wout_hh, wout_ll, hidden_grad):
    classes, nodes = ret_loc.shape
    start = got.shape[0] - classes * (nodes // LANES)
    ret_i = [got[pl.ds(start + t * classes, classes), :] for t in range(nodes // LANES)]
    returned_t = ret_loc[...] + ret_e[...] + jnp.concatenate(ret_i, axis=1)
    both = jnp.concatenate(halves(returned_t.T), axis=1)
    across = ((1,), (1,))
    hidden_grad[...] = mm(both, wout_hh[...], across) + mm(both, wout_ll[...], across)


def sum_repeated(received, *refs):
    out = refs[-1]
    total = received[0]
    for k in range(1, received.shape[0]):
        total = total + received[k]
    out[...] = jnp.broadcast_to(total[None], out.shape)


def assemble(nodes_total, own, other, grad_in, grad_out, mean_loss):
    deep = grad_in.shape[0] // 2
    hid = grad_out.shape[0] // 2
    tiles = grad_in.shape[1] // LANES
    core = lax.rem(lax.axis_index(AXIS), 2)
    for half, which in ((own, core), (other, 1 - core)):
        at = pl.ds(pl.multiple_of(which * deep, deep), deep)
        for t in range(tiles):
            grad_in[at, t * LANES : (t + 1) * LANES] = half[pl.ds(t * deep, deep), :]
        at = pl.ds(pl.multiple_of(which * hid, hid), hid)
        grad_out[at, :] = half[pl.ds(tiles * deep, hid), :]
    end = pl.ds(2 * hid - 8, 8)
    value = grad_out[end, :]
    there = last_element(value)
    mean_loss[0, 0] = jnp.sum(jnp.where(there, value, 0.0)) / nodes_total
    others = jnp.sum(jnp.where(there, 0.0, value), axis=1, keepdims=True)
    grad_out[end, :] = jnp.where(there, -others, value)


def call(body, outs, args, scalars=0, anywhere=0, flops=0, scratch=(), space=pltpu.VMEM, name=""):
    smem = pl.BlockSpec(memory_space=pltpu.SMEM)
    vmem = pl.BlockSpec(memory_space=pltpu.VMEM)
    moved = sum(a.size * a.dtype.itemsize for a in args)
    return pl.pallas_call(
        body,
        out_shape=[jax.ShapeDtypeStruct(shape, kind) for shape, kind in outs],
        in_specs=[smem] * scalars
        + [pl.BlockSpec(memory_space=space)] * (len(args) - scalars - anywhere)
        + [pl.BlockSpec(memory_space=pl.ANY)] * anywhere,
        out_specs=[smem if shape == (1, 1) else vmem for shape, _ in outs],
        scratch_shapes=scratch,
        cost_estimate=pl.CostEstimate(flops=flops, bytes_accessed=moved, transcendentals=0),
        compiler_params=pltpu.CompilerParams(vmem_limit_bytes=VMEM_LIMIT),
        name=name or body.__name__,
    )(*args)


def per_device(features, adjacency, block_index, block_counts, labels, weight_in, weight_out):
    here, slots, rows = adjacency.shape[:3]
    nodes = here * rows
    deep, hid = weight_in.shape
    classes = weight_out.shape[1]

    feat_e = beside(features)
    loc = ((nodes, nodes), BF16)
    halo = ((nodes, 2 * nodes), BF16)
    w_pair = ((hid, 2 * classes), BF16)
    loc_h, loc_l, halo_h, halo_l, s_loc, win_h, win_l, wout_hl, wout_hh, wout_ll, onehot, feat_out = call(
        prepare,
        [loc, loc, halo, halo, ((nodes, deep), F32), ((deep, hid), BF16), ((deep, hid), BF16),
         w_pair, w_pair, w_pair, ((nodes, classes), F32), ((nodes, deep), F32)],
        [pltpu.with_memory_space_constraint(v, pltpu.HBM)
         for v in (block_index, block_counts, adjacency, features, weight_in, weight_out, labels.reshape(1, nodes))],
        scalars=2,
        flops=6 * nodes * nodes * deep,
        scratch=[
            pltpu.VMEM(adjacency.shape, F32),
            pltpu.VMEM(features.shape, F32),
            pltpu.VMEM(weight_in.shape, F32),
            pltpu.VMEM(weight_out.shape, F32),
            pltpu.VMEM((1, nodes), jnp.int32),
            pltpu.VMEM((here, 3 * here, rows, rows), F32),
            pltpu.SemaphoreType.DMA((4 + here * slots,)),
        ],
        space=pltpu.HBM,
    )
    feat_i = mate(feat_out)
    (s_loc,) = call(
        add_features,
        [((nodes, deep), F32)],
        [halo_h, halo_l, s_loc, feat_e],
        flops=6 * nodes * nodes * deep,
    )
    wide_f, wide_h = ((nodes, hid), F32), ((nodes, hid), BF16)
    thin, thin_t, in_t = ((nodes, classes), F32), ((classes, nodes), F32), ((deep, nodes), BF16)
    (spread_in,) = call(
        spread, [((nodes, deep), F32)], [halo_h, halo_l, s_loc, feat_i], flops=6 * nodes * nodes * deep
    )
    spread_e = beside(spread_in)
    spread_i = mate(spread_in)
    in_oh, in_ol = call(turn, [in_t, in_t], [spread_in])

    def layer_of(high, low, rows_in, before, name, part):
        return call(
            functools.partial(forward, first=name == "forward_own", part=part),
            [thin, wide_f, wide_h, wide_h] + [in_t] * (0 if name == "forward_own" else 2),
            [high, low, rows_in, win_h, win_l, wout_hl, before],
            flops=16 * nodes * nodes * deep,
            name=name,
        )

    logits_o, slope_o, *kept_o = layer_of(loc_h, loc_l, spread_in, onehot, "forward_own", 0)
    logits_i, slope_i, *kept_i = layer_of(halo_h, halo_l, spread_i, logits_o, "forward_mate", 0)
    values, slope_e, *kept_e = layer_of(halo_h, halo_l, spread_e, logits_i, "forward_beside", 1)
    grads_t, loss = call(classify, [((2 * classes, nodes), BF16), ((8, LANES), F32)], [values, onehot])
    half = (deep * hid + hid * classes) // LANES // 2
    hids = [*kept_o[:2], *kept_i[:2], *kept_e[:2]]
    in_ts = [in_oh, in_ol, *kept_i[2:], *kept_e[2:]]
    *pre, ret_loc, out_i, out_e, give = call(
        backward,
        [wide_h] * 6 + [thin_t] * 3 + [((half + classes * (nodes // LANES), LANES), F32)],
        [grads_t, halo_h, halo_l, loc_h, loc_l, slope_o, slope_i, slope_e, *hids,
         *in_ts, wout_hh, wout_ll, loss],
        flops=30 * nodes * nodes * deep,
    )
    got = mate(give)
    keep, logits = call(
        backward_kept,
        [((half, LANES), F32), thin],
        [*hids, *in_ts, *pre, ret_loc, out_i, out_e, loss, values],
        flops=10 * nodes * nodes * deep,
    )
    big, mid = groups((X, Y), (X, Z)), groups((Z,), (Y,))
    wide, narrow = len(big[0]), len(mid[0])
    shard = half // wide
    received = exchange((keep + got[:half]).reshape(wide, shard, LANES), big)
    ret_e = beside(out_e)
    (summed,) = call(sum_repeated, [((narrow, shard, LANES), F32)], [received])
    received = exchange(summed, mid)
    (summed,) = call(sum_repeated, [((1, shard, LANES), F32)], [received])
    (summed,) = call(sum_repeated, [((wide, shard, LANES), F32)], [summed, ret_e], anywhere=1)
    own = exchange(summed, big).reshape(half, LANES)
    other = mate(own)
    (hidden_grad,) = call(
        finish_hidden, [wide_f], [ret_loc, ret_e, got, wout_hh, wout_ll], flops=4 * nodes * nodes * deep
    )
    grad_in, grad_out, mean_loss = call(
        functools.partial(assemble, nodes * lax.axis_size(AXIS)),
        [((deep, hid), F32), ((hid, classes), F32), ((1, 1), F32)],
        [own, other],
        name="assemble",
    )
    return (logits, mean_loss.reshape(()), hidden_grad, grad_in, grad_out)


def solution(mesh):
    split = P(AXIS)
    return jax.shard_map(
        per_device,
        mesh=mesh,
        in_specs=(split, split, split, split, split, P(), P()),
        out_specs=(split, P(), split, P(), P()),
        check_vma=False,
    )
```

```python
import functools
import math

import jax
import jax.numpy as jnp
import numpy as np
from jax import lax
from jax.experimental import pallas as pl
from jax.experimental.pallas import tpu as pltpu
from jax.sharding import PartitionSpec as P

AXIS = "rows"
GRID = (4, 8, 8, 2)
X, Z, Y = range(3)
LANES = 128
F32 = jnp.float32
BF16 = jnp.bfloat16
VMEM_LIMIT = 24 * 1024 * 1024
CHUNK = 256
SQRT_HALF = 0.7071067811865476
INV_SQRT_2PI = 0.3989422804014327
HALF_ERFC = (
    0.0251311707,
    -0.0914511383,
    0.0845433265,
    -0.00280424249,
    0.0707159187,
    0.0842709431,
    0.103921354,
    0.112834799,
    0.112837931,
)


def mate(value):
    return lax.ppermute(value, AXIS, [(i, i ^ 1) for i in range(lax.axis_size(AXIS))])


def beside(value):
    pairs = [(i, i + 1) for i in range(1, lax.axis_size(AXIS) - 1, 2)]
    return lax.ppermute(value, AXIS, pairs + [(b, a) for a, b in pairs])


def groups(*per_core):
    ids = np.arange(math.prod(GRID)).reshape(GRID)
    found = []
    for core, axes in enumerate(per_core):
        rest = [axis for axis in range(3) if axis not in axes]
        size = math.prod(GRID[axis] for axis in axes)
        found += ids[..., core].transpose(rest + list(axes)).reshape(-1, size).tolist()
    return found


def exchange(value, members):
    return lax.all_to_all(value, AXIS, 0, 0, axis_index_groups=members, tiled=True)


def repeated(value, count):
    return jnp.broadcast_to(value[None], (count,) + value.shape)


def halves(value):
    high = value.astype(BF16)
    return high, (value - high.astype(F32)).astype(BF16)


def mm(a, b, dims=((1,), (0,))):
    return lax.dot_general(a, b, (dims, ((), ())), preferred_element_type=F32)


def fold(wide):
    half = wide.shape[1] // 2
    return wide[:, :half] + wide[:, half:]


def prepare(block_index, block_counts, adjacency, features, w_in, w_out, labels,
            loc_h, loc_l, halo_h, halo_l, s_loc, win_h, win_l, wout_hl, wout_hh, wout_ll, onehot, feat_out,
            slots_in, feat_in, win_in, wout_in, labels_in, band, sems):
    here, slots, rows, _ = adjacency.shape
    moves = [(features, feat_in), (w_in, win_in), (w_out, wout_in), (labels, labels_in)]
    moves += [(adjacency.at[b, k], slots_in.at[b, k]) for b in range(here) for k in range(slots)]
    moves = [pltpu.make_async_copy(source, target, sems.at[i]) for i, (source, target) in enumerate(moves)]
    for move in moves:
        move.start()
    me = lax.axis_index(AXIS)
    core = lax.rem(me, 2)
    first = me * here
    band[...] = jnp.zeros_like(band)
    for move in moves[:4]:
        move.wait()
    high, low = halves(win_in[...])
    win_h[...] = high
    win_l[...] = low
    high, low = halves(wout_in[...])
    classes = high.shape[1]
    for ref, left, right in ((wout_hl, high, low), (wout_hh, high, high), (wout_ll, low, low)):
        ref[:, :classes] = left
        ref[:, classes:] = right
    columns = lax.broadcasted_iota(jnp.int32, (classes, labels_in.shape[1]), 0)
    onehot[...] = jnp.where(columns == labels_in[...], 1.0, 0.0).T
    feat_out[...] = feat_in[...]
    feat_h, feat_l = halves(feat_in[...])
    for b in range(here):
        for k in range(slots):
            moves[4 + b * slots + k].wait()
            near = block_index[b, k] - first
            right = near >= here
            outside = jnp.where(right, near - here, near + here)
            outside += jnp.where(right == (core == 0), 0, 2 * here)
            place = jnp.where((near >= 0) & (near < here), here + near, outside)

            @pl.when(k < block_counts[b])
            def _():
                band[b, place] += slots_in[b, k]

        at = pl.ds(b * rows, rows)
        for s in range(3 * here):
            high, low = halves(band[b, s])
            if here <= s < 2 * here:
                cols = pl.ds((s - here) * rows, rows)
                loc_h[at, cols] = high
                loc_l[at, cols] = low
            else:
                cols = pl.ds((s if s < here else s - here) * rows, rows)
                halo_h[at, cols] = high
                halo_l[at, cols] = low
        s_loc[at, :] = mm(loc_h[at, :], feat_h) + mm(loc_h[at, :], feat_l) + mm(loc_l[at, :], feat_h)


def add_features(halo_h, halo_l, s_loc, feat_e, out):
    half = feat_e.shape[0]
    high, low = halves(feat_e[...])
    he, le = halo_h[:, half:], halo_l[:, half:]
    out[...] = s_loc[...] + mm(he, high) + mm(he, low) + mm(le, high)


def spread(halo_h, halo_l, s_loc, feat_i, spread_in, longer):
    half = feat_i.shape[0]
    high, low = halves(feat_i[...])
    hi, li = halo_h[:, :half], halo_l[:, :half]
    value = s_loc[...] + mm(hi, high) + mm(hi, low) + mm(li, high)
    spread_in[...] = value
    longer[:half, :] = value
    longer[half:, :] = jnp.zeros_like(longer[half:, :])


def layer(spread_in, win_h, win_l):
    s_h, s_l = halves(spread_in)
    pre = mm(s_h, win_h[...]) + mm(s_h, win_l[...]) + mm(s_l, win_h[...])
    bell = jnp.exp(-0.5 * pre * pre)
    t = 1.0 / (1.0 + (0.4 * SQRT_HALF) * jnp.abs(pre))
    poly = jnp.full_like(t, HALF_ERFC[0])
    for term in HALF_ERFC[1:]:
        poly = poly * t + term
    tail = bell * (t * poly)
    gate = jnp.where(pre < 0, tail, 1.0 - tail)
    return pre * gate, gate + pre * (INV_SQRT_2PI * bell)


def forward(high_band, low_band, spread_in, win_h, win_l, wout_hl, logits_before,
            scores_sum, slope, hid_h, hid_l, *in_t, first, part):
    nodes = slope.shape[0]
    rows_in = spread_in[:nodes, :]
    hidden, slope[...] = layer(rows_in, win_h, win_l)
    high, low = halves(hidden)
    hid_h[...] = high
    hid_l[...] = low
    pair = jnp.concatenate(halves(fold(mm(high, wout_hl[...]) + mm(low, wout_hl[...]))), axis=1)
    cols = slice(part * nodes, (part + 1) * nodes)
    logits = fold(mm(high_band[:, cols], pair) + mm(low_band[:, cols], pair))
    scores_sum[...] = logits if first else logits_before[...] + logits
    if in_t:
        turn(rows_in, *in_t)


def turn(spread_in, in_th, in_tl):
    high, low = halves(spread_in[...].T)
    in_th[...] = high
    in_tl[...] = low


def stacked(grads, high, low):
    tall = mm(grads, high) + mm(grads, low)
    half = tall.shape[0] // 2
    return tall[:half] + tall[half:]


def classify(values, onehot, grads_t, loss):
    scores = values[...]
    totals = jnp.log(jnp.sum(jnp.exp(scores), axis=1, keepdims=True))
    hot = onehot[...]
    grads_t[...] = jnp.concatenate(halves((jnp.exp(scores - totals) - hot).T), axis=0)
    row_loss = totals - jnp.sum(hot * scores, axis=1, keepdims=True)
    loss[...] = jnp.broadcast_to(jnp.sum(row_loss, axis=0, keepdims=True), loss.shape)


def gradient_half(which, parts, loss, out):
    deep, hid = parts[0][2][0].shape[0] // 2, parts[0][1][0].shape[1] // 2
    at = pl.ds(pl.multiple_of(which * deep, deep), deep)
    cols = pl.ds(pl.multiple_of(which * hid, hid), hid)
    grad_in = grad_out_t = 0.0
    for returned_t, (hid_h, hid_l), (in_th, in_tl), (pre_h, pre_l) in parts:
        high, low = in_th[at, :], in_tl[at, :]
        tall = mm(jnp.concatenate([high, low], axis=0), pre_h)
        grad_in = grad_in + (tall[:deep] + tall[deep:] + mm(high, pre_l))
        tall = jnp.concatenate(halves(returned_t), axis=0)
        grad_out_t = grad_out_t + stacked(tall, hid_h[:, cols], hid_l[:, cols])
    for t in range(grad_in.shape[1] // LANES):
        out[pl.ds(t * deep, deep), :] = grad_in[:, t * LANES : (t + 1) * LANES]
    grad_out = grad_out_t.T
    grad_out = jnp.where(last_element(grad_out) & (which == 1), loss[:1, :], grad_out)
    rows = deep * (grad_in.shape[1] // LANES)
    out[pl.ds(rows, hid), :] = grad_out
    return rows + hid


def last_element(value):
    row = lax.broadcasted_iota(jnp.int32, value.shape, 0)
    column = lax.broadcasted_iota(jnp.int32, value.shape, 1)
    return (row == value.shape[0] - 1) & (column == value.shape[1] - 1)


def backward(grads_t, halo_h, halo_l, loc_h, loc_l, slope_o, slope_i, slope_e, hid_oh, hid_ol, hid_ih, hid_il, hid_eh, hid_el,
             in_oh, in_ol, in_ih, in_il, in_eh, in_el, wout_hh, wout_ll, loss,
             pre_oh, pre_ol, pre_ih, pre_il, pre_eh, pre_el, ret_loc, out_i, out_e, give):
    grads = grads_t[...]
    half = loc_h.shape[1]
    own = stacked(grads, loc_h[...], loc_l[...])
    near = stacked(grads, halo_h[:, :half], halo_l[:, :half])
    far = stacked(grads, halo_h[:, half:], halo_l[:, half:])
    ret_loc[...] = own
    out_i[...] = near
    out_e[...] = far
    across = ((1,), (1,))
    parts = []
    for returned_t, slope, hidden, inputs, pre_h, pre_l in (
        (own, slope_o, (hid_oh, hid_ol), (in_oh, in_ol), pre_oh, pre_ol),
        (near, slope_i, (hid_ih, hid_il), (in_ih, in_il), pre_ih, pre_il),
        (far, slope_e, (hid_eh, hid_el), (in_eh, in_el), pre_eh, pre_el),
    ):
        both = jnp.concatenate(halves(returned_t.T), axis=1)
        hidden_grad = mm(both, wout_hh[...], across) + mm(both, wout_ll[...], across)
        high, low = halves(hidden_grad * slope[...])
        pre_h[...] = high
        pre_l[...] = low
        parts.append((returned_t, hidden, inputs, (high, low)))
    other = 1 - lax.rem(lax.axis_index(AXIS), 2)
    end = gradient_half(other, parts, loss, give)
    classes = near.shape[0]
    for t in range(half // LANES):
        give[pl.ds(end + t * classes, classes), :] = near[:, t * LANES : (t + 1) * LANES]


def backward_kept(hid_oh, hid_ol, hid_ih, hid_il, hid_eh, hid_el, in_oh, in_ol, in_ih, in_il, in_eh, in_el,
                  pre_oh, pre_ol, pre_ih, pre_il, pre_eh, pre_el, ret_loc, out_i, out_e, loss, values,
                  keep, logits):
    core = lax.rem(lax.axis_index(AXIS), 2)
    parts = (
        (ret_loc[...], (hid_oh, hid_ol), (in_oh, in_ol), (pre_oh[...], pre_ol[...])),
        (out_i[...], (hid_ih, hid_il), (in_ih, in_il), (pre_ih[...], pre_il[...])),
        (out_e[...], (hid_eh, hid_el), (in_eh, in_el), (pre_eh[...], pre_el[...])),
    )
    gradient_half(core, parts, loss, keep)
    logits[...] = values[...]


def finish_hidden(ret_loc, ret_e, got, wout_hh, wout_ll, hidden_grad):
    classes, nodes = ret_loc.shape
    start = got.shape[0] - classes * (nodes // LANES)
    ret_i = [got[pl.ds(start + t * classes, classes), :] for t in range(nodes // LANES)]
    returned_t = ret_loc[...] + ret_e[...] + jnp.concatenate(ret_i, axis=1)
    both = jnp.concatenate(halves(returned_t.T), axis=1)
    across = ((1,), (1,))
    hidden_grad[...] = mm(both, wout_hh[...], across) + mm(both, wout_ll[...], across)


def sum_repeated(received, *refs):
    out = refs[-1]
    total = received[0]
    for k in range(1, received.shape[0]):
        total = total + received[k]
    out[...] = jnp.broadcast_to(total[None], out.shape)


def assemble(nodes_total, own, other, grad_in, grad_out, mean_loss):
    deep = grad_in.shape[0] // 2
    hid = grad_out.shape[0] // 2
    tiles = grad_in.shape[1] // LANES
    core = lax.rem(lax.axis_index(AXIS), 2)
    for half, which in ((own, core), (other, 1 - core)):
        at = pl.ds(pl.multiple_of(which * deep, deep), deep)
        for t in range(tiles):
            grad_in[at, t * LANES : (t + 1) * LANES] = half[pl.ds(t * deep, deep), :]
        at = pl.ds(pl.multiple_of(which * hid, hid), hid)
        grad_out[at, :] = half[pl.ds(tiles * deep, hid), :]
    end = pl.ds(2 * hid - 8, 8)
    value = grad_out[end, :]
    there = last_element(value)
    mean_loss[0, 0] = jnp.sum(jnp.where(there, value, 0.0)) / nodes_total
    others = jnp.sum(jnp.where(there, 0.0, value), axis=1, keepdims=True)
    grad_out[end, :] = jnp.where(there, -others, value)


def call(body, outs, args, scalars=0, anywhere=0, flops=0, scratch=(), space=pltpu.VMEM, cheap=False, name=""):
    smem = pl.BlockSpec(memory_space=pltpu.SMEM)
    vmem = pl.BlockSpec(memory_space=pltpu.VMEM)
    moved = 0 if cheap else sum(a.size * a.dtype.itemsize for a in args)
    flops = 0 if cheap else flops
    return pl.pallas_call(
        body,
        out_shape=[jax.ShapeDtypeStruct(shape, kind) for shape, kind in outs],
        in_specs=[smem] * scalars
        + [pl.BlockSpec(memory_space=space)] * (len(args) - scalars - anywhere)
        + [pl.BlockSpec(memory_space=pl.ANY)] * anywhere,
        out_specs=[smem if shape == (1, 1) else vmem for shape, _ in outs],
        scratch_shapes=scratch,
        cost_estimate=pl.CostEstimate(flops=flops, bytes_accessed=moved, transcendentals=0),
        compiler_params=pltpu.CompilerParams(vmem_limit_bytes=VMEM_LIMIT),
        name=name or body.__name__,
    )(*args)


def per_device(features, adjacency, block_index, block_counts, labels, weight_in, weight_out):
    here, slots, rows = adjacency.shape[:3]
    nodes = here * rows
    deep, hid = weight_in.shape
    classes = weight_out.shape[1]

    feat_e = beside(features)
    loc = ((nodes, nodes), BF16)
    halo = ((nodes, 2 * nodes), BF16)
    w_pair = ((hid, 2 * classes), BF16)
    loc_h, loc_l, halo_h, halo_l, s_loc, win_h, win_l, wout_hl, wout_hh, wout_ll, onehot, feat_out = call(
        prepare,
        [loc, loc, halo, halo, ((nodes, deep), F32), ((deep, hid), BF16), ((deep, hid), BF16),
         w_pair, w_pair, w_pair, ((nodes, classes), F32), ((nodes, deep), F32)],
        [pltpu.with_memory_space_constraint(v, pltpu.HBM)
         for v in (block_index, block_counts, adjacency, features, weight_in, weight_out, labels.reshape(1, nodes))],
        scalars=2,
        flops=6 * nodes * nodes * deep,
        scratch=[
            pltpu.VMEM(adjacency.shape, F32),
            pltpu.VMEM(features.shape, F32),
            pltpu.VMEM(weight_in.shape, F32),
            pltpu.VMEM(weight_out.shape, F32),
            pltpu.VMEM((1, nodes), jnp.int32),
            pltpu.VMEM((here, 3 * here, rows, rows), F32),
            pltpu.SemaphoreType.DMA((4 + here * slots,)),
        ],
        space=pltpu.HBM,
    )
    feat_i = mate(feat_out)
    (s_loc,) = call(
        add_features,
        [((nodes, deep), F32)],
        [halo_h, halo_l, s_loc, feat_e],
        flops=6 * nodes * nodes * deep,
    )
    wide_f, wide_h = ((nodes, hid), F32), ((nodes, hid), BF16)
    thin, thin_t, in_t = ((nodes, classes), F32), ((classes, nodes), F32), ((deep, nodes), BF16)
    spread_in, longer = call(
        spread, [((nodes, deep), F32), ((nodes + 8, deep), F32)], [halo_h, halo_l, s_loc, feat_i], flops=6 * nodes * nodes * deep
    )
    spread_e = beside(longer)
    spread_i = mate(spread_in)
    in_oh, in_ol = call(turn, [in_t, in_t], [spread_in])

    def layer_of(high, low, rows_in, before, name, part):
        return call(
            functools.partial(forward, first=name == "forward_own", part=part),
            [thin, wide_f, wide_h, wide_h] + [in_t] * (0 if name == "forward_own" else 2),
            [high, low, rows_in, win_h, win_l, wout_hl, before],
            flops=16 * nodes * nodes * deep,
            cheap=name == "forward_mate",
            name=name,
        )

    logits_o, slope_o, *kept_o = layer_of(loc_h, loc_l, spread_in, onehot, "forward_own", 0)
    logits_i, slope_i, *kept_i = layer_of(halo_h, halo_l, spread_i, logits_o, "forward_mate", 0)
    values, slope_e, *kept_e = layer_of(halo_h, halo_l, spread_e, logits_i, "forward_beside", 1)
    grads_t, loss = call(classify, [((2 * classes, nodes), BF16), ((8, LANES), F32)], [values, onehot])
    half = (deep * hid + hid * classes) // LANES // 2
    hids = [*kept_o[:2], *kept_i[:2], *kept_e[:2]]
    in_ts = [in_oh, in_ol, *kept_i[2:], *kept_e[2:]]
    *pre, ret_loc, out_i, out_e, give = call(
        backward,
        [wide_h] * 6 + [thin_t] * 3 + [((half + classes * (nodes // LANES), LANES), F32)],
        [grads_t, halo_h, halo_l, loc_h, loc_l, slope_o, slope_i, slope_e, *hids,
         *in_ts, wout_hh, wout_ll, loss],
        flops=30 * nodes * nodes * deep,
    )
    got = mate(give)
    keep, logits = call(
        backward_kept,
        [((half, LANES), F32), thin],
        [*hids, *in_ts, *pre, ret_loc, out_i, out_e, loss, values],
        flops=10 * nodes * nodes * deep,
    )
    big, mid = groups((X, Y), (X, Z)), groups((Z,), (Y,))
    wide, narrow = len(big[0]), len(mid[0])
    shard = half // wide
    received = exchange((keep + got[:half]).reshape(wide, shard, LANES), big)
    ret_e = beside(out_e)
    (summed,) = call(sum_repeated, [((narrow, shard, LANES), F32)], [received])
    received = exchange(summed, mid)
    (summed,) = call(sum_repeated, [((1, shard, LANES), F32)], [received])
    (summed,) = call(sum_repeated, [((wide, shard, LANES), F32)], [summed, ret_e], anywhere=1)
    own = exchange(summed, big).reshape(half, LANES)
    other = mate(own)
    (hidden_grad,) = call(
        finish_hidden, [wide_f], [ret_loc, ret_e, got, wout_hh, wout_ll], flops=4 * nodes * nodes * deep
    )
    grad_in, grad_out, mean_loss = call(
        functools.partial(assemble, nodes * lax.axis_size(AXIS)),
        [((deep, hid), F32), ((hid, classes), F32), ((1, 1), F32)],
        [own, other],
        name="assemble",
    )
    return (logits, mean_loss.reshape(()), hidden_grad, grad_in, grad_out)


def solution(mesh):
    split = P(AXIS)
    return jax.shard_map(
        per_device,
        mesh=mesh,
        in_specs=(split, split, split, split, split, P(), P()),
        out_specs=(split, P(), split, P(), P()),
        check_vma=False,
    )
```

```python
import functools
import math

import jax
import jax.numpy as jnp
import numpy as np
from jax import lax
from jax.experimental import pallas as pl
from jax.experimental.pallas import tpu as pltpu
from jax.sharding import PartitionSpec as P

AXIS = "rows"
GRID = (4, 8, 8, 2)
X, Z, Y = range(3)
LANES = 128
F32 = jnp.float32
BF16 = jnp.bfloat16
VMEM_LIMIT = 24 * 1024 * 1024
CHUNK = 256
SQRT_HALF = 0.7071067811865476
INV_SQRT_2PI = 0.3989422804014327
HALF_ERFC = (
    0.0251311707,
    -0.0914511383,
    0.0845433265,
    -0.00280424249,
    0.0707159187,
    0.0842709431,
    0.103921354,
    0.112834799,
    0.112837931,
)


def mate(value):
    return lax.ppermute(value, AXIS, [(i, i ^ 1) for i in range(lax.axis_size(AXIS))])


def beside(value):
    pairs = [(i, i + 1) for i in range(1, lax.axis_size(AXIS) - 1, 2)]
    return lax.ppermute(value, AXIS, pairs + [(b, a) for a, b in pairs])


def groups(*per_core):
    ids = np.arange(math.prod(GRID)).reshape(GRID)
    found = []
    for core, axes in enumerate(per_core):
        rest = [axis for axis in range(3) if axis not in axes]
        size = math.prod(GRID[axis] for axis in axes)
        found += ids[..., core].transpose(rest + list(axes)).reshape(-1, size).tolist()
    return found


def exchange(value, members):
    return lax.all_to_all(value, AXIS, 0, 0, axis_index_groups=members, tiled=True)


def repeated(value, count):
    return jnp.broadcast_to(value[None], (count,) + value.shape)


def halves(value):
    high = value.astype(BF16)
    return high, (value - high.astype(F32)).astype(BF16)


def mm(a, b, dims=((1,), (0,))):
    return lax.dot_general(a, b, (dims, ((), ())), preferred_element_type=F32)


def fold(wide):
    half = wide.shape[1] // 2
    return wide[:, :half] + wide[:, half:]


def prepare(block_index, block_counts, adjacency, features, w_in, w_out, labels,
            loc_h, loc_l, halo_h, halo_l, s_loc, win_h, win_l, wout_hl, wout_hh, wout_ll, onehot, feat_out,
            slots_in, feat_in, win_in, wout_in, labels_in, band, sems):
    here, slots, rows, _ = adjacency.shape
    moves = [(features, feat_in), (w_in, win_in), (w_out, wout_in), (labels, labels_in)]
    moves += [(adjacency.at[b, k], slots_in.at[b, k]) for b in range(here) for k in range(slots)]
    moves = [pltpu.make_async_copy(source, target, sems.at[i]) for i, (source, target) in enumerate(moves)]
    for move in moves:
        move.start()
    me = lax.axis_index(AXIS)
    core = lax.rem(me, 2)
    first = me * here
    band[...] = jnp.zeros_like(band)
    for move in moves[:4]:
        move.wait()
    high, low = halves(win_in[...])
    win_h[...] = high
    win_l[...] = low
    high, low = halves(wout_in[...])
    classes = high.shape[1]
    for ref, left, right in ((wout_hl, high, low), (wout_hh, high, high), (wout_ll, low, low)):
        ref[:, :classes] = left
        ref[:, classes:] = right
    columns = lax.broadcasted_iota(jnp.int32, (classes, labels_in.shape[1]), 0)
    onehot[...] = jnp.where(columns == labels_in[...], 1.0, 0.0).T
    feat_out[...] = feat_in[...]
    feat_h, feat_l = halves(feat_in[...])
    for b in range(here):
        for k in range(slots):
            moves[4 + b * slots + k].wait()
            near = block_index[b, k] - first
            right = near >= here
            outside = jnp.where(right, near - here, near + here)
            outside += jnp.where(right == (core == 0), 0, 2 * here)
            place = jnp.where((near >= 0) & (near < here), here + near, outside)

            @pl.when(k < block_counts[b])
            def _():
                band[b, place] += slots_in[b, k]

        at = pl.ds(b * rows, rows)
        for s in range(3 * here):
            high, low = halves(band[b, s])
            if here <= s < 2 * here:
                cols = pl.ds((s - here) * rows, rows)
                loc_h[at, cols] = high
                loc_l[at, cols] = low
            else:
                cols = pl.ds((s if s < here else s - here) * rows, rows)
                halo_h[at, cols] = high
                halo_l[at, cols] = low
        s_loc[at, :] = mm(loc_h[at, :], feat_h) + mm(loc_h[at, :], feat_l) + mm(loc_l[at, :], feat_h)


def add_features(halo_h, halo_l, s_loc, feat_e, out):
    half = feat_e.shape[0]
    high, low = halves(feat_e[...])
    he, le = halo_h[:, half:], halo_l[:, half:]
    out[...] = s_loc[...] + mm(he, high) + mm(he, low) + mm(le, high)


def spread(halo_h, halo_l, s_loc, feat_i, spread_in, longer):
    half = feat_i.shape[0]
    high, low = halves(feat_i[...])
    hi, li = halo_h[:, :half], halo_l[:, :half]
    value = s_loc[...] + mm(hi, high) + mm(hi, low) + mm(li, high)
    spread_in[...] = value
    longer[:half, :] = value
    longer[half:, :] = jnp.zeros_like(longer[half:, :])


def layer(spread_in, win_h, win_l):
    s_h, s_l = halves(spread_in)
    pre = mm(s_h, win_h[...]) + mm(s_h, win_l[...]) + mm(s_l, win_h[...])
    bell = jnp.exp(-0.5 * pre * pre)
    t = 1.0 / (1.0 + (0.4 * SQRT_HALF) * jnp.abs(pre))
    poly = jnp.full_like(t, HALF_ERFC[0])
    for term in HALF_ERFC[1:]:
        poly = poly * t + term
    tail = bell * (t * poly)
    gate = jnp.where(pre < 0, tail, 1.0 - tail)
    return pre * gate, gate + pre * (INV_SQRT_2PI * bell)


def forward(high_band, low_band, spread_in, win_h, win_l, wout_hl, logits_before,
            scores_sum, slope, hid_h, hid_l, *in_t, first, part):
    nodes = slope.shape[0]
    rows_in = spread_in[:nodes, :]
    hidden, slope[...] = layer(rows_in, win_h, win_l)
    high, low = halves(hidden)
    hid_h[...] = high
    hid_l[...] = low
    pair = jnp.concatenate(halves(fold(mm(high, wout_hl[...]) + mm(low, wout_hl[...]))), axis=1)
    cols = slice(part * nodes, (part + 1) * nodes)
    logits = fold(mm(high_band[:, cols], pair) + mm(low_band[:, cols], pair))
    scores_sum[...] = logits if first else logits_before[...] + logits
    if in_t:
        turn(rows_in, *in_t)


def turn(spread_in, in_th, in_tl):
    high, low = halves(spread_in[...].T)
    in_th[...] = high
    in_tl[...] = low


def stacked(grads, high, low):
    tall = mm(grads, high) + mm(grads, low)
    half = tall.shape[0] // 2
    return tall[:half] + tall[half:]


def classify(values, onehot, grads_t, loss):
    scores = values[...]
    totals = jnp.log(jnp.sum(jnp.exp(scores), axis=1, keepdims=True))
    hot = onehot[...]
    grads_t[...] = jnp.concatenate(halves((jnp.exp(scores - totals) - hot).T), axis=0)
    row_loss = totals - jnp.sum(hot * scores, axis=1, keepdims=True)
    loss[...] = jnp.broadcast_to(jnp.sum(row_loss, axis=0, keepdims=True), loss.shape)


def gradient_half(which, parts, loss, out):
    deep, hid = parts[0][2][0].shape[0] // 2, parts[0][1][0].shape[1] // 2
    at = pl.ds(pl.multiple_of(which * deep, deep), deep)
    cols = pl.ds(pl.multiple_of(which * hid, hid), hid)
    grad_in = grad_out_t = 0.0
    for returned_t, (hid_h, hid_l), (in_th, in_tl), (pre_h, pre_l) in parts:
        high, low = in_th[at, :], in_tl[at, :]
        tall = mm(jnp.concatenate([high, low], axis=0), pre_h)
        grad_in = grad_in + (tall[:deep] + tall[deep:] + mm(high, pre_l))
        tall = jnp.concatenate(halves(returned_t), axis=0)
        grad_out_t = grad_out_t + stacked(tall, hid_h[:, cols], hid_l[:, cols])
    for t in range(grad_in.shape[1] // LANES):
        out[pl.ds(t * deep, deep), :] = grad_in[:, t * LANES : (t + 1) * LANES]
    grad_out = grad_out_t.T
    grad_out = jnp.where(last_element(grad_out) & (which == 1), loss[:1, :], grad_out)
    rows = deep * (grad_in.shape[1] // LANES)
    out[pl.ds(rows, hid), :] = grad_out
    return rows + hid


def last_element(value):
    row = lax.broadcasted_iota(jnp.int32, value.shape, 0)
    column = lax.broadcasted_iota(jnp.int32, value.shape, 1)
    return (row == value.shape[0] - 1) & (column == value.shape[1] - 1)


def backward(grads_t, halo_h, halo_l, loc_h, loc_l, slope_o, slope_i, slope_e, hid_oh, hid_ol, hid_ih, hid_il, hid_eh, hid_el,
             in_oh, in_ol, in_ih, in_il, in_eh, in_el, wout_hh, wout_ll, loss,
             pre_oh, pre_ol, pre_ih, pre_il, pre_eh, pre_el, ret_loc, out_i, out_e, give):
    grads = grads_t[...]
    half = loc_h.shape[1]
    own = stacked(grads, loc_h[...], loc_l[...])
    near = stacked(grads, halo_h[:, :half], halo_l[:, :half])
    far = stacked(grads, halo_h[:, half:], halo_l[:, half:])
    ret_loc[...] = own
    out_i[...] = near
    out_e[...] = far
    across = ((1,), (1,))
    parts = []
    for returned_t, slope, hidden, inputs, pre_h, pre_l in (
        (own, slope_o, (hid_oh, hid_ol), (in_oh, in_ol), pre_oh, pre_ol),
        (near, slope_i, (hid_ih, hid_il), (in_ih, in_il), pre_ih, pre_il),
        (far, slope_e, (hid_eh, hid_el), (in_eh, in_el), pre_eh, pre_el),
    ):
        both = jnp.concatenate(halves(returned_t.T), axis=1)
        hidden_grad = mm(both, wout_hh[...], across) + mm(both, wout_ll[...], across)
        high, low = halves(hidden_grad * slope[...])
        pre_h[...] = high
        pre_l[...] = low
        parts.append((returned_t, hidden, inputs, (high, low)))
    other = 1 - lax.rem(lax.axis_index(AXIS), 2)
    end = gradient_half(other, parts, loss, give)
    classes = near.shape[0]
    for t in range(half // LANES):
        give[pl.ds(end + t * classes, classes), :] = near[:, t * LANES : (t + 1) * LANES]


def backward_kept(hid_oh, hid_ol, hid_ih, hid_il, hid_eh, hid_el, in_oh, in_ol, in_ih, in_il, in_eh, in_el,
                  pre_oh, pre_ol, pre_ih, pre_il, pre_eh, pre_el, ret_loc, out_i, out_e, loss,
                  keep):
    core = lax.rem(lax.axis_index(AXIS), 2)
    parts = (
        (ret_loc[...], (hid_oh, hid_ol), (in_oh, in_ol), (pre_oh[...], pre_ol[...])),
        (out_i[...], (hid_ih, hid_il), (in_ih, in_il), (pre_ih[...], pre_il[...])),
        (out_e[...], (hid_eh, hid_el), (in_eh, in_el), (pre_eh[...], pre_el[...])),
    )
    gradient_half(core, parts, loss, keep)


def from_beside(*refs):
    halo_h, halo_l, loc_h, loc_l, spread_e, win_h, win_l, wout_hl, wout_hh, wout_ll, logits_i, onehot = refs[:12]
    slope_o, slope_i, hid_oh, hid_ol, hid_ih, hid_il, in_oh, in_ol, in_ih, in_il = refs[12:22]
    values, slope_e, hid_eh, hid_el, in_eh, in_el, grads_t, loss = refs[22:30]
    forward(halo_h, halo_l, spread_e, win_h, win_l, wout_hl, logits_i,
            values, slope_e, hid_eh, hid_el, in_eh, in_el, first=False, part=1)
    classify(values, onehot, grads_t, loss)
    backward(grads_t, halo_h, halo_l, loc_h, loc_l, slope_o, slope_i, slope_e, hid_oh, hid_ol, hid_ih, hid_il, hid_eh, hid_el,
             in_oh, in_ol, in_ih, in_il, in_eh, in_el, wout_hh, wout_ll, loss, *refs[30:])


def put_logits(values, logits, token):
    logits[...] = values[...]
    token[...] = values[:8, :]


def finish_hidden(ret_loc, ret_e, got, wout_hh, wout_ll, hidden_grad):
    classes, nodes = ret_loc.shape
    start = got.shape[0] - classes * (nodes // LANES)
    ret_i = [got[pl.ds(start + t * classes, classes), :] for t in range(nodes // LANES)]
    returned_t = ret_loc[...] + ret_e[...] + jnp.concatenate(ret_i, axis=1)
    both = jnp.concatenate(halves(returned_t.T), axis=1)
    across = ((1,), (1,))
    hidden_grad[...] = mm(both, wout_hh[...], across) + mm(both, wout_ll[...], across)


def sum_repeated(received, *refs):
    out = refs[-1]
    total = received[0]
    for k in range(1, received.shape[0]):
        total = total + received[k]
    out[...] = jnp.broadcast_to(total[None], out.shape)


def assemble(nodes_total, own, other, grad_in, grad_out, mean_loss):
    deep = grad_in.shape[0] // 2
    hid = grad_out.shape[0] // 2
    tiles = grad_in.shape[1] // LANES
    core = lax.rem(lax.axis_index(AXIS), 2)
    for half, which in ((own, core), (other, 1 - core)):
        at = pl.ds(pl.multiple_of(which * deep, deep), deep)
        for t in range(tiles):
            grad_in[at, t * LANES : (t + 1) * LANES] = half[pl.ds(t * deep, deep), :]
        at = pl.ds(pl.multiple_of(which * hid, hid), hid)
        grad_out[at, :] = half[pl.ds(tiles * deep, hid), :]
    end = pl.ds(2 * hid - 8, 8)
    value = grad_out[end, :]
    there = last_element(value)
    mean_loss[0, 0] = jnp.sum(jnp.where(there, value, 0.0)) / nodes_total
    others = jnp.sum(jnp.where(there, 0.0, value), axis=1, keepdims=True)
    grad_out[end, :] = jnp.where(there, -others, value)


def call(body, outs, args, scalars=0, anywhere=0, flops=0, scratch=(), space=pltpu.VMEM, cheap=False, limit=VMEM_LIMIT, name=""):
    smem = pl.BlockSpec(memory_space=pltpu.SMEM)
    vmem = pl.BlockSpec(memory_space=pltpu.VMEM)
    moved = 0 if cheap else sum(a.size * a.dtype.itemsize for a in args)
    flops = 0 if cheap else flops
    return pl.pallas_call(
        body,
        out_shape=[jax.ShapeDtypeStruct(shape, kind) for shape, kind in outs],
        in_specs=[smem] * scalars
        + [pl.BlockSpec(memory_space=space)] * (len(args) - scalars - anywhere)
        + [pl.BlockSpec(memory_space=pl.ANY)] * anywhere,
        out_specs=[smem if shape == (1, 1) else vmem for shape, _ in outs],
        scratch_shapes=scratch,
        cost_estimate=pl.CostEstimate(flops=flops, bytes_accessed=moved, transcendentals=0),
        compiler_params=pltpu.CompilerParams(vmem_limit_bytes=limit),
        name=name or body.__name__,
    )(*args)


def per_device(features, adjacency, block_index, block_counts, labels, weight_in, weight_out):
    here, slots, rows = adjacency.shape[:3]
    nodes = here * rows
    deep, hid = weight_in.shape
    classes = weight_out.shape[1]

    feat_e = beside(features)
    loc = ((nodes, nodes), BF16)
    halo = ((nodes, 2 * nodes), BF16)
    w_pair = ((hid, 2 * classes), BF16)
    loc_h, loc_l, halo_h, halo_l, s_loc, win_h, win_l, wout_hl, wout_hh, wout_ll, onehot, feat_out = call(
        prepare,
        [loc, loc, halo, halo, ((nodes, deep), F32), ((deep, hid), BF16), ((deep, hid), BF16),
         w_pair, w_pair, w_pair, ((nodes, classes), F32), ((nodes, deep), F32)],
        [pltpu.with_memory_space_constraint(v, pltpu.HBM)
         for v in (block_index, block_counts, adjacency, features, weight_in, weight_out, labels.reshape(1, nodes))],
        scalars=2,
        flops=6 * nodes * nodes * deep,
        scratch=[
            pltpu.VMEM(adjacency.shape, F32),
            pltpu.VMEM(features.shape, F32),
            pltpu.VMEM(weight_in.shape, F32),
            pltpu.VMEM(weight_out.shape, F32),
            pltpu.VMEM((1, nodes), jnp.int32),
            pltpu.VMEM((here, 3 * here, rows, rows), F32),
            pltpu.SemaphoreType.DMA((4 + here * slots,)),
        ],
        space=pltpu.HBM,
    )
    feat_i = mate(feat_out)
    (s_loc,) = call(
        add_features,
        [((nodes, deep), F32)],
        [halo_h, halo_l, s_loc, feat_e],
        flops=6 * nodes * nodes * deep,
    )
    wide_f, wide_h = ((nodes, hid), F32), ((nodes, hid), BF16)
    thin, thin_t, in_t = ((nodes, classes), F32), ((classes, nodes), F32), ((deep, nodes), BF16)
    spread_in, longer = call(
        spread, [((nodes, deep), F32), ((nodes + 8, deep), F32)], [halo_h, halo_l, s_loc, feat_i], flops=6 * nodes * nodes * deep
    )
    spread_e = beside(longer)
    spread_i = mate(spread_in)
    in_oh, in_ol = call(turn, [in_t, in_t], [spread_in])

    def layer_of(high, low, rows_in, before, name, part):
        return call(
            functools.partial(forward, first=name == "forward_own", part=part),
            [thin, wide_f, wide_h, wide_h] + [in_t] * (0 if name == "forward_own" else 2),
            [high, low, rows_in, win_h, win_l, wout_hl, before],
            flops=16 * nodes * nodes * deep,
            cheap=name == "forward_mate",
            name=name,
        )

    logits_o, slope_o, *kept_o = layer_of(loc_h, loc_l, spread_in, onehot, "forward_own", 0)
    logits_i, slope_i, *kept_i = layer_of(halo_h, halo_l, spread_i, logits_o, "forward_mate", 0)
    half = (deep * hid + hid * classes) // LANES // 2
    values, slope_e, hid_eh, hid_el, in_eh, in_el, _, loss, *pre, ret_loc, out_i, out_e, give = call(
        from_beside,
        [thin, wide_f, wide_h, wide_h, in_t, in_t, ((2 * classes, nodes), BF16), ((8, LANES), F32)]
        + [wide_h] * 6 + [thin_t] * 3 + [((half + classes * (nodes // LANES), LANES), F32)],
        [halo_h, halo_l, loc_h, loc_l, spread_e, win_h, win_l, wout_hl, wout_hh, wout_ll, logits_i, onehot,
         slope_o, slope_i, *kept_o[:2], *kept_i[:2], in_oh, in_ol, *kept_i[2:]],
        flops=46 * nodes * nodes * deep,
        limit=VMEM_LIMIT,
    )
    hids = [*kept_o[:2], *kept_i[:2], hid_eh, hid_el]
    in_ts = [in_oh, in_ol, *kept_i[2:], in_eh, in_el]
    got = mate(give)
    logits, token = call(put_logits, [thin, ((8, LANES), F32)], [values])
    (keep,) = call(
        backward_kept,
        [((half, LANES), F32)],
        [*hids, *in_ts, *pre, ret_loc, out_i, out_e, loss],
        flops=10 * nodes * nodes * deep,
    )
    big, mid = groups((X, Y), (X, Z)), groups((Z,), (Y,))
    wide, narrow = len(big[0]), len(mid[0])
    shard = half // wide
    received = exchange((keep + got[:half]).reshape(wide, shard, LANES), big)
    ret_e = beside(out_e)
    (summed,) = call(sum_repeated, [((narrow, shard, LANES), F32)], [received, token])
    received = exchange(summed, mid)
    (summed,) = call(sum_repeated, [((1, shard, LANES), F32)], [received])
    (summed,) = call(sum_repeated, [((wide, shard, LANES), F32)], [summed, ret_e], anywhere=1)
    own = exchange(summed, big).reshape(half, LANES)
    other = mate(own)
    (hidden_grad,) = call(
        finish_hidden, [wide_f], [ret_loc, ret_e, got, wout_hh, wout_ll], flops=4 * nodes * nodes * deep
    )
    grad_in, grad_out, mean_loss = call(
        functools.partial(assemble, nodes * lax.axis_size(AXIS)),
        [((deep, hid), F32), ((hid, classes), F32), ((1, 1), F32)],
        [own, other],
        name="assemble",
    )
    return (logits, mean_loss.reshape(()), hidden_grad, grad_in, grad_out)


def solution(mesh):
    split = P(AXIS)
    return jax.shard_map(
        per_device,
        mesh=mesh,
        in_specs=(split, split, split, split, split, P(), P()),
        out_specs=(split, P(), split, P(), P()),
        check_vma=False,
    )
```

```python
import functools
import math

import jax
import jax.numpy as jnp
import numpy as np
from jax import lax
from jax.experimental import pallas as pl
from jax.experimental.pallas import tpu as pltpu
from jax.sharding import PartitionSpec as P

AXIS = "rows"
GRID = (4, 8, 8, 2)
X, Z, Y = range(3)
LANES = 128
F32 = jnp.float32
BF16 = jnp.bfloat16
VMEM_LIMIT = 24 * 1024 * 1024
CHUNK = 256
SQRT_HALF = 0.7071067811865476
INV_SQRT_2PI = 0.3989422804014327
HALF_ERFC = (
    0.0251311707,
    -0.0914511383,
    0.0845433265,
    -0.00280424249,
    0.0707159187,
    0.0842709431,
    0.103921354,
    0.112834799,
    0.112837931,
)


def mate(value):
    return lax.ppermute(value, AXIS, [(i, i ^ 1) for i in range(lax.axis_size(AXIS))])


def beside(value):
    pairs = [(i, i + 1) for i in range(1, lax.axis_size(AXIS) - 1, 2)]
    return lax.ppermute(value, AXIS, pairs + [(b, a) for a, b in pairs])


def groups(*per_core):
    ids = np.arange(math.prod(GRID)).reshape(GRID)
    found = []
    for core, axes in enumerate(per_core):
        rest = [axis for axis in range(3) if axis not in axes]
        size = math.prod(GRID[axis] for axis in axes)
        found += ids[..., core].transpose(rest + list(axes)).reshape(-1, size).tolist()
    return found


def exchange(value, members):
    return lax.all_to_all(value, AXIS, 0, 0, axis_index_groups=members, tiled=True)


def repeated(value, count):
    return jnp.broadcast_to(value[None], (count,) + value.shape)


def halves(value):
    high = value.astype(BF16)
    return high, (value - high.astype(F32)).astype(BF16)


def mm(a, b, dims=((1,), (0,))):
    return lax.dot_general(a, b, (dims, ((), ())), preferred_element_type=F32)


def fold(wide):
    half = wide.shape[1] // 2
    return wide[:, :half] + wide[:, half:]


def prepare(block_index, block_counts, adjacency, features, w_in, w_out, labels,
            loc_h, loc_l, halo_h, halo_l, s_loc, win_h, win_l, wout_hl, wout_hh, wout_ll, onehot, feat_out,
            slots_in, feat_in, win_in, wout_in, labels_in, band, sems):
    here, slots, rows, _ = adjacency.shape
    moves = [(features, feat_in), (w_in, win_in), (w_out, wout_in), (labels, labels_in)]
    moves += [(adjacency.at[b, k], slots_in.at[b, k]) for b in range(here) for k in range(slots)]
    moves = [pltpu.make_async_copy(source, target, sems.at[i]) for i, (source, target) in enumerate(moves)]
    for move in moves:
        move.start()
    me = lax.axis_index(AXIS)
    core = lax.rem(me, 2)
    first = me * here
    band[...] = jnp.zeros_like(band)
    for move in moves[:4]:
        move.wait()
    high, low = halves(win_in[...])
    win_h[...] = high
    win_l[...] = low
    high, low = halves(wout_in[...])
    classes = high.shape[1]
    for ref, left, right in ((wout_hl, high, low), (wout_hh, high, high), (wout_ll, low, low)):
        ref[:, :classes] = left
        ref[:, classes:] = right
    columns = lax.broadcasted_iota(jnp.int32, (classes, labels_in.shape[1]), 0)
    onehot[...] = jnp.where(columns == labels_in[...], 1.0, 0.0).T
    feat_out[...] = feat_in[...]
    feat_h, feat_l = halves(feat_in[...])
    for b in range(here):
        for k in range(slots):
            moves[4 + b * slots + k].wait()
            near = block_index[b, k] - first
            right = near >= here
            outside = jnp.where(right, near - here, near + here)
            outside += jnp.where(right == (core == 0), 0, 2 * here)
            place = jnp.where((near >= 0) & (near < here), here + near, outside)

            @pl.when(k < block_counts[b])
            def _():
                band[b, place] += slots_in[b, k]

        at = pl.ds(b * rows, rows)
        for s in range(3 * here):
            high, low = halves(band[b, s])
            if here <= s < 2 * here:
                cols = pl.ds((s - here) * rows, rows)
                loc_h[at, cols] = high
                loc_l[at, cols] = low
            else:
                cols = pl.ds((s if s < here else s - here) * rows, rows)
                halo_h[at, cols] = high
                halo_l[at, cols] = low
        s_loc[at, :] = mm(loc_h[at, :], feat_h) + mm(loc_h[at, :], feat_l) + mm(loc_l[at, :], feat_h)


def add_features(halo_h, halo_l, s_loc, feat_e, out):
    half = feat_e.shape[0]
    high, low = halves(feat_e[...])
    he, le = halo_h[:, half:], halo_l[:, half:]
    out[...] = s_loc[...] + mm(he, high) + mm(he, low) + mm(le, high)


def spread(halo_h, halo_l, s_loc, feat_i, spread_in, longer):
    half = feat_i.shape[0]
    high, low = halves(feat_i[...])
    hi, li = halo_h[:, :half], halo_l[:, :half]
    value = s_loc[...] + mm(hi, high) + mm(hi, low) + mm(li, high)
    spread_in[...] = value
    longer[:half, :] = value
    longer[half:, :] = jnp.zeros_like(longer[half:, :])


def layer(spread_in, win_h, win_l):
    s_h, s_l = halves(spread_in)
    pre = mm(s_h, win_h[...]) + mm(s_h, win_l[...]) + mm(s_l, win_h[...])
    bell = jnp.exp(-0.5 * pre * pre)
    t = 1.0 / (1.0 + (0.4 * SQRT_HALF) * jnp.abs(pre))
    poly = jnp.full_like(t, HALF_ERFC[0])
    for term in HALF_ERFC[1:]:
        poly = poly * t + term
    tail = bell * (t * poly)
    gate = jnp.where(pre < 0, tail, 1.0 - tail)
    return pre * gate, gate + pre * (INV_SQRT_2PI * bell)


def forward(high_band, low_band, spread_in, win_h, win_l, wout_hl, logits_before,
            scores_sum, slope, hid_h, hid_l, *in_t, first, part):
    nodes = slope.shape[0]
    rows_in = spread_in[:nodes, :]
    hidden, slope[...] = layer(rows_in, win_h, win_l)
    high, low = halves(hidden)
    hid_h[...] = high
    hid_l[...] = low
    pair = jnp.concatenate(halves(fold(mm(high, wout_hl[...]) + mm(low, wout_hl[...]))), axis=1)
    cols = slice(part * nodes, (part + 1) * nodes)
    logits = fold(mm(high_band[:, cols], pair) + mm(low_band[:, cols], pair))
    scores_sum[...] = logits if first else logits_before[...] + logits
    if in_t:
        turn(rows_in, *in_t)


def turn(spread_in, in_th, in_tl):
    high, low = halves(spread_in[...].T)
    in_th[...] = high
    in_tl[...] = low


def stacked(grads, high, low):
    tall = mm(grads, high) + mm(grads, low)
    half = tall.shape[0] // 2
    return tall[:half] + tall[half:]


def classify(values, onehot, grads_t, loss):
    scores = values[...]
    totals = jnp.log(jnp.sum(jnp.exp(scores), axis=1, keepdims=True))
    hot = onehot[...]
    grads_t[...] = jnp.concatenate(halves((jnp.exp(scores - totals) - hot).T), axis=0)
    row_loss = totals - jnp.sum(hot * scores, axis=1, keepdims=True)
    loss[...] = jnp.broadcast_to(jnp.sum(row_loss, axis=0, keepdims=True), loss.shape)


def gradient_half(which, parts, loss, out):
    deep, hid = parts[0][2][0].shape[0] // 2, parts[0][1][0].shape[1] // 2
    at = pl.ds(pl.multiple_of(which * deep, deep), deep)
    cols = pl.ds(pl.multiple_of(which * hid, hid), hid)
    grad_in = grad_out_t = 0.0
    for returned_t, (hid_h, hid_l), (in_th, in_tl), (pre_h, pre_l) in parts:
        high, low = in_th[at, :], in_tl[at, :]
        tall = mm(jnp.concatenate([high, low], axis=0), pre_h)
        grad_in = grad_in + (tall[:deep] + tall[deep:] + mm(high, pre_l))
        tall = jnp.concatenate(halves(returned_t), axis=0)
        grad_out_t = grad_out_t + stacked(tall, hid_h[:, cols], hid_l[:, cols])
    for t in range(grad_in.shape[1] // LANES):
        out[pl.ds(t * deep, deep), :] = grad_in[:, t * LANES : (t + 1) * LANES]
    grad_out = grad_out_t.T
    grad_out = jnp.where(last_element(grad_out) & (which == 1), loss[:1, :], grad_out)
    rows = deep * (grad_in.shape[1] // LANES)
    out[pl.ds(rows, hid), :] = grad_out


def last_element(value):
    row = lax.broadcasted_iota(jnp.int32, value.shape, 0)
    column = lax.broadcasted_iota(jnp.int32, value.shape, 1)
    return (row == value.shape[0] - 1) & (column == value.shape[1] - 1)


def backward(grads_t, halo_h, halo_l, loc_h, loc_l, slope_o, slope_i, slope_e, hid_oh, hid_ol, hid_ih, hid_il, hid_eh, hid_el,
             in_oh, in_ol, in_ih, in_il, in_eh, in_el, wout_hh, wout_ll, loss,
             pre_oh, pre_ol, pre_ih, pre_il, pre_eh, pre_el, ret_loc, out_i, out_e, give):
    grads = grads_t[...]
    half = loc_h.shape[1]
    own = stacked(grads, loc_h[...], loc_l[...])
    near = stacked(grads, halo_h[:, :half], halo_l[:, :half])
    far = stacked(grads, halo_h[:, half:], halo_l[:, half:])
    ret_loc[...] = own
    out_i[...] = near
    out_e[...] = far
    across = ((1,), (1,))
    parts = []
    for returned_t, slope, hidden, inputs, pre_h, pre_l in (
        (own, slope_o, (hid_oh, hid_ol), (in_oh, in_ol), pre_oh, pre_ol),
        (near, slope_i, (hid_ih, hid_il), (in_ih, in_il), pre_ih, pre_il),
        (far, slope_e, (hid_eh, hid_el), (in_eh, in_el), pre_eh, pre_el),
    ):
        both = jnp.concatenate(halves(returned_t.T), axis=1)
        hidden_grad = mm(both, wout_hh[...], across) + mm(both, wout_ll[...], across)
        high, low = halves(hidden_grad * slope[...])
        pre_h[...] = high
        pre_l[...] = low
        parts.append((returned_t, hidden, inputs, (high, low)))
    other = 1 - lax.rem(lax.axis_index(AXIS), 2)
    gradient_half(other, parts, loss, give)


def backward_kept(hid_oh, hid_ol, hid_ih, hid_il, hid_eh, hid_el, in_oh, in_ol, in_ih, in_il, in_eh, in_el,
                  pre_oh, pre_ol, pre_ih, pre_il, pre_eh, pre_el, ret_loc, out_i, out_e, loss,
                  keep):
    core = lax.rem(lax.axis_index(AXIS), 2)
    parts = (
        (ret_loc[...], (hid_oh, hid_ol), (in_oh, in_ol), (pre_oh[...], pre_ol[...])),
        (out_i[...], (hid_ih, hid_il), (in_ih, in_il), (pre_ih[...], pre_il[...])),
        (out_e[...], (hid_eh, hid_el), (in_eh, in_el), (pre_eh[...], pre_el[...])),
    )
    gradient_half(core, parts, loss, keep)


def put_logits(values, logits, token):
    logits[...] = values[...]
    token[...] = values[:8, :]


def finish_hidden(ret_loc, ret_e, ret_i, wout_hh, wout_ll, hidden_grad):
    returned = (ret_loc[...] + ret_e[...] + ret_i[...]).T
    both = jnp.concatenate(halves(returned), axis=1)
    across = ((1,), (1,))
    hidden_grad[...] = mm(both, wout_hh[...], across) + mm(both, wout_ll[...], across)


def sum_repeated(received, *refs):
    out = refs[-1]
    total = received[0]
    for k in range(1, received.shape[0]):
        total = total + received[k]
    out[...] = jnp.broadcast_to(total[None], out.shape)


def assemble(nodes_total, own, other, grad_in, grad_out, mean_loss):
    deep = grad_in.shape[0] // 2
    hid = grad_out.shape[0] // 2
    tiles = grad_in.shape[1] // LANES
    core = lax.rem(lax.axis_index(AXIS), 2)
    for half, which in ((own, core), (other, 1 - core)):
        at = pl.ds(pl.multiple_of(which * deep, deep), deep)
        for t in range(tiles):
            grad_in[at, t * LANES : (t + 1) * LANES] = half[pl.ds(t * deep, deep), :]
        at = pl.ds(pl.multiple_of(which * hid, hid), hid)
        grad_out[at, :] = half[pl.ds(tiles * deep, hid), :]
    end = pl.ds(2 * hid - 8, 8)
    value = grad_out[end, :]
    there = last_element(value)
    mean_loss[0, 0] = jnp.sum(jnp.where(there, value, 0.0)) / nodes_total
    others = jnp.sum(jnp.where(there, 0.0, value), axis=1, keepdims=True)
    grad_out[end, :] = jnp.where(there, -others, value)


def call(body, outs, args, scalars=0, anywhere=0, flops=0, scratch=(), space=pltpu.VMEM, cheap=False, name=""):
    smem = pl.BlockSpec(memory_space=pltpu.SMEM)
    vmem = pl.BlockSpec(memory_space=pltpu.VMEM)
    moved = 0 if cheap else sum(a.size * a.dtype.itemsize for a in args)
    flops = 0 if cheap else flops
    return pl.pallas_call(
        body,
        out_shape=[jax.ShapeDtypeStruct(shape, kind) for shape, kind in outs],
        in_specs=[smem] * scalars
        + [pl.BlockSpec(memory_space=space)] * (len(args) - scalars - anywhere)
        + [pl.BlockSpec(memory_space=pl.ANY)] * anywhere,
        out_specs=[smem if shape == (1, 1) else vmem for shape, _ in outs],
        scratch_shapes=scratch,
        cost_estimate=pl.CostEstimate(flops=flops, bytes_accessed=moved, transcendentals=0),
        compiler_params=pltpu.CompilerParams(vmem_limit_bytes=VMEM_LIMIT),
        name=name or body.__name__,
    )(*args)


def per_device(features, adjacency, block_index, block_counts, labels, weight_in, weight_out):
    here, slots, rows = adjacency.shape[:3]
    nodes = here * rows
    deep, hid = weight_in.shape
    classes = weight_out.shape[1]

    feat_e = beside(features)
    loc = ((nodes, nodes), BF16)
    halo = ((nodes, 2 * nodes), BF16)
    w_pair = ((hid, 2 * classes), BF16)
    loc_h, loc_l, halo_h, halo_l, s_loc, win_h, win_l, wout_hl, wout_hh, wout_ll, onehot, feat_out = call(
        prepare,
        [loc, loc, halo, halo, ((nodes, deep), F32), ((deep, hid), BF16), ((deep, hid), BF16),
         w_pair, w_pair, w_pair, ((nodes, classes), F32), ((nodes, deep), F32)],
        [pltpu.with_memory_space_constraint(v, pltpu.HBM)
         for v in (block_index, block_counts, adjacency, features, weight_in, weight_out, labels.reshape(1, nodes))],
        scalars=2,
        flops=6 * nodes * nodes * deep,
        scratch=[
            pltpu.VMEM(adjacency.shape, F32),
            pltpu.VMEM(features.shape, F32),
            pltpu.VMEM(weight_in.shape, F32),
            pltpu.VMEM(weight_out.shape, F32),
            pltpu.VMEM((1, nodes), jnp.int32),
            pltpu.VMEM((here, 3 * here, rows, rows), F32),
            pltpu.SemaphoreType.DMA((4 + here * slots,)),
        ],
        space=pltpu.HBM,
    )
    feat_i = mate(feat_out)
    (s_loc,) = call(
        add_features,
        [((nodes, deep), F32)],
        [halo_h, halo_l, s_loc, feat_e],
        flops=6 * nodes * nodes * deep,
    )
    wide_f, wide_h = ((nodes, hid), F32), ((nodes, hid), BF16)
    thin, thin_t, in_t = ((nodes, classes), F32), ((classes, nodes), F32), ((deep, nodes), BF16)
    spread_in, longer = call(
        spread, [((nodes, deep), F32), ((nodes + 8, deep), F32)], [halo_h, halo_l, s_loc, feat_i], flops=6 * nodes * nodes * deep
    )
    spread_e = beside(longer)
    spread_i = mate(spread_in)
    in_oh, in_ol = call(turn, [in_t, in_t], [spread_in])

    def layer_of(high, low, rows_in, before, name, part):
        return call(
            functools.partial(forward, first=name == "forward_own", part=part),
            [thin, wide_f, wide_h, wide_h] + [in_t] * (0 if name == "forward_own" else 2),
            [high, low, rows_in, win_h, win_l, wout_hl, before],
            flops=16 * nodes * nodes * deep,
            cheap=name == "forward_mate",
            name=name,
        )

    logits_o, slope_o, *kept_o = layer_of(loc_h, loc_l, spread_in, onehot, "forward_own", 0)
    logits_i, slope_i, *kept_i = layer_of(halo_h, halo_l, spread_i, logits_o, "forward_mate", 0)
    values, slope_e, *kept_e = layer_of(halo_h, halo_l, spread_e, logits_i, "forward_beside", 1)
    grads_t, loss = call(classify, [((2 * classes, nodes), BF16), ((8, LANES), F32)], [values, onehot])
    half = (deep * hid + hid * classes) // LANES // 2
    hids = [*kept_o[:2], *kept_i[:2], *kept_e[:2]]
    in_ts = [in_oh, in_ol, *kept_i[2:], *kept_e[2:]]
    *pre, ret_loc, out_i, out_e, give = call(
        backward,
        [wide_h] * 6 + [thin_t] * 3 + [((half, LANES), F32)],
        [grads_t, halo_h, halo_l, loc_h, loc_l, slope_o, slope_i, slope_e, *hids,
         *in_ts, wout_hh, wout_ll, loss],
        flops=30 * nodes * nodes * deep,
    )
    got = mate(give)
    logits, token = call(put_logits, [thin, ((8, LANES), F32)], [values])
    (keep,) = call(
        backward_kept,
        [((half, LANES), F32)],
        [*hids, *in_ts, *pre, ret_loc, out_i, out_e, loss],
        flops=10 * nodes * nodes * deep,
    )
    big, mid = groups((X, Y), (X, Z)), groups((Z,), (Y,))
    wide, narrow = len(big[0]), len(mid[0])
    shard = half // wide
    received = exchange((keep + got).reshape(wide, shard, LANES), big)
    ret_e = beside(out_e)
    ret_i = mate(out_i)
    (summed,) = call(sum_repeated, [((narrow, shard, LANES), F32)], [received, token])
    received = exchange(summed, mid)
    (summed,) = call(sum_repeated, [((1, shard, LANES), F32)], [received])
    (summed,) = call(sum_repeated, [((wide, shard, LANES), F32)], [summed, ret_e, ret_i], anywhere=2)
    own = exchange(summed, big).reshape(half, LANES)
    other = mate(own)
    (hidden_grad,) = call(
        finish_hidden, [wide_f], [ret_loc, ret_e, ret_i, wout_hh, wout_ll], flops=4 * nodes * nodes * deep
    )
    grad_in, grad_out, mean_loss = call(
        functools.partial(assemble, nodes * lax.axis_size(AXIS)),
        [((deep, hid), F32), ((hid, classes), F32), ((1, 1), F32)],
        [own, other],
        name="assemble",
    )
    return (logits, mean_loss.reshape(()), hidden_grad, grad_in, grad_out)


def solution(mesh):
    split = P(AXIS)
    return jax.shard_map(
        per_device,
        mesh=mesh,
        in_specs=(split, split, split, split, split, P(), P()),
        out_specs=(split, P(), split, P(), P()),
        check_vma=False,
    )
```

```python
import functools
import math

import jax
import jax.numpy as jnp
import numpy as np
from jax import lax
from jax.experimental import pallas as pl
from jax.experimental.pallas import tpu as pltpu
from jax.sharding import PartitionSpec as P

AXIS = "rows"
GRID = (4, 8, 8, 2)
X, Z, Y = range(3)
LANES = 128
F32 = jnp.float32
BF16 = jnp.bfloat16
VMEM_LIMIT = 24 * 1024 * 1024
CHUNK = 256
SQRT_HALF = 0.7071067811865476
INV_SQRT_2PI = 0.3989422804014327
HALF_ERFC = (
    0.0251311707,
    -0.0914511383,
    0.0845433265,
    -0.00280424249,
    0.0707159187,
    0.0842709431,
    0.103921354,
    0.112834799,
    0.112837931,
)


def mate(value):
    return lax.ppermute(value, AXIS, [(i, i ^ 1) for i in range(lax.axis_size(AXIS))])


def beside(value):
    pairs = [(i, i + 1) for i in range(1, lax.axis_size(AXIS) - 1, 2)]
    return lax.ppermute(value, AXIS, pairs + [(b, a) for a, b in pairs])


def groups(*per_core):
    ids = np.arange(math.prod(GRID)).reshape(GRID)
    found = []
    for core, axes in enumerate(per_core):
        rest = [axis for axis in range(3) if axis not in axes]
        size = math.prod(GRID[axis] for axis in axes)
        found += ids[..., core].transpose(rest + list(axes)).reshape(-1, size).tolist()
    return found


def exchange(value, members):
    return lax.all_to_all(value, AXIS, 0, 0, axis_index_groups=members, tiled=True)


def repeated(value, count):
    return jnp.broadcast_to(value[None], (count,) + value.shape)


def halves(value):
    high = value.astype(BF16)
    return high, (value - high.astype(F32)).astype(BF16)


def mm(a, b, dims=((1,), (0,))):
    return lax.dot_general(a, b, (dims, ((), ())), preferred_element_type=F32)


def fold(wide):
    half = wide.shape[1] // 2
    return wide[:, :half] + wide[:, half:]


def prepare(block_index, block_counts, adjacency, features, w_in, w_out, labels,
            loc_h, loc_l, halo_h, halo_l, s_loc, win_h, win_l, wout_hl, wout_hh, wout_ll, onehot, feat_out,
            slots_in, feat_in, win_in, wout_in, labels_in, band, sems):
    here, slots, rows, _ = adjacency.shape
    moves = [(features, feat_in), (w_in, win_in), (w_out, wout_in), (labels, labels_in)]
    moves += [(adjacency.at[b, k], slots_in.at[b, k]) for b in range(here) for k in range(slots)]
    moves = [pltpu.make_async_copy(source, target, sems.at[i]) for i, (source, target) in enumerate(moves)]
    for move in moves:
        move.start()
    me = lax.axis_index(AXIS)
    core = lax.rem(me, 2)
    first = me * here
    band[...] = jnp.zeros_like(band)
    for move in moves[:4]:
        move.wait()
    high, low = halves(win_in[...])
    win_h[...] = high
    win_l[...] = low
    high, low = halves(wout_in[...])
    classes = high.shape[1]
    for ref, left, right in ((wout_hl, high, low), (wout_hh, high, high), (wout_ll, low, low)):
        ref[:, :classes] = left
        ref[:, classes:] = right
    columns = lax.broadcasted_iota(jnp.int32, (classes, labels_in.shape[1]), 0)
    onehot[...] = jnp.where(columns == labels_in[...], 1.0, 0.0).T
    feat_out[...] = feat_in[...]
    feat_h, feat_l = halves(feat_in[...])
    for b in range(here):
        for k in range(slots):
            moves[4 + b * slots + k].wait()
            near = block_index[b, k] - first
            right = near >= here
            outside = jnp.where(right, near - here, near + here)
            outside += jnp.where(right == (core == 0), 0, 2 * here)
            place = jnp.where((near >= 0) & (near < here), here + near, outside)

            @pl.when(k < block_counts[b])
            def _():
                band[b, place] += slots_in[b, k]

        at = pl.ds(b * rows, rows)
        for s in range(3 * here):
            high, low = halves(band[b, s])
            if here <= s < 2 * here:
                cols = pl.ds((s - here) * rows, rows)
                loc_h[at, cols] = high
                loc_l[at, cols] = low
            else:
                cols = pl.ds((s if s < here else s - here) * rows, rows)
                halo_h[at, cols] = high
                halo_l[at, cols] = low
        s_loc[at, :] = mm(loc_h[at, :], feat_h) + mm(loc_h[at, :], feat_l) + mm(loc_l[at, :], feat_h)


def add_features(halo_h, halo_l, s_loc, feat_e, out):
    half = feat_e.shape[0]
    high, low = halves(feat_e[...])
    he, le = halo_h[:, half:], halo_l[:, half:]
    out[...] = s_loc[...] + mm(he, high) + mm(he, low) + mm(le, high)


def spread(halo_h, halo_l, s_loc, feat_i, spread_in, longer):
    half = feat_i.shape[0]
    high, low = halves(feat_i[...])
    hi, li = halo_h[:, :half], halo_l[:, :half]
    value = s_loc[...] + mm(hi, high) + mm(hi, low) + mm(li, high)
    spread_in[...] = value
    longer[:half, :] = value
    longer[half:, :] = jnp.zeros_like(longer[half:, :])


def layer(spread_in, win_h, win_l):
    s_h, s_l = halves(spread_in)
    pre = mm(s_h, win_h[...]) + mm(s_h, win_l[...]) + mm(s_l, win_h[...])
    bell = jnp.exp(-0.5 * pre * pre)
    t = 1.0 / (1.0 + (0.4 * SQRT_HALF) * jnp.abs(pre))
    poly = jnp.full_like(t, HALF_ERFC[0])
    for term in HALF_ERFC[1:]:
        poly = poly * t + term
    tail = bell * (t * poly)
    gate = jnp.where(pre < 0, tail, 1.0 - tail)
    return pre * gate, gate + pre * (INV_SQRT_2PI * bell)


def forward(high_band, low_band, spread_in, win_h, win_l, wout_hl, logits_before,
            scores_sum, slope, hid_h, hid_l, *in_t, first, part):
    nodes = slope.shape[0]
    rows_in = spread_in[:nodes, :]
    hidden, slope[...] = layer(rows_in, win_h, win_l)
    high, low = halves(hidden)
    hid_h[...] = high
    hid_l[...] = low
    pair = jnp.concatenate(halves(fold(mm(high, wout_hl[...]) + mm(low, wout_hl[...]))), axis=1)
    cols = slice(part * nodes, (part + 1) * nodes)
    logits = fold(mm(high_band[:, cols], pair) + mm(low_band[:, cols], pair))
    scores_sum[...] = logits if first else logits_before[...] + logits
    if in_t:
        turn(rows_in, *in_t)


def turn(spread_in, in_th, in_tl):
    high, low = halves(spread_in[...].T)
    in_th[...] = high
    in_tl[...] = low


def stacked(grads, high, low):
    tall = mm(grads, high) + mm(grads, low)
    half = tall.shape[0] // 2
    return tall[:half] + tall[half:]


def classify(values, onehot, loss):
    scores = values[...]
    totals = jnp.log(jnp.sum(jnp.exp(scores), axis=1, keepdims=True))
    hot = onehot[...]
    row_loss = totals - jnp.sum(hot * scores, axis=1, keepdims=True)
    loss[...] = jnp.broadcast_to(jnp.sum(row_loss, axis=0, keepdims=True), loss.shape)
    return jnp.concatenate(halves((jnp.exp(scores - totals) - hot).T), axis=0)


def gradient_half(which, parts, loss, out):
    deep, hid = parts[0][2][0].shape[0] // 2, parts[0][1][0].shape[1] // 2
    at = pl.ds(pl.multiple_of(which * deep, deep), deep)
    cols = pl.ds(pl.multiple_of(which * hid, hid), hid)
    grad_in = grad_out_t = 0.0
    for returned_t, (hid_h, hid_l), (in_th, in_tl), (pre_h, pre_l) in parts:
        high, low = in_th[at, :], in_tl[at, :]
        tall = mm(jnp.concatenate([high, low], axis=0), pre_h)
        grad_in = grad_in + (tall[:deep] + tall[deep:] + mm(high, pre_l))
        tall = jnp.concatenate(halves(returned_t), axis=0)
        grad_out_t = grad_out_t + stacked(tall, hid_h[:, cols], hid_l[:, cols])
    for t in range(grad_in.shape[1] // LANES):
        out[pl.ds(t * deep, deep), :] = grad_in[:, t * LANES : (t + 1) * LANES]
    grad_out = grad_out_t.T
    grad_out = jnp.where(last_element(grad_out) & (which == 1), loss[:1, :], grad_out)
    rows = deep * (grad_in.shape[1] // LANES)
    out[pl.ds(rows, hid), :] = grad_out


def last_element(value):
    row = lax.broadcasted_iota(jnp.int32, value.shape, 0)
    column = lax.broadcasted_iota(jnp.int32, value.shape, 1)
    return (row == value.shape[0] - 1) & (column == value.shape[1] - 1)


def backward(values, onehot, halo_h, halo_l, loc_h, loc_l, slope_o, slope_i, slope_e, hid_oh, hid_ol, hid_ih, hid_il, hid_eh, hid_el,
             in_oh, in_ol, in_ih, in_il, in_eh, in_el, wout_hh, wout_ll,
             loss, pre_oh, pre_ol, pre_ih, pre_il, pre_eh, pre_el, ret_loc, out_i, out_e, give):
    grads = classify(values, onehot, loss)
    half = loc_h.shape[1]
    own = stacked(grads, loc_h[...], loc_l[...])
    near = stacked(grads, halo_h[:, :half], halo_l[:, :half])
    far = stacked(grads, halo_h[:, half:], halo_l[:, half:])
    ret_loc[...] = own
    out_i[...] = near
    out_e[...] = far
    across = ((1,), (1,))
    parts = []
    for returned_t, slope, hidden, inputs, pre_h, pre_l in (
        (own, slope_o, (hid_oh, hid_ol), (in_oh, in_ol), pre_oh, pre_ol),
        (near, slope_i, (hid_ih, hid_il), (in_ih, in_il), pre_ih, pre_il),
        (far, slope_e, (hid_eh, hid_el), (in_eh, in_el), pre_eh, pre_el),
    ):
        both = jnp.concatenate(halves(returned_t.T), axis=1)
        hidden_grad = mm(both, wout_hh[...], across) + mm(both, wout_ll[...], across)
        high, low = halves(hidden_grad * slope[...])
        pre_h[...] = high
        pre_l[...] = low
        parts.append((returned_t, hidden, inputs, (high, low)))
    other = 1 - lax.rem(lax.axis_index(AXIS), 2)
    gradient_half(other, parts, loss, give)


def backward_kept(hid_oh, hid_ol, hid_ih, hid_il, hid_eh, hid_el, in_oh, in_ol, in_ih, in_il, in_eh, in_el,
                  pre_oh, pre_ol, pre_ih, pre_il, pre_eh, pre_el, ret_loc, out_i, out_e, loss,
                  keep):
    core = lax.rem(lax.axis_index(AXIS), 2)
    parts = (
        (ret_loc[...], (hid_oh, hid_ol), (in_oh, in_ol), (pre_oh[...], pre_ol[...])),
        (out_i[...], (hid_ih, hid_il), (in_ih, in_il), (pre_ih[...], pre_il[...])),
        (out_e[...], (hid_eh, hid_el), (in_eh, in_el), (pre_eh[...], pre_el[...])),
    )
    gradient_half(core, parts, loss, keep)


def put_logits(values, logits, token):
    logits[...] = values[...]
    token[...] = values[:8, :]


def finish_hidden(ret_loc, ret_e, ret_i, wout_hh, wout_ll, hidden_grad):
    returned = (ret_loc[...] + ret_e[...] + ret_i[...]).T
    both = jnp.concatenate(halves(returned), axis=1)
    across = ((1,), (1,))
    hidden_grad[...] = mm(both, wout_hh[...], across) + mm(both, wout_ll[...], across)


def sum_repeated(received, *refs):
    out = refs[-1]
    total = received[0]
    for k in range(1, received.shape[0]):
        total = total + received[k]
    out[...] = jnp.broadcast_to(total[None], out.shape)


def assemble(nodes_total, own, other, grad_in, grad_out, mean_loss):
    deep = grad_in.shape[0] // 2
    hid = grad_out.shape[0] // 2
    tiles = grad_in.shape[1] // LANES
    core = lax.rem(lax.axis_index(AXIS), 2)
    for half, which in ((own, core), (other, 1 - core)):
        at = pl.ds(pl.multiple_of(which * deep, deep), deep)
        for t in range(tiles):
            grad_in[at, t * LANES : (t + 1) * LANES] = half[pl.ds(t * deep, deep), :]
        at = pl.ds(pl.multiple_of(which * hid, hid), hid)
        grad_out[at, :] = half[pl.ds(tiles * deep, hid), :]
    end = pl.ds(2 * hid - 8, 8)
    value = grad_out[end, :]
    there = last_element(value)
    mean_loss[0, 0] = jnp.sum(jnp.where(there, value, 0.0)) / nodes_total
    others = jnp.sum(jnp.where(there, 0.0, value), axis=1, keepdims=True)
    grad_out[end, :] = jnp.where(there, -others, value)


def call(body, outs, args, scalars=0, anywhere=0, flops=0, scratch=(), space=pltpu.VMEM, cheap=False, name=""):
    smem = pl.BlockSpec(memory_space=pltpu.SMEM)
    vmem = pl.BlockSpec(memory_space=pltpu.VMEM)
    moved = 0 if cheap else sum(a.size * a.dtype.itemsize for a in args)
    flops = 0 if cheap else flops
    return pl.pallas_call(
        body,
        out_shape=[jax.ShapeDtypeStruct(shape, kind) for shape, kind in outs],
        in_specs=[smem] * scalars
        + [pl.BlockSpec(memory_space=space)] * (len(args) - scalars - anywhere)
        + [pl.BlockSpec(memory_space=pl.ANY)] * anywhere,
        out_specs=[smem if shape == (1, 1) else vmem for shape, _ in outs],
        scratch_shapes=scratch,
        cost_estimate=pl.CostEstimate(flops=flops, bytes_accessed=moved, transcendentals=0),
        compiler_params=pltpu.CompilerParams(vmem_limit_bytes=VMEM_LIMIT),
        name=name or body.__name__,
    )(*args)


def per_device(features, adjacency, block_index, block_counts, labels, weight_in, weight_out):
    here, slots, rows = adjacency.shape[:3]
    nodes = here * rows
    deep, hid = weight_in.shape
    classes = weight_out.shape[1]

    feat_e = beside(features)
    loc = ((nodes, nodes), BF16)
    halo = ((nodes, 2 * nodes), BF16)
    w_pair = ((hid, 2 * classes), BF16)
    loc_h, loc_l, halo_h, halo_l, s_loc, win_h, win_l, wout_hl, wout_hh, wout_ll, onehot, feat_out = call(
        prepare,
        [loc, loc, halo, halo, ((nodes, deep), F32), ((deep, hid), BF16), ((deep, hid), BF16),
         w_pair, w_pair, w_pair, ((nodes, classes), F32), ((nodes, deep), F32)],
        [pltpu.with_memory_space_constraint(v, pltpu.HBM)
         for v in (block_index, block_counts, adjacency, features, weight_in, weight_out, labels.reshape(1, nodes))],
        scalars=2,
        flops=6 * nodes * nodes * deep,
        scratch=[
            pltpu.VMEM(adjacency.shape, F32),
            pltpu.VMEM(features.shape, F32),
            pltpu.VMEM(weight_in.shape, F32),
            pltpu.VMEM(weight_out.shape, F32),
            pltpu.VMEM((1, nodes), jnp.int32),
            pltpu.VMEM((here, 3 * here, rows, rows), F32),
            pltpu.SemaphoreType.DMA((4 + here * slots,)),
        ],
        space=pltpu.HBM,
    )
    feat_i = mate(feat_out)
    (s_loc,) = call(
        add_features,
        [((nodes, deep), F32)],
        [halo_h, halo_l, s_loc, feat_e],
        flops=6 * nodes * nodes * deep,
    )
    wide_f, wide_h = ((nodes, hid), F32), ((nodes, hid), BF16)
    thin, thin_t, in_t = ((nodes, classes), F32), ((classes, nodes), F32), ((deep, nodes), BF16)
    spread_in, longer = call(
        spread, [((nodes, deep), F32), ((nodes + 8, deep), F32)], [halo_h, halo_l, s_loc, feat_i], flops=6 * nodes * nodes * deep
    )
    spread_e = beside(longer)
    spread_i = mate(spread_in)
    in_oh, in_ol = call(turn, [in_t, in_t], [spread_in])

    def layer_of(high, low, rows_in, before, name, part):
        return call(
            functools.partial(forward, first=name == "forward_own", part=part),
            [thin, wide_f, wide_h, wide_h] + [in_t] * (0 if name == "forward_own" else 2),
            [high, low, rows_in, win_h, win_l, wout_hl, before],
            flops=16 * nodes * nodes * deep,
            cheap=name == "forward_mate",
            name=name,
        )

    logits_o, slope_o, *kept_o = layer_of(loc_h, loc_l, spread_in, onehot, "forward_own", 0)
    logits_i, slope_i, *kept_i = layer_of(halo_h, halo_l, spread_i, logits_o, "forward_mate", 0)
    values, slope_e, *kept_e = layer_of(halo_h, halo_l, spread_e, logits_i, "forward_beside", 1)
    half = (deep * hid + hid * classes) // LANES // 2
    hids = [*kept_o[:2], *kept_i[:2], *kept_e[:2]]
    in_ts = [in_oh, in_ol, *kept_i[2:], *kept_e[2:]]
    loss, *pre, ret_loc, out_i, out_e, give = call(
        backward,
        [((8, LANES), F32)] + [wide_h] * 6 + [thin_t] * 3 + [((half, LANES), F32)],
        [values, onehot, halo_h, halo_l, loc_h, loc_l, slope_o, slope_i, slope_e, *hids,
         *in_ts, wout_hh, wout_ll],
        flops=30 * nodes * nodes * deep,
    )
    got = mate(give)
    logits, token = call(put_logits, [thin, ((8, LANES), F32)], [values])
    (keep,) = call(
        backward_kept,
        [((half, LANES), F32)],
        [*hids, *in_ts, *pre, ret_loc, out_i, out_e, loss],
        flops=10 * nodes * nodes * deep,
    )
    big, mid = groups((X, Y), (X, Z)), groups((Z,), (Y,))
    wide, narrow = len(big[0]), len(mid[0])
    shard = half // wide
    received = exchange((keep + got).reshape(wide, shard, LANES), big)
    ret_e = beside(out_e)
    ret_i = mate(out_i)
    (summed,) = call(sum_repeated, [((narrow, shard, LANES), F32)], [received, token])
    received = exchange(summed, mid)
    (summed,) = call(sum_repeated, [((1, shard, LANES), F32)], [received])
    (summed,) = call(sum_repeated, [((wide, shard, LANES), F32)], [summed, ret_e, ret_i], anywhere=2)
    own = exchange(summed, big).reshape(half, LANES)
    other = mate(own)
    (hidden_grad,) = call(
        finish_hidden, [wide_f], [ret_loc, ret_e, ret_i, wout_hh, wout_ll], flops=4 * nodes * nodes * deep
    )
    grad_in, grad_out, mean_loss = call(
        functools.partial(assemble, nodes * lax.axis_size(AXIS)),
        [((deep, hid), F32), ((hid, classes), F32), ((1, 1), F32)],
        [own, other],
        name="assemble",
    )
    return (logits, mean_loss.reshape(()), hidden_grad, grad_in, grad_out)


def solution(mesh):
    split = P(AXIS)
    return jax.shard_map(
        per_device,
        mesh=mesh,
        in_specs=(split, split, split, split, split, P(), P()),
        out_specs=(split, P(), split, P(), P()),
        check_vma=False,
    )
```
